32 devices in a mesh: gy: 16 (over z, y, x), gx: 2 (over core).
Axes of the slice: x: 2, y: 2, z: 4, core: 2. Of those that a mesh axis runs over, the one named last changes fastest.
Arguments:
- state: float32 [3, 8, 512, 512], P(None, None, 'gy', 'gx'), may hold values from -6 to 6
- parent_rows: bfloat16 [2048, 24, 256], P(('gy', 'gx')), may hold values from -6 to 6
- dest: int32 [2048, 1], P(('gy', 'gx')), may hold values from 0 to 15; in each aligned block of 64 rows (0 to 63, 64 to 127, ...) at most 8 rows name the same one
- pick: int32 [2048], P(('gy', 'gx')), may hold values from 0 to 63
- offset: int32 [2048], P(('gy', 'gx')), may hold values from 0 to 31
- wet: int32 [512, 512], P('gy', 'gx'), may hold values 0 or 1
Outputs:
- state_out: float32 [3, 8, 512, 512], P(None, None, 'gy', 'gx')
- profile: float32 [3, 512], P(None, 'gy')
The draws below stay inside these ranges and needn't reach their ends.
Inputs may be any that keep to these rules, and one draw needn't show every extreme that they name: `dest`: among the 64 rows of one device at most 8 name the same tile, a bound that some block reaches.
All inputs are finite; a program needn't handle non-finite values. No bound on the sum of `wet` on one device may be relied on, other than what follows from the above.
Results may differ from the reference program's by a relative error of at most 0.0003.
Values may be sent and summed in bfloat16 or wider, within the bound.
No kernel may reach another device: no remote copies, remote signals or barrier semaphores. Data moves between devices by JAX's collectives and lax.ppermute only.
A program may use at most 64 MiB of HBM per device.

```python
import math
import jax
import jax.numpy as jnp
import numpy as np
from jax import lax

Z = 8
CX = 256
CY = 32
SEND = 64
STEPS = 3
CAP = 8
NY = 512
NX = 512
PROWS = 2048
N_GY = 16
N_GX = 2


def plant(drawn, key, low, high):
    dims = drawn.shape
    index_at = [jax.random.randint(jax.random.fold_in(key, axis), (), 0, dims[axis]) for axis in range(len(dims))]
    drawn = drawn.at[tuple(index_at)].set(low)
    longest = dims.index(max(dims))
    index_at[longest] = (index_at[longest] + 1) % dims[longest]
    return drawn.at[tuple(index_at)].set(high)


def shard_levels(rng, shape, shards, smallest, largest):
    def one(position, shards_of):
        steps = jax.random.uniform(jax.random.fold_in(jax.random.fold_in(rng, 6), position), (shards_of,), jnp.float32, smallest / len(shards), largest / len(shards))
        return jnp.repeat(jnp.exp(steps), shape[position] // shards_of).reshape((-1,) + (1,) * (len(shape) - position - 1))

    loudness = one(*shards[0])
    for cut in shards[1:]:
        loudness = loudness * one(*cut)
    return loudness


def routed_block(rng, own, number, rows, amount, top, reach, slope):
    order = jax.random.permutation(rng, amount)
    crowded, usual = portions_of(amount, rows * top, reach, slope, True), portions_of(amount, rows * top, reach, slope, False)
    places = jnp.arange(amount)

    def named(tallies, turn):
        used = int((tallies > 0).sum())
        fixed = max(1, used // 4)
        shifted = fixed + (places - fixed + turn * (used - fixed)) % max(1, amount - fixed)
        return jnp.zeros((amount,), jnp.int32).at[order[jnp.where(places < fixed, places, shifted)]].set(jnp.asarray(tallies, jnp.int32))

    tallies = jnp.where(number % 4 == 0, named(crowded, number // 4), named(usual, number - number // 4 - 1))
    mixed = jax.random.permutation(jax.random.fold_in(own, 3), amount)
    donor, sink = mixed[0:amount // 2 * 2:2], mixed[1:amount // 2 * 2:2]
    margin = jnp.minimum(tallies[donor] - 1, reach - tallies[sink]) // 2
    margin = jnp.where((donor == order[0]) | (sink == order[0]) | (tallies[sink] == 0), 0, jnp.maximum(margin, 0))
    shifted = jax.random.randint(jax.random.fold_in(own, 4), (amount // 2,), 0, 1 << 20) % (margin + 1)
    tallies = tallies.at[donor].add(-shifted).at[sink].add(shifted)
    labels = jnp.searchsorted(jnp.cumsum(tallies), jnp.arange(rows * top), side="right").astype(jnp.int32)
    grid = labels.reshape(top, rows).T
    grid = grid[jax.random.permutation(jax.random.fold_in(own, 1), rows)]
    turn = jax.random.randint(jax.random.fold_in(own, 2), (rows, 1), 0, top)
    return jnp.take_along_axis(grid, (jnp.arange(top)[None, :] + turn) % top, axis=1)


def portions_of(amount, total, most, skew, full):
    loads = [(1 << 20) // math.isqrt(standing ** skew) + 1 for standing in range(1, amount + 1)]
    largest = most if full else min(most, max(-(-total // amount), total * loads[0] // sum(loads)))
    least = 1 if total - largest >= amount - 1 else 0
    given, spare = [largest] + [least] * (amount - 1), total - largest - least * (amount - 1)
    while spare > 0:
        movable = [i for i in range(1, amount) if given[i] < largest] or [i for i in range(1, amount) if given[i] < most]
        whole, remaining = sum([loads[i] for i in movable]), spare
        for i in movable:
            extra = min(most - given[i], max(1, remaining * loads[i] // whole), spare)
            given[i] = given[i] + extra
            spare = spare - extra
    return np.array(given)


def gaussian(own_key, extent, spread, most, shards=(), kind=jnp.bfloat16):
    loudness = shard_levels(own_key, extent, shards, -0.22, 0.18) if shards else 1.0
    result = jax.random.normal(own_key, extent, jnp.float32) * spread * loudness
    return jnp.minimum(jnp.maximum(result, -most), most).astype(kind)


def setup_inputs(seed: int = 0) -> dict:
    streams_of = jax.random.split(jax.random.key(seed), 7)
    state = gaussian(streams_of[0], (3, Z, NY, NX), 1.0, 6.0, ((2, 16), (3, 2)), jnp.float32)
    parent_rows = gaussian(streams_of[1], (PROWS, 3 * Z, CX), 1.0, 6.0, ((0, 32),))
    dest_keys = jax.random.split(jax.random.fold_in(streams_of[2], 1), PROWS // SEND)
    dest_turns = jax.random.permutation(jax.random.fold_in(streams_of[2], 3), PROWS // SEND)
    dest = jax.vmap(lambda own, number: routed_block(jax.random.fold_in(streams_of[2], 2), own, number, SEND, N_GY, 1, CAP, 2))(dest_keys, dest_turns).reshape((PROWS, 1))
    pick = plant(jax.random.randint(streams_of[3], (PROWS,), 0, SEND), jax.random.fold_in(streams_of[3], 1), 0, SEND - 1).astype(jnp.int32)
    offset = plant(jax.random.randint(streams_of[4], (PROWS,), 0, CY), jax.random.fold_in(streams_of[4], 1), 0, CY - 1).astype(jnp.int32)
    wet = plant((jax.random.randint(streams_of[5], (NY, NX), 0, 4) < 3).astype(jnp.int32), jax.random.fold_in(streams_of[5], 1), 0, 1)
    return {"state": state, "parent_rows": parent_rows, "dest": dest, "pick": pick, "offset": offset, "wet": wet}


KH = 0.2
KZ = 0.05
ADV = 0.25
PG = 0.5
GAMMA = 0.5
DISPERSE = 2.0

def advance(padded, force, count, mask):
    centre = padded[:, :, 1:-1, 1:-1]
    east = padded[:, :, 1:-1, 2:]
    west = padded[:, :, 1:-1, :-2]
    north = padded[:, :, 2:, 1:-1]
    south = padded[:, :, :-2, 1:-1]
    lap = east + west + north + south - 4.0 * centre
    upper = jnp.concatenate([centre[:, 1:], centre[:, -1:]], axis=1)
    lower = jnp.concatenate([centre[:, :1], centre[:, :-1]], axis=1)
    lapz = upper + lower - 2.0 * centre
    ddx = 0.5 * (east[0] - west[0])
    ddy = 0.5 * (north[0] - south[0])
    tracer, across, along = (centre[0], centre[1], centre[2])
    tnew = tracer + KH * lap[0] + KZ * lapz[0] - ADV * (across * ddx + along * ddy)
    unew = across + KH * lap[1] + KZ * lapz[1] - PG * ddx
    vnew = along + KH * lap[2] + KZ * lapz[2] - PG * ddy
    relax = 1.0 / (1.0 + GAMMA * count)
    tnew = (tnew + GAMMA * force[0]) * relax
    unew = unew * relax
    vnew = (vnew + GAMMA * force[1]) * relax
    return jnp.stack([tnew, unew, vnew]) * mask

def reference(state, parent_rows, dest, pick, offset, wet):
    total = dest.shape[0]
    device = jnp.arange(total, dtype=jnp.int32) // SEND
    source = device * SEND + pick
    target = (dest[:, 0] * CY + offset).reshape(N_GY, N_GX, SEND)
    source = source.reshape(N_GY, N_GX, SEND)
    forces = []
    counts = []
    for column in range(N_GX):
        picked = parent_rows[source[:, column].reshape(-1)].astype(jnp.float32).reshape(-1, 3 * Z * CX)
        where = target[:, column].reshape(-1)
        forces.append(jax.ops.segment_sum(picked, where, num_segments=NY))
        counts.append(jax.ops.segment_sum(jnp.ones(where.shape, jnp.float32), where, num_segments=NY))
    force = jnp.stack(forces, axis=1).reshape(NY, N_GX, 3, Z, CX)
    force = jnp.transpose(force, (2, 3, 0, 1, 4)).reshape(3, Z, NY, NX)
    count = jnp.repeat(jnp.stack(counts, axis=1), CX, axis=1)
    mask = wet.astype(jnp.float32)
    current = state
    for step in range(STEPS):
        padded = jnp.pad(current, ((0, 0), (0, 0), (1, 1), (1, 1)))
        current = advance(padded, force, count, mask)
    tracer = current[0]
    along = current[2]
    stokes = force[2] / (1.0 + count)
    rim = jnp.pad(tracer, ((0, 0), (1, 1), (0, 0)))
    ddy = 0.5 * (rim[:, 2:] - rim[:, :-2])
    raw = jnp.stack([lax.optimization_barrier(jnp.sum(along * tracer, axis=(0, 2))), lax.optimization_barrier(jnp.sum(stokes * tracer, axis=(0, 2))), -DISPERSE * lax.optimization_barrier(jnp.sum(ddy, axis=(0, 2)))])
    scale = jnp.sqrt(jnp.mean(raw * raw) + 1e-06)
    return (current, raw / scale)
```

```python
import functools

import jax
import jax.numpy as jnp
from jax import lax
from jax.experimental import pallas as pl
from jax.experimental.pallas import tpu as pltpu
from jax.sharding import PartitionSpec as P

SEND = 64
STEPS = 3

KH = 0.2
KZ = 0.05
ADV = 0.25
PG = 0.5
GAMMA = 0.5
DISPERSE = 2.0

EDGE = 3
RIM = 4
LANES = 128
VMEM_LIMIT = 48 * 1024 * 1024


def call(body, out_shape, flops=0, moved=0, **more):
    return pl.pallas_call(
        body,
        out_shape=out_shape,
        compiler_params=pltpu.CompilerParams(vmem_limit_bytes=VMEM_LIMIT),
        cost_estimate=pl.CostEstimate(flops=flops, bytes_accessed=moved, transcendentals=0),
        **more,
    )


def iota(shape, dim):
    return lax.broadcasted_iota(jnp.int32, shape, dim)


def gather_body(capacity, slots, dest_ref, pick_ref, offset_ref, rows_ref, out_ref):
    send, planes, cols = rows_ref.shape
    dest = dest_ref[...]
    eye = iota((send, send), 0) == iota((send, send), 1)
    dest_column = jnp.sum(jnp.where(eye, dest, 0), axis=1, keepdims=True)
    earlier = (dest_column == dest) & (iota((send, send), 0) < iota((send, send), 1))
    rank = jnp.sum(earlier.astype(jnp.int32), axis=0, keepdims=True)
    slot_of = dest * capacity + rank
    taken = iota((slots, send), 0) == slot_of
    source = jnp.sum(jnp.where(taken, pick_ref[...] + 1, 0), axis=1, keepdims=True) - 1
    label = jnp.sum(jnp.where(taken, offset_ref[...] + 1, 0), axis=1, keepdims=True)
    group = 8
    lane = iota((slots, send * group), 1)
    select = jnp.concatenate(
        [(lane == source * group + j).astype(jnp.float32).astype(jnp.bfloat16) for j in range(group)], axis=0
    )
    for g in range(planes // group):
        block = rows_ref[:, g * group : (g + 1) * group, :].reshape(send * group, cols)
        got = jnp.dot(select, block, preferred_element_type=jnp.float32).astype(jnp.bfloat16)
        for j in range(group):
            at = (g * group + j) * cols
            out_ref[:, at : at + cols] = got[j * slots : (j + 1) * slots]
    out_ref[:, planes * cols :] = jnp.broadcast_to(label, (slots, LANES)).astype(jnp.float32).astype(jnp.bfloat16)


def landing_body(planes, cols, arrived_ref, force_ref, edge_ref):
    slots = arrived_ref.shape[0]
    rows = force_ref.shape[1]
    width = planes * cols
    label = arrived_ref[:, width:].astype(jnp.float32)
    landing = (label == (iota((slots, LANES), 1) + 1).astype(jnp.float32)).astype(jnp.float32)
    landing = landing.T[:rows].astype(jnp.bfloat16)
    count = jnp.dot(landing, jnp.ones((slots, LANES), jnp.bfloat16), preferred_element_type=jnp.float32)
    lane = iota((rows, LANES), 1)
    moving = 2 * planes // 3
    edge = count
    for j in range(planes):
        force = jnp.dot(landing, arrived_ref[:, j * cols : (j + 1) * cols], preferred_element_type=jnp.float32)
        force_ref[j] = force
        if j < moving:
            at = EDGE * j
            first = pltpu.roll(force[:, :LANES], at, 1)
            edge = jnp.where((lane >= at) & (lane < at + EDGE), first, edge)
            at = EDGE * (moving + j)
            last = pltpu.roll(force[:, cols - LANES :], (at + EDGE) % LANES, 1)
            edge = jnp.where((lane >= at) & (lane < at + EDGE), last, edge)
    edge_ref[...] = edge


def outer_body(force_ref, edge_ref, *refs):
    sides, (up_ref, down_ref) = refs[:-2], refs[-2:]
    rows, cols = force_ref.shape[1:]
    moving = up_ref.shape[0] - 2
    up_ref[:moving] = force_ref[:moving, rows - RIM :]
    down_ref[:moving] = force_ref[:moving, :RIM]
    parts = [edge_ref[...]] + [side[...] for side in sides]
    parts = parts + [jnp.zeros_like(parts[0])] * (4 - len(parts))
    for k in range(2):
        pair = jnp.concatenate(parts[2 * k : 2 * k + 2], axis=1)
        up_ref[moving + k] = pair[rows - RIM :]
        down_ref[moving + k] = pair[:RIM]


def extend_body(state_ref, wet_ref, north_ref, south_ref, out_ref, first_ref, last_ref):
    planes, rows, cols = state_ref.shape
    total = rows + 2 * RIM
    lane = iota((total, LANES), 1)
    first = jnp.zeros((total, LANES), jnp.float32)
    last = jnp.zeros((total, LANES), jnp.float32)
    for j in range(planes + 1):
        own = state_ref[j] if j < planes else wet_ref[...].astype(jnp.float32)
        whole = jnp.concatenate([own, jnp.concatenate([north_ref[j], south_ref[j]], axis=0)], axis=0)
        out_ref[j] = whole
        at = EDGE * j
        keep = (lane >= at) & (lane < at + EDGE)
        first = jnp.where(keep, pltpu.roll(whole[:, :LANES], at, 1), first)
        last = jnp.where(keep, pltpu.roll(whole[:, cols - LANES :], (at + EDGE) % LANES, 1), last)
    first_ref[...] = first
    last_ref[...] = last


def side_tile(west, west_at, east, east_at):
    lane = iota(west.shape, 1)
    right = pltpu.roll(east, (LANES - east_at) % LANES, 1)
    left = pltpu.roll(west, (2 * LANES - EDGE - west_at) % LANES, 1)
    return jnp.where(lane < EDGE, right, jnp.where(lane >= LANES - EDGE, left, 0.0))


def around(field):
    rows, cols = field.shape
    return (
        pltpu.roll(field, cols - 1, 1),
        pltpu.roll(field, 1, 1),
        pltpu.roll(field, rows - 1, 0),
        pltpu.roll(field, 1, 0),
    )


def moved(load, levels, z):
    upper, lower = min(z + 1, levels - 1), max(z - 1, 0)
    results = []
    tracer, across, along = (load(f * levels + z) for f in range(3))
    east, west, north, south = around(tracer)
    ddx, ddy = 0.5 * (east - west), 0.5 * (north - south)
    extra = (ADV * (across * ddx + along * ddy), PG * ddx, PG * ddy)
    for f, centre in enumerate((tracer, across, along)):
        sides = (east, west, north, south) if f == 0 else around(centre)
        lap = (sides[0] + sides[1]) + (sides[2] + sides[3]) - 4.0 * centre
        lapz = load(f * levels + upper) + load(f * levels + lower) - 2.0 * centre
        results.append(centre + KH * lap + KZ * lapz - extra[f])
    return results


def first_body(ext_ref, west_ref, east_ref, out_ref, mask_ref, full_ref):
    planes = ext_ref.shape[0] - 1
    levels = planes // 3
    cols = ext_ref.shape[2]
    west, east = west_ref[...], east_ref[...]
    for j in range(planes + 1):
        tile = side_tile(west, EDGE * j, east, EDGE * j)
        if j == planes:
            mask_ref[:, :cols] = ext_ref[j]
            mask_ref[:, cols:] = tile
        else:
            full_ref[j, :, :cols] = ext_ref[j]
            full_ref[j, :, cols:] = tile
    for z in range(levels):
        for f, value in enumerate(moved(lambda j: full_ref[j], levels, z)):
            out_ref[f * levels + z] = value


def steps_body(sides, devices, first_ref, mask_ref, force_ref, edge_ref, north_ref, south_ref, *refs):
    side_refs = refs[:sides]
    state_ref, parts_ref, push_ref, one_ref, two_ref = refs[sides:]
    planes, total, wide = first_ref.shape
    levels = planes // 3
    rows, cols = force_ref.shape[1:]
    moving = 2 * levels
    mask = mask_ref[...]

    def joined(index):
        return jnp.concatenate([north_ref[index], south_ref[index]], axis=0)

    own_edge = edge_ref[...]
    pairs = [joined(moving), joined(moving + 1)]
    outer = [pairs[k // 2][:, (k % 2) * LANES : (k % 2 + 1) * LANES] for k in range(3)]
    edges = [jnp.concatenate([side[...], outer[1 + k]], axis=0) for k, side in enumerate(side_refs)]
    west, east = edges[0], edges[-1]
    own = jnp.concatenate([own_edge, outer[0]], axis=0)

    def counts(edge):
        return jnp.broadcast_to(edge[:, LANES - 1 :], (total, LANES))

    lane = iota((total, LANES), 1)
    count_side = jnp.where(lane < LANES // 2, counts(east), counts(west))
    count = jnp.concatenate([counts(own)] * (cols // LANES) + [count_side], axis=1)
    relax = mask / (1.0 + GAMMA * count)
    half = GAMMA * relax

    for j in range(moving):
        tile = side_tile(west, EDGE * (moving + j), east, EDGE * j)
        whole = jnp.concatenate([force_ref[j], joined(j)], axis=0)
        push_ref[j, :, :cols] = whole * half[:, :cols]
        push_ref[j, :, cols:] = tile * half[:, cols:]

    def finish(values, z):
        tracer, across, along = values
        return (tracer * relax + push_ref[z], across * relax, along * relax + push_ref[levels + z])

    for z in range(levels):
        for f, value in enumerate(finish([first_ref[f * levels + z] for f in range(3)], z)):
            one_ref[f * levels + z] = value
    for z in range(levels):
        for f, value in enumerate(finish(moved(lambda j: one_ref[j], levels, z), z)):
            two_ref[f * levels + z] = value
    share = 1.0 / (1.0 + count[:rows, :1])
    sums = [jnp.zeros((rows, cols), jnp.float32) for _ in range(3)]
    for z in range(levels):
        values = finish(moved(lambda j: two_ref[j], levels, z), z)
        for f, value in enumerate(values):
            state_ref[f * levels + z] = value[:rows, :cols]
        tracer = values[0]
        inner = tracer[:rows, :cols]
        ddy = pltpu.roll(tracer, total - 1, 0)[:rows, :cols] - pltpu.roll(tracer, 1, 0)[:rows, :cols]
        sums[0] = sums[0] + values[2][:rows, :cols] * inner
        sums[1] = sums[1] + force_ref[moving + z] * inner
        sums[2] = sums[2] + ddy
    raw = [jnp.sum(value, axis=1, keepdims=True) for value in sums]
    raw = [raw[0], raw[1] * share, raw[2] * (-0.5 * DISPERSE)]
    row, lane = iota((rows, LANES), 0), iota((rows, LANES), 1)
    packed = jnp.zeros((rows, LANES), jnp.float32)
    for q in range(3):
        packed = packed + jnp.where(lane == q * rows + row, raw[q], 0.0)
    packed = jnp.sum(packed, axis=0, keepdims=True)
    parts_ref[...] = jnp.broadcast_to(packed, (devices, LANES))


def profile_body(across, along, me_ref, parts_ref, out_ref):
    rows = out_ref.shape[1]
    parts = parts_ref[...]
    devices = parts.shape[0]
    total = parts
    for k in range(1, across):
        total = total + pltpu.roll(parts, devices - k, 0)
    row = iota(parts.shape, 0)
    squares = jnp.sum(jnp.where(row % across == 0, total * total, 0.0), keepdims=True)
    scale = jnp.sqrt(squares / (3 * rows * along) + 1e-06)
    mine = jnp.sum(jnp.where(row == me_ref[0] * across, total, 0.0), axis=0, keepdims=True) / scale
    for q in range(3):
        out_ref[q : q + 1, :] = mine[:, q * rows : (q + 1) * rows]


def per_device(state, parent_rows, dest, pick, offset, wet):
    fields, levels, rows, cols = state.shape
    planes = fields * levels
    moving = 2 * levels
    along, across = lax.axis_size("gy"), lax.axis_size("gx")
    capacity = 2 * SEND // along
    slots = along * capacity
    total, wide = rows + 2 * RIM, cols + LANES
    f32 = jnp.float32
    northward = [(i, i + 1) for i in range(along - 1)]
    southward = [(i + 1, i) for i in range(along - 1)]
    eastward = [(i, i + 1) for i in range(across - 1)]
    westward = [(i + 1, i) for i in range(across - 1)]

    payload = call(
        functools.partial(gather_body, capacity, slots),
        jax.ShapeDtypeStruct((slots, planes * cols + LANES), jnp.bfloat16),
        flops=2 * 8 * slots * SEND * planes * cols,
        moved=2 * (SEND + slots) * planes * cols,
    )(dest.reshape(1, SEND), pick.reshape(1, SEND), offset.reshape(1, SEND), parent_rows)
    arrived = lax.all_to_all(payload, "gy", split_axis=0, concat_axis=0, tiled=True)

    cells = state.reshape(planes, rows, cols)
    mask = wet.astype(f32)[None]
    to_north = jnp.concatenate([cells[:, rows - RIM :], mask[:, rows - RIM :]], axis=0)
    to_south = jnp.concatenate([cells[:, :RIM], mask[:, :RIM]], axis=0)
    from_south = lax.ppermute(to_north, "gy", northward)
    from_north = lax.ppermute(to_south, "gy", southward)
    ext, first, last = call(
        extend_body,
        (
            jax.ShapeDtypeStruct((planes + 1, total, cols), f32),
            jax.ShapeDtypeStruct((total, LANES), f32),
            jax.ShapeDtypeStruct((total, LANES), f32),
        ),
        moved=8 * planes * total * cols,
    )(cells, wet, from_north, from_south)
    from_west = lax.ppermute(last, "gx", eastward)
    from_east = lax.ppermute(first, "gx", westward)
    begun, ext_mask = call(
        first_body,
        (jax.ShapeDtypeStruct((planes, total, wide), f32), jax.ShapeDtypeStruct((total, wide), f32)),
        flops=20 * planes * total * wide,
        moved=8 * planes * total * wide,
        scratch_shapes=[pltpu.VMEM((planes, total, wide), f32)],
    )(ext, from_west, from_east)

    force, edge = call(
        functools.partial(landing_body, planes, cols),
        (jax.ShapeDtypeStruct((planes, rows, cols), f32), jax.ShapeDtypeStruct((rows, LANES), f32)),
        flops=2 * rows * slots * planes * cols,
        moved=2 * slots * planes * cols + 4 * rows * planes * cols,
    )(arrived)
    if across == 2:
        sides = [lax.ppermute(edge, "gx", [(0, 1), (1, 0)])]
    else:
        sides = [lax.ppermute(edge, "gx", eastward), lax.ppermute(edge, "gx", westward)]
    outer = jax.ShapeDtypeStruct((moving + 2, RIM, cols), f32)
    up, down = call(outer_body, (outer, outer), moved=16 * moving * RIM * cols)(force, edge, *sides)
    below = lax.ppermute(up, "gy", northward)
    above = lax.ppermute(down, "gy", southward)
    new_state, parts = call(
        functools.partial(steps_body, len(sides), along * across),
        (jax.ShapeDtypeStruct((planes, rows, cols), f32), jax.ShapeDtypeStruct((along * across, LANES), f32)),
        flops=60 * planes * total * wide,
        moved=8 * planes * total * wide,
        scratch_shapes=[
            pltpu.VMEM((moving, total, wide), f32),
            pltpu.VMEM((planes, total, wide), f32),
            pltpu.VMEM((planes, total, wide), f32),
        ],
    )(begun, ext_mask, force, edge, above, below, *sides)
    every = lax.all_to_all(parts, ("gy", "gx"), split_axis=0, concat_axis=0, tiled=True)
    me = lax.axis_index("gy").astype(jnp.int32).reshape(1)
    profile = call(
        functools.partial(profile_body, across, along),
        jax.ShapeDtypeStruct((3, rows), f32),
        in_specs=[pl.BlockSpec(memory_space=pltpu.SMEM), pl.BlockSpec(memory_space=pltpu.VMEM)],
    )(me, every)
    return new_state.reshape(state.shape), profile


def solution(mesh):
    in_specs = (
        P(None, None, "gy", "gx"),
        P(("gy", "gx"), None, None),
        P(("gy", "gx"), None),
        P(("gy", "gx")),
        P(("gy", "gx")),
        P("gy", "gx"),
    )
    out_specs = (P(None, None, "gy", "gx"), P(None, "gy"))
    return jax.shard_map(
        per_device, mesh=mesh, in_specs=in_specs, out_specs=out_specs, check_vma=False
    )
```

```python
import functools

import jax
import jax.numpy as jnp
from jax import lax
from jax.experimental import pallas as pl
from jax.experimental.pallas import tpu as pltpu
from jax.sharding import PartitionSpec as P

SEND = 64
STEPS = 3

KH = 0.2
KZ = 0.05
ADV = 0.25
PG = 0.5
GAMMA = 0.5
DISPERSE = 2.0

EDGE = 3
RIM = 4
LANES = 128
STATE_SCALE = 8192.0
FORCE_SCALE = 64.0
VMEM_LIMIT = 16 * 1024 * 1024
VMEM_MOST = 60 * 1024 * 1024


def call(body, out_shape, flops=0, moved=0, limit=VMEM_LIMIT, **more):
    return pl.pallas_call(
        body,
        out_shape=out_shape,
        compiler_params=pltpu.CompilerParams(vmem_limit_bytes=limit),
        cost_estimate=pl.CostEstimate(flops=flops, bytes_accessed=moved, transcendentals=0),
        **more,
    )


def iota(shape, dim):
    return lax.broadcasted_iota(jnp.int32, shape, dim)


def gather_body(capacity, slots, *refs):
    sources, out_ref, targets, held_ref, copied, sent = refs[:4], refs[4], refs[5:9], refs[9], refs[10], refs[11]
    copies = [
        pltpu.make_async_copy(source, target, copied.at[k]) for k, (source, target) in enumerate(zip(sources, targets))
    ]
    for copy in copies:
        copy.start()
    dest_ref, pick_ref, offset_ref, rows_ref = targets
    send, planes, cols = rows_ref.shape
    for copy in copies[:3]:
        copy.wait()
    dest = dest_ref[...]
    eye = iota((send, send), 0) == iota((send, send), 1)
    dest_column = jnp.sum(jnp.where(eye, dest, 0), axis=1, keepdims=True)
    earlier = (dest_column == dest) & (iota((send, send), 0) < iota((send, send), 1))
    rank = jnp.sum(earlier.astype(jnp.int32), axis=0, keepdims=True)
    slot_of = dest * capacity + rank
    taken = iota((slots, send), 0) == slot_of
    source = jnp.sum(jnp.where(taken, pick_ref[...] + 1, 0), axis=1, keepdims=True) - 1
    label = jnp.sum(jnp.where(taken, offset_ref[...] + 1, 0), axis=1, keepdims=True)
    group = 8
    lane = iota((slots, send * group), 1)
    select = jnp.concatenate(
        [(lane == source * group + j).astype(jnp.float32).astype(jnp.bfloat16) for j in range(group)], axis=0
    )
    width = planes * cols
    held_ref[:, width:] = jnp.broadcast_to(label, (slots, LANES)).astype(jnp.float32).astype(jnp.bfloat16)
    copies[3].wait()
    parts = []

    def send_columns(start, size):
        part = pltpu.make_async_copy(
            held_ref.at[:, pl.ds(start, size)], out_ref.at[:, pl.ds(start, size)], sent.at[len(parts)]
        )
        part.start()
        parts.append(part)

    send_columns(width, LANES)
    for g in range(planes // group):
        block = rows_ref[:, g * group : (g + 1) * group, :].reshape(send * group, cols)
        got = jnp.dot(select, block, preferred_element_type=jnp.float32).astype(jnp.bfloat16)
        for j in range(group):
            at = (g * group + j) * cols
            held_ref[:, at : at + cols] = got[j * slots : (j + 1) * slots]
        send_columns(g * group * cols, group * cols)
    for part in parts:
        part.wait()


def landing_body(planes, cols, token_ref, arrived_ref, force_ref, edge_ref):
    slots = arrived_ref.shape[0]
    rows = force_ref.shape[1]
    width = planes * cols
    label = arrived_ref[:, width:].astype(jnp.float32)
    landing = (label == (iota((slots, LANES), 1) + 1).astype(jnp.float32)).astype(jnp.float32)
    landing = landing.T[:rows].astype(jnp.bfloat16)
    count = jnp.dot(landing, jnp.ones((slots, LANES), jnp.bfloat16), preferred_element_type=jnp.float32)
    moving = 2 * planes // 3
    edge = count
    for j in range(planes):
        force = jnp.dot(landing, arrived_ref[:, j * cols : (j + 1) * cols], preferred_element_type=jnp.float32)
        force_ref[j] = force
        if j < moving:
            edge = packed(edge, force[:, :LANES], 0, EDGE * j)
            edge = packed(edge, force[:, cols - LANES :], LANES - EDGE, EDGE * (moving + j))
    edge_ref[...] = edge


def packed(into, tile, start, at):
    lane = iota(tile.shape, 1)
    shifted = pltpu.roll(tile, (at - start) % LANES, 1)
    return jnp.where((lane >= at) & (lane < at + EDGE), shifted, into)


def sides_body(state_ref, wet_ref, first_ref, last_ref):
    planes, rows, cols = state_ref.shape
    first = jnp.zeros((rows, LANES), jnp.float32)
    last = jnp.zeros((rows, LANES), jnp.float32)
    for j in range(planes + 1):
        own = state_ref[j] if j < planes else wet_ref[...].astype(jnp.float32)
        first = packed(first, own[:, :LANES], 0, EDGE * j)
        last = packed(last, own[:, cols - LANES :], LANES - EDGE, EDGE * j)
    first_ref[...] = first
    last_ref[...] = last


def side_tile(west, west_at, east, east_at):
    lane = iota(west.shape, 1)
    right = pltpu.roll(east, (LANES - east_at) % LANES, 1)
    left = pltpu.roll(west, (2 * LANES - EDGE - west_at) % LANES, 1)
    return jnp.where(lane < EDGE, right, jnp.where(lane >= LANES - EDGE, left, 0.0))


def around(field):
    rows, cols = field.shape
    return (
        pltpu.roll(field, cols - 1, 1),
        pltpu.roll(field, 1, 1),
        pltpu.roll(field, rows - 1, 0),
        pltpu.roll(field, 1, 0),
    )


def around_between(field, north_row, south_row):
    east, west, north, south = around(field)
    row = iota(field.shape, 0)
    return east, west, jnp.where(row == field.shape[0] - 1, north_row, north), jnp.where(row == 0, south_row, south)


def moved(load, near, levels, z):
    upper, lower = min(z + 1, levels - 1), max(z - 1, 0)
    results = []
    fields = [load(f * levels + z) for f in range(3)]
    tracer, across, along = fields
    around_tracer = near(z, tracer)
    east, west, north, south = around_tracer
    ddx, ddy = 0.5 * (east - west), 0.5 * (north - south)
    extra = (ADV * (across * ddx + along * ddy), PG * ddx, PG * ddy)
    for f, centre in enumerate(fields):
        sides = around_tracer if f == 0 else near(f * levels + z, centre)
        lap = (sides[0] + sides[1]) + (sides[2] + sides[3]) - 4.0 * centre
        lapz = load(f * levels + upper) + load(f * levels + lower) - 2.0 * centre
        results.append(centre + KH * lap + KZ * lapz - extra[f])
    return results


def added(sign, along, tracer, across_near, along_near):
    return [
        (KH - sign * 0.5 * ADV * along) * tracer,
        KH * across_near,
        KH * along_near - sign * 0.5 * PG * tracer,
    ]


def begin_body(state_ref, wet_ref, west_ref, east_ref, full_ref, mask_ref, begun_ref, token_ref):
    planes, rows, cols = state_ref.shape
    levels = planes // 3
    west, east = west_ref[...], east_ref[...]
    for j in range(planes):
        full_ref[j, :, :cols] = state_ref[j]
        full_ref[j, :, cols:] = side_tile(west, EDGE * j, east, EDGE * j)
    mask_ref[:, :cols] = wet_ref[...].astype(jnp.float32)
    mask_ref[:, cols:] = side_tile(west, EDGE * planes, east, EDGE * planes)
    for z in range(levels):
        values = moved(lambda j: full_ref[j], lambda j, field: around_between(field, 0.0, 0.0), levels, z)
        for f, value in enumerate(values):
            begun_ref[f * levels + z] = value
    token_ref[...] = jnp.zeros_like(token_ref)


def outer_body(force_ref, edge_ref, state_ref, wet_ref, west_ref, east_ref, *refs):
    sides, (up_ref, down_ref) = refs[:-2], refs[-2:]
    planes, rows, cols = state_ref.shape
    moving = 2 * planes // 3
    ends = ((up_ref, slice(rows - RIM, rows)), (down_ref, slice(0, RIM)))
    for out_ref, at in ends:
        out_ref[:moving] = force_ref[:moving, at] * FORCE_SCALE
        out_ref[moving : moving + planes] = state_ref[:, at] * STATE_SCALE
        out_ref[moving + planes] = wet_ref[at].astype(jnp.float32) * STATE_SCALE
        parts = [west_ref[at], east_ref[at], edge_ref[at]] + [side[at] for side in sides]
        for k, part in enumerate(parts):
            lane = (k % 2) * LANES
            out_ref[moving + planes + 1 + k // 2, :, lane : lane + LANES] = part * (STATE_SCALE if k < 2 else FORCE_SCALE)


def steps_body(sides, devices, full_ref, mask_ref, begun_ref, force_ref, edge_ref, north_ref, south_ref, *refs):
    side_refs = refs[:sides]
    state_ref, parts_ref, push_ref, halo_ref, one_ref, two_ref = refs[sides:]
    planes, rows, wide = full_ref.shape
    levels = planes // 3
    cols = wide - LANES
    total = rows + 2 * RIM
    moving = 2 * levels
    last = rows - 2 * RIM

    def joined(index):
        both = jnp.concatenate([north_ref[index], south_ref[index]], axis=0)
        if index > moving + planes:
            return both
        return both * (1.0 / (FORCE_SCALE if index < moving else STATE_SCALE))

    pairs = [joined(moving + planes + 1 + k) for k in range((sides + 4) // 2)]
    outer = [
        pairs[k // 2][:, (k % 2) * LANES : (k % 2 + 1) * LANES] * (1.0 / (STATE_SCALE if k < 2 else FORCE_SCALE))
        for k in range(3 + sides)
    ]
    edges = [jnp.concatenate([side[...], outer[3 + k]], axis=0) for k, side in enumerate(side_refs)]
    west, east = edges[0], edges[-1]
    own = jnp.concatenate([edge_ref[...], outer[2]], axis=0)

    def counts(edge):
        return jnp.broadcast_to(edge[:, LANES - 1 :], (total, LANES))

    lane = iota((total, LANES), 1)
    count_side = jnp.where(lane < LANES // 2, counts(east), counts(west))
    count = jnp.concatenate([counts(own)] * (cols // LANES) + [count_side], axis=1)

    def halo(index, at):
        return jnp.concatenate([joined(index), side_tile(outer[0], at, outer[1], at)], axis=1)

    mask = jnp.concatenate([mask_ref[...], halo(moving + planes, EDGE * planes)], axis=0)
    relax = mask / (1.0 + GAMMA * count)
    half = GAMMA * relax

    for j in range(moving):
        tile = side_tile(west, EDGE * (moving + j), east, EDGE * j)
        whole = jnp.concatenate([force_ref[j], joined(j)], axis=0)
        push_ref[j, :, :cols] = whole * half[:, :cols]
        push_ref[j, :, cols:] = tile * half[:, cols:]
    for j in range(planes):
        halo_ref[j] = halo(moving + j, EDGE * j)

    def finish(values, z, at=(slice(None),)):
        tracer, across, along = values
        rated = relax[at]
        return (tracer * rated + push_ref[(z, *at)], across * rated, along * rated + push_ref[(levels + z, *at)])

    row = iota((2 * RIM, wide), 0)
    head, tail = slice(0, 2 * RIM), slice(last, rows)

    def near(j, field):
        return around_between(field, full_ref[j, :1], full_ref[j, rows - 1 :])

    for z in range(levels):
        index = [f * levels + z for f in range(3)]
        beyond = [halo_ref[j] for j in index]
        north = [jnp.where(row == 2 * RIM - 1, value[:1], 0.0) for value in beyond]
        south = [jnp.where(row == 0, value[2 * RIM - 1 :], 0.0) for value in beyond]
        first = added(-1.0, full_ref[index[2], head], *south)
        final = added(1.0, full_ref[index[2], tail], *north)
        blocks = (
            (head, [begun_ref[j, head] + extra for j, extra in zip(index, first)]),
            (slice(2 * RIM, last), [begun_ref[j, 2 * RIM : last] for j in index]),
            (tail, [begun_ref[j, tail] + extra for j, extra in zip(index, final)]),
            (slice(rows, total), moved(lambda j: halo_ref[j], near, levels, z)),
        )
        for at, values in blocks:
            for j, value in zip(index, finish(values, z, (at,))):
                one_ref[j, at] = value

    for z in range(levels):
        for f, value in enumerate(finish(moved(lambda j: one_ref[j], lambda j, field: around(field), levels, z), z)):
            two_ref[f * levels + z] = value
    share = 1.0 / (1.0 + count[:rows, :1])
    sums = [jnp.zeros((rows, cols), jnp.float32) for _ in range(3)]
    own_cols = (slice(None), slice(0, cols))
    for z in range(levels):
        values = moved(
            lambda j: two_ref[j, :, :cols],
            lambda j, field: tuple(side[:, :cols] for side in around(two_ref[j])),
            levels,
            z,
        )
        values = finish(values, z, own_cols)
        for f, value in enumerate(values):
            state_ref[f * levels + z] = value[:rows]
        tracer = values[0]
        inner = tracer[:rows]
        ddy = pltpu.roll(tracer, total - 1, 0)[:rows] - pltpu.roll(tracer, 1, 0)[:rows]
        sums[0] = sums[0] + values[2][:rows] * inner
        sums[1] = sums[1] + force_ref[moving + z] * inner
        sums[2] = sums[2] + ddy
    raw = [jnp.sum(value, axis=1, keepdims=True) for value in sums]
    raw = [raw[0], raw[1] * share, raw[2] * (-0.5 * DISPERSE)]
    row, lane = iota((rows, LANES), 0), iota((rows, LANES), 1)
    part = jnp.zeros((rows, LANES), jnp.float32)
    for q in range(3):
        part = part + jnp.where(lane == q * rows + row, raw[q], 0.0)
    part = jnp.sum(part, axis=0, keepdims=True)
    parts_ref[...] = jnp.broadcast_to(part, (devices, LANES))


def profile_body(across, along, me_ref, parts_ref, out_ref):
    rows = out_ref.shape[1]
    parts = parts_ref[...]
    devices = parts.shape[0]
    total = parts
    for k in range(1, across):
        total = total + pltpu.roll(parts, devices - k, 0)
    row = iota(parts.shape, 0)
    squares = jnp.sum(jnp.where(row % across == 0, total * total, 0.0), keepdims=True)
    scale = jnp.sqrt(squares / (3 * rows * along) + 1e-06)
    mine = jnp.sum(jnp.where(row == me_ref[0] * across, total, 0.0), axis=0, keepdims=True) / scale
    for q in range(3):
        out_ref[q : q + 1, :] = mine[:, q * rows : (q + 1) * rows]


def per_device(state, parent_rows, dest, pick, offset, wet):
    fields, levels, rows, cols = state.shape
    planes = fields * levels
    moving = 2 * levels
    along, across = lax.axis_size("gy"), lax.axis_size("gx")
    capacity = 2 * SEND // along
    slots = along * capacity
    total, wide = rows + 2 * RIM, cols + LANES
    f32 = jnp.float32
    even_pairs = [(i, i ^ 1) for i in range(along)]
    odd_pairs = [(i, ((i + 1) ^ 1) - 1) for i in range(1, along - 1)]
    eastward = [(i, i + 1) for i in range(across - 1)]
    westward = [(i + 1, i) for i in range(across - 1)]

    payload = call(
        functools.partial(gather_body, capacity, slots),
        jax.ShapeDtypeStruct((slots, planes * cols + LANES), jnp.bfloat16),
        flops=2 * 8 * slots * SEND * planes * cols,
        moved=2 * (SEND + slots) * planes * cols,
        limit=VMEM_MOST,
        in_specs=[pl.BlockSpec(memory_space=pl.ANY)] * 4,
        out_specs=pl.BlockSpec(memory_space=pl.ANY),
        scratch_shapes=[pltpu.VMEM((1, SEND), jnp.int32)] * 3
        + [
            pltpu.VMEM(parent_rows.shape, jnp.bfloat16),
            pltpu.VMEM((slots, planes * cols + LANES), jnp.bfloat16),
            pltpu.SemaphoreType.DMA((4,)),
            pltpu.SemaphoreType.DMA((4,)),
        ],
    )(dest.reshape(1, SEND), pick.reshape(1, SEND), offset.reshape(1, SEND), parent_rows)
    arrived = lax.all_to_all(payload, "gy", split_axis=0, concat_axis=0, tiled=True)

    cells = state.reshape(planes, rows, cols)
    packed_side = jax.ShapeDtypeStruct((rows, LANES), f32)
    first, last = call(sides_body, (packed_side, packed_side), moved=4 * planes * rows * cols)(cells, wet)
    from_west = lax.ppermute(last, "gx", eastward)
    from_east = lax.ppermute(first, "gx", westward)
    own_wide = jax.ShapeDtypeStruct((planes, rows, wide), f32)
    full, mask, begun, token = call(
        begin_body,
        (own_wide, jax.ShapeDtypeStruct((rows, wide), f32), own_wide, jax.ShapeDtypeStruct((8, LANES), f32)),
        flops=20 * planes * rows * wide,
        moved=12 * planes * rows * wide,
    )(cells, wet, from_west, from_east)

    force, edge = call(
        functools.partial(landing_body, planes, cols),
        (jax.ShapeDtypeStruct((planes, rows, cols), f32), packed_side),
        flops=2 * rows * slots * planes * cols,
        moved=2 * slots * planes * cols + 4 * rows * planes * cols,
    )(token, arrived)
    if across == 2:
        sides = [lax.ppermute(edge, "gx", [(0, 1), (1, 0)])]
    else:
        sides = [lax.ppermute(edge, "gx", eastward), lax.ppermute(edge, "gx", westward)]
    outer = jax.ShapeDtypeStruct((moving + planes + 1 + (len(sides) + 4) // 2, RIM, cols), f32)
    up, down = call(outer_body, (outer, outer), moved=16 * (moving + planes) * RIM * cols)(
        force, edge, cells, wet, from_west, from_east, *sides
    )
    even = lax.axis_index("gy") % 2 == 0
    far = lax.ppermute(jnp.where(even, down, up).astype(jnp.float16), "gy", odd_pairs).astype(f32)
    near = lax.ppermute(jnp.where(even, up, down).astype(jnp.float16), "gy", even_pairs).astype(f32)
    above, below = jnp.where(even, near, far), jnp.where(even, far, near)
    new_state, parts = call(
        functools.partial(steps_body, len(sides), along * across),
        (jax.ShapeDtypeStruct((planes, rows, cols), f32), jax.ShapeDtypeStruct((along * across, LANES), f32)),
        flops=60 * planes * total * wide,
        moved=8 * planes * total * wide,
        scratch_shapes=[
            pltpu.VMEM((moving, total, wide), f32),
            pltpu.VMEM((planes, 2 * RIM, wide), f32),
            pltpu.VMEM((planes, total, wide), f32),
            pltpu.VMEM((planes, total, wide), f32),
        ],
    )(full, mask, begun, force, edge, above, below, *sides)
    every = lax.all_to_all(parts, ("gy", "gx"), split_axis=0, concat_axis=0, tiled=True)
    me = lax.axis_index("gy").astype(jnp.int32).reshape(1)
    profile = call(
        functools.partial(profile_body, across, along),
        jax.ShapeDtypeStruct((3, rows), f32),
        in_specs=[pl.BlockSpec(memory_space=pltpu.SMEM), pl.BlockSpec(memory_space=pltpu.VMEM)],
    )(me, every)
    return new_state.reshape(state.shape), profile


def solution(mesh):
    in_specs = (
        P(None, None, "gy", "gx"),
        P(("gy", "gx"), None, None),
        P(("gy", "gx"), None),
        P(("gy", "gx")),
        P(("gy", "gx")),
        P("gy", "gx"),
    )
    out_specs = (P(None, None, "gy", "gx"), P(None, "gy"))
    return jax.shard_map(
        per_device, mesh=mesh, in_specs=in_specs, out_specs=out_specs, check_vma=False
    )
```

```python
import functools

import jax
import jax.numpy as jnp
from jax import lax
from jax.experimental import pallas as pl
from jax.experimental.pallas import tpu as pltpu
from jax.sharding import PartitionSpec as P

SEND = 64
STEPS = 3

KH = 0.2
KZ = 0.05
ADV = 0.25
PG = 0.5
GAMMA = 0.5
DISPERSE = 2.0

EDGE = 3
RIM = 4
LANES = 128
STATE_SCALE = 8192.0
FORCE_SCALE = 64.0
VMEM_LIMIT = 16 * 1024 * 1024
VMEM_MOST = 60 * 1024 * 1024


def call(body, out_shape, flops=0, moved=0, limit=VMEM_LIMIT, **more):
    return pl.pallas_call(
        body,
        out_shape=out_shape,
        compiler_params=pltpu.CompilerParams(vmem_limit_bytes=limit),
        cost_estimate=pl.CostEstimate(flops=flops, bytes_accessed=moved, transcendentals=0),
        **more,
    )


def iota(shape, dim):
    return lax.broadcasted_iota(jnp.int32, shape, dim)


def gather_body(capacity, slots, *refs):
    sources, out_ref, targets, held_ref, copied, sent = refs[:4], refs[4], refs[5:9], refs[9], refs[10], refs[11]
    copies = [
        pltpu.make_async_copy(source, target, copied.at[k]) for k, (source, target) in enumerate(zip(sources, targets))
    ]
    for copy in copies:
        copy.start()
    dest_ref, pick_ref, offset_ref, rows_ref = targets
    send, planes, cols = rows_ref.shape
    for copy in copies[:3]:
        copy.wait()
    dest = dest_ref[...]
    eye = iota((send, send), 0) == iota((send, send), 1)
    dest_column = jnp.sum(jnp.where(eye, dest, 0), axis=1, keepdims=True)
    earlier = (dest_column == dest) & (iota((send, send), 0) < iota((send, send), 1))
    rank = jnp.sum(earlier.astype(jnp.int32), axis=0, keepdims=True)
    slot_of = dest * capacity + rank
    taken = iota((slots, send), 0) == slot_of
    source = jnp.sum(jnp.where(taken, pick_ref[...] + 1, 0), axis=1, keepdims=True) - 1
    label = jnp.sum(jnp.where(taken, offset_ref[...] + 1, 0), axis=1, keepdims=True)
    group = 8
    lane = iota((slots, send * group), 1)
    select = jnp.concatenate(
        [(lane == source * group + j).astype(jnp.float32).astype(jnp.bfloat16) for j in range(group)], axis=0
    )
    width = planes * cols
    held_ref[:, width:] = jnp.broadcast_to(label, (slots, LANES)).astype(jnp.float32).astype(jnp.bfloat16)
    copies[3].wait()
    parts = []

    def send_columns(start, size):
        part = pltpu.make_async_copy(
            held_ref.at[:, pl.ds(start, size)], out_ref.at[:, pl.ds(start, size)], sent.at[len(parts)]
        )
        part.start()
        parts.append(part)

    send_columns(width, LANES)
    for g in range(planes // group):
        block = rows_ref[:, g * group : (g + 1) * group, :].reshape(send * group, cols)
        got = jnp.dot(select, block, preferred_element_type=jnp.float32).astype(jnp.bfloat16)
        for j in range(group):
            at = (g * group + j) * cols
            held_ref[:, at : at + cols] = got[j * slots : (j + 1) * slots]
        send_columns(g * group * cols, group * cols)
    for part in parts:
        part.wait()


def landing_body(planes, cols, token_ref, arrived_ref, force_ref, edge_ref):
    slots = arrived_ref.shape[0]
    rows = force_ref.shape[1]
    width = planes * cols
    label = arrived_ref[:, width:].astype(jnp.float32)
    landing = (label == (iota((slots, LANES), 1) + 1).astype(jnp.float32)).astype(jnp.float32)
    landing = landing.T[:rows].astype(jnp.bfloat16)
    count = jnp.dot(landing, jnp.ones((slots, LANES), jnp.bfloat16), preferred_element_type=jnp.float32)
    moving = 2 * planes // 3
    edge = count
    for j in range(planes):
        force = jnp.dot(landing, arrived_ref[:, j * cols : (j + 1) * cols], preferred_element_type=jnp.float32)
        force_ref[j] = force
        if j < moving:
            edge = packed(edge, force[:, :LANES], 0, EDGE * j)
            edge = packed(edge, force[:, cols - LANES :], LANES - EDGE, EDGE * (moving + j))
    edge_ref[...] = edge


def packed(into, tile, start, at):
    lane = iota(tile.shape, 1)
    shifted = pltpu.roll(tile, (at - start) % LANES, 1)
    return jnp.where((lane >= at) & (lane < at + EDGE), shifted, into)


def sides_body(state_ref, wet_ref, first_ref, last_ref):
    planes, rows, cols = state_ref.shape
    first = jnp.zeros((rows, LANES), jnp.float32)
    last = jnp.zeros((rows, LANES), jnp.float32)
    for j in range(planes + 1):
        own = state_ref[j] if j < planes else wet_ref[...].astype(jnp.float32)
        first = packed(first, own[:, :LANES], 0, EDGE * j)
        last = packed(last, own[:, cols - LANES :], LANES - EDGE, EDGE * j)
    first_ref[...] = first
    last_ref[...] = last


def side_tile(west, west_at, east, east_at):
    lane = iota(west.shape, 1)
    right = pltpu.roll(east, (LANES - east_at) % LANES, 1)
    left = pltpu.roll(west, (2 * LANES - EDGE - west_at) % LANES, 1)
    return jnp.where(lane < EDGE, right, jnp.where(lane >= LANES - EDGE, left, 0.0))


def around(field):
    rows, cols = field.shape
    return (
        pltpu.roll(field, cols - 1, 1),
        pltpu.roll(field, 1, 1),
        pltpu.roll(field, rows - 1, 0),
        pltpu.roll(field, 1, 0),
    )


def around_between(field, north_row, south_row):
    east, west, north, south = around(field)
    row = iota(field.shape, 0)
    return east, west, jnp.where(row == field.shape[0] - 1, north_row, north), jnp.where(row == 0, south_row, south)


def moved(load, near, levels, z):
    upper, lower = min(z + 1, levels - 1), max(z - 1, 0)
    results = []
    fields = [load(f * levels + z) for f in range(3)]
    tracer, across, along = fields
    around_tracer = near(z, tracer)
    east, west, north, south = around_tracer
    ddx, ddy = 0.5 * (east - west), 0.5 * (north - south)
    extra = (ADV * (across * ddx + along * ddy), PG * ddx, PG * ddy)
    for f, centre in enumerate(fields):
        sides = around_tracer if f == 0 else near(f * levels + z, centre)
        lap = (sides[0] + sides[1]) + (sides[2] + sides[3]) - 4.0 * centre
        lapz = load(f * levels + upper) + load(f * levels + lower) - 2.0 * centre
        results.append(centre + KH * lap + KZ * lapz - extra[f])
    return results


def added(sign, along, tracer, across_near, along_near):
    return [
        (KH - sign * 0.5 * ADV * along) * tracer,
        KH * across_near,
        KH * along_near - sign * 0.5 * PG * tracer,
    ]


def begin_body(state_ref, wet_ref, west_ref, east_ref, full_ref, mask_ref, begun_ref, token_ref):
    planes, rows, cols = state_ref.shape
    levels = planes // 3
    west, east = west_ref[...], east_ref[...]
    for j in range(planes):
        full_ref[j, :, :cols] = state_ref[j]
        full_ref[j, :, cols:] = side_tile(west, EDGE * j, east, EDGE * j)
    mask_ref[:, :cols] = wet_ref[...].astype(jnp.float32)
    mask_ref[:, cols:] = side_tile(west, EDGE * planes, east, EDGE * planes)
    for z in range(levels):
        values = moved(lambda j: full_ref[j], lambda j, field: around_between(field, 0.0, 0.0), levels, z)
        for f, value in enumerate(values):
            begun_ref[f * levels + z] = value
    token_ref[...] = jnp.zeros_like(token_ref)


def outer_body(force_ref, edge_ref, state_ref, wet_ref, west_ref, east_ref, *refs):
    sides, (up_ref, down_ref) = refs[:-2], refs[-2:]
    planes, rows, cols = state_ref.shape
    moving = 2 * planes // 3
    ends = ((up_ref, slice(rows - RIM, rows)), (down_ref, slice(0, RIM)))
    for out_ref, at in ends:
        out_ref[:moving] = force_ref[:moving, at] * FORCE_SCALE
        out_ref[moving : moving + planes] = state_ref[:, at] * STATE_SCALE
        out_ref[moving + planes] = wet_ref[at].astype(jnp.float32) * STATE_SCALE
        parts = [west_ref[at], east_ref[at], edge_ref[at]] + [side[at] for side in sides]
        for k, part in enumerate(parts):
            lane = (k % 2) * LANES
            out_ref[moving + planes + 1 + k // 2, :, lane : lane + LANES] = part * (STATE_SCALE if k < 2 else FORCE_SCALE)


def factors(mask, own, west, east, force_rows, push_ref):
    moving, total, wide = push_ref.shape
    cols = wide - LANES

    def counts(edge):
        return jnp.broadcast_to(edge[:, LANES - 1 :], (total, LANES))

    lane = iota((total, LANES), 1)
    count_side = jnp.where(lane < LANES // 2, counts(east), counts(west))
    relax = mask / (1.0 + GAMMA * jnp.concatenate([counts(own)] * (cols // LANES) + [count_side], axis=1))
    half = GAMMA * relax
    for j in range(moving):
        push_ref[j, :, :cols] = force_rows(j) * half[:, :cols]
        push_ref[j, :, cols:] = side_tile(west, EDGE * (moving + j), east, EDGE * j) * half[:, cols:]
    return relax


def finish(relax, push_ref, levels, values, z, at=(slice(None),)):
    tracer, across, along = values
    rated = relax[at]
    return (tracer * rated + push_ref[(z, *at)], across * rated, along * rated + push_ref[(levels + z, *at)])


def two_more(relax, push_ref, one_ref, two_ref, last):
    levels = one_ref.shape[0] // 3
    cols = one_ref.shape[2] - LANES
    for z in range(levels):
        values = moved(lambda j: one_ref[j], lambda j, field: around(field), levels, z)
        for f, value in enumerate(finish(relax, push_ref, levels, values, z)):
            two_ref[f * levels + z] = value
    for z in range(levels):
        values = moved(
            lambda j: two_ref[j, :, :cols],
            lambda j, field: tuple(side[:, :cols] for side in around(two_ref[j])),
            levels,
            z,
        )
        last(z, finish(relax, push_ref, levels, values, z, (slice(None), slice(0, cols))))


def terms(values, stokes):
    rows, total = stokes.shape[0], values[0].shape[0]
    tracer = values[0]
    ddy = pltpu.roll(tracer, total - 1, 0)[:rows] - pltpu.roll(tracer, 1, 0)[:rows]
    return [values[2][:rows] * tracer[:rows], stokes * tracer[:rows], ddy]


def transports(sums, count, child, all_rows):
    raw = [jnp.sum(value, axis=1, keepdims=True) for value in sums]
    raw = [raw[0], raw[1] / (1.0 + count), raw[2] * (-0.5 * DISPERSE)]
    lane = iota(child.shape, 1)
    part = jnp.zeros(child.shape, jnp.float32)
    for q in range(3):
        part = part + jnp.where((child >= 0) & (lane == q * all_rows + child), raw[q], 0.0)
    return jnp.sum(part, axis=0, keepdims=True)


def inner_body(mask_ref, begun_ref, force_ref, edge_ref, *refs):
    side_refs, (middle_ref, ends_ref, part_ref, push_ref, one_ref, two_ref) = refs[:-6], refs[-6:]
    planes, rows, wide = begun_ref.shape
    levels = planes // 3
    cols = wide - LANES
    moving = 2 * levels
    tile = 2 * RIM
    relax = factors(
        mask_ref[...], edge_ref[...], side_refs[0][...], side_refs[-1][...], lambda j: force_ref[j], push_ref
    )
    for z in range(levels):
        index = [f * levels + z for f in range(3)]
        for j, value in zip(index, finish(relax, push_ref, levels, [begun_ref[j] for j in index], z)):
            one_ref[j] = value
    sums = [jnp.zeros((rows, cols), jnp.float32) for _ in range(3)]

    def last(z, values):
        for f, value in enumerate(values):
            middle_ref[f, z] = value[tile : rows - tile]
            ends_ref[f, z, :tile] = value[:tile]
            ends_ref[f, z, tile:] = value[rows - tile :]
        for q, term in enumerate(terms(values, force_ref[moving + z])):
            sums[q] = sums[q] + term

    two_more(relax, push_ref, one_ref, two_ref, last)
    row = iota((rows, LANES), 0)
    child = jnp.where((row >= RIM) & (row < rows - RIM), row, -1)
    part_ref[...] = transports(sums, edge_ref[:, LANES - 1 :], child, rows)


def steps_body(
    sides, full_ref, mask_ref, begun_ref, force_ref, edge_ref, north_ref, south_ref, middle_ref, ends_ref, part_ref, *refs
):
    side_refs = refs[:sides]
    state_ref, parts_ref, push_ref, halo_ref, one_ref, two_ref, held_ref, sent = refs[sides:]
    planes, rows, wide = full_ref.shape
    levels = planes // 3
    cols = wide - LANES
    moving = 2 * levels
    tile = 2 * RIM
    own_rows, total = 2 * tile, 3 * tile
    tail = slice(rows - tile, rows)
    copies = [pltpu.make_async_copy(middle_ref, state_ref.at[:, :, pl.ds(tile, rows - 2 * tile)], sent.at[0])]
    copies[0].start()

    def slab(ref, *index):
        return [ref[(*index, slice(0, tile))], ref[(*index, tail)]]

    def joined(index):
        both = jnp.concatenate([north_ref[index], south_ref[index]], axis=0)
        if index > moving + planes:
            return both
        return both * (1.0 / (FORCE_SCALE if index < moving else STATE_SCALE))

    pairs = [joined(moving + planes + 1 + k) for k in range((sides + 4) // 2)]
    outer = [
        pairs[k // 2][:, (k % 2) * LANES : (k % 2 + 1) * LANES] * (1.0 / (STATE_SCALE if k < 2 else FORCE_SCALE))
        for k in range(3 + sides)
    ]
    edges = [jnp.concatenate([*slab(side), outer[3 + k]], axis=0) for k, side in enumerate(side_refs)]
    own = jnp.concatenate([*slab(edge_ref), outer[2]], axis=0)

    def halo(index, at):
        return jnp.concatenate([joined(index), side_tile(outer[0], at, outer[1], at)], axis=1)

    mask = jnp.concatenate([*slab(mask_ref), halo(moving + planes, EDGE * planes)], axis=0)
    relax = factors(
        mask,
        own,
        edges[0],
        edges[-1],
        lambda j: jnp.concatenate([*slab(force_ref, j), joined(j)], axis=0),
        push_ref,
    )
    for j in range(planes):
        halo_ref[j] = halo(moving + j, EDGE * j)
    row = iota((tile, wide), 0)

    def near(j, field):
        return around_between(field, full_ref[j, :1], full_ref[j, rows - 1 :])

    for z in range(levels):
        index = [f * levels + z for f in range(3)]
        beyond = [halo_ref[j] for j in index]
        north = [jnp.where(row == tile - 1, value[:1], 0.0) for value in beyond]
        south = [jnp.where(row == 0, value[tile - 1 :], 0.0) for value in beyond]
        first = added(-1.0, full_ref[index[2], :tile], *south)
        final = added(1.0, full_ref[index[2], tail], *north)
        blocks = (
            [begun_ref[j, :tile] + extra for j, extra in zip(index, first)],
            [begun_ref[j, tail] + extra for j, extra in zip(index, final)],
            moved(lambda j: halo_ref[j], near, levels, z),
        )
        for k, values in enumerate(blocks):
            at = slice(k * tile, (k + 1) * tile)
            for j, value in zip(index, finish(relax, push_ref, levels, values, z, (at,))):
                one_ref[j, at] = value

    sums = [jnp.zeros((own_rows, cols), jnp.float32) for _ in range(3)]
    row = iota((tile, cols), 0)
    batch = levels // 2

    def last(z, values):
        for f, value in enumerate(values):
            held_ref[f, z, :tile] = jnp.where(row < RIM, value[:tile], ends_ref[f, z, :tile])
            held_ref[f, z, tile:] = jnp.where(row < RIM, ends_ref[f, z, tile:], value[tile:own_rows])
        stokes = jnp.concatenate(slab(force_ref, moving + z), axis=0)
        for q, term in enumerate(terms(values, stokes)):
            sums[q] = sums[q] + term
        if z % batch == batch - 1:
            at = pl.ds(z + 1 - batch, batch)
            for k, start in enumerate((0, rows - tile)):
                copies.append(
                    pltpu.make_async_copy(
                        held_ref.at[:, at, pl.ds(k * tile, tile)],
                        state_ref.at[:, at, pl.ds(start, tile)],
                        sent.at[len(copies)],
                    )
                )
                copies[-1].start()

    two_more(relax, push_ref, one_ref, two_ref, last)
    row = iota((own_rows, LANES), 0)
    child = jnp.where(row < RIM, row, jnp.where(row >= own_rows - RIM, row + rows - own_rows, -1))
    part = transports(sums, own[:own_rows, LANES - 1 :], child, rows) + part_ref[...]
    parts_ref[...] = jnp.broadcast_to(part, parts_ref.shape)
    for copy in copies:
        copy.wait()


def profile_body(across, along, me_ref, parts_ref, out_ref):
    rows = out_ref.shape[1]
    parts = parts_ref[...]
    devices = parts.shape[0]
    total = parts
    for k in range(1, across):
        total = total + pltpu.roll(parts, devices - k, 0)
    row = iota(parts.shape, 0)
    squares = jnp.sum(jnp.where(row % across == 0, total * total, 0.0), keepdims=True)
    scale = jnp.sqrt(squares / (3 * rows * along) + 1e-06)
    mine = jnp.sum(jnp.where(row == me_ref[0] * across, total, 0.0), axis=0, keepdims=True) / scale
    for q in range(3):
        out_ref[q : q + 1, :] = mine[:, q * rows : (q + 1) * rows]


def per_device(state, parent_rows, dest, pick, offset, wet):
    fields, levels, rows, cols = state.shape
    planes = fields * levels
    moving = 2 * levels
    along, across = lax.axis_size("gy"), lax.axis_size("gx")
    capacity = 2 * SEND // along
    slots = along * capacity
    wide = cols + LANES
    f32 = jnp.float32
    even_pairs = [(i, i ^ 1) for i in range(along)]
    odd_pairs = [(i, ((i + 1) ^ 1) - 1) for i in range(1, along - 1)]
    eastward = [(i, i + 1) for i in range(across - 1)]
    westward = [(i + 1, i) for i in range(across - 1)]

    payload = call(
        functools.partial(gather_body, capacity, slots),
        jax.ShapeDtypeStruct((slots, planes * cols + LANES), jnp.bfloat16),
        flops=2 * 8 * slots * SEND * planes * cols,
        moved=2 * (SEND + slots) * planes * cols,
        limit=VMEM_MOST,
        in_specs=[pl.BlockSpec(memory_space=pl.ANY)] * 4,
        out_specs=pl.BlockSpec(memory_space=pl.ANY),
        scratch_shapes=[pltpu.VMEM((1, SEND), jnp.int32)] * 3
        + [
            pltpu.VMEM(parent_rows.shape, jnp.bfloat16),
            pltpu.VMEM((slots, planes * cols + LANES), jnp.bfloat16),
            pltpu.SemaphoreType.DMA((4,)),
            pltpu.SemaphoreType.DMA((4,)),
        ],
    )(dest.reshape(1, SEND), pick.reshape(1, SEND), offset.reshape(1, SEND), parent_rows)
    arrived = lax.all_to_all(payload, "gy", split_axis=0, concat_axis=0, tiled=True)

    cells = state.reshape(planes, rows, cols)
    packed_side = jax.ShapeDtypeStruct((rows, LANES), f32)
    first, last = call(sides_body, (packed_side, packed_side), moved=4 * planes * rows * cols)(cells, wet)
    from_west = lax.ppermute(last, "gx", eastward)
    from_east = lax.ppermute(first, "gx", westward)
    own_wide = jax.ShapeDtypeStruct((planes, rows, wide), f32)
    full, mask, begun, token = call(
        begin_body,
        (own_wide, jax.ShapeDtypeStruct((rows, wide), f32), own_wide, jax.ShapeDtypeStruct((8, LANES), f32)),
        flops=20 * planes * rows * wide,
        moved=12 * planes * rows * wide,
    )(cells, wet, from_west, from_east)

    force, edge = call(
        functools.partial(landing_body, planes, cols),
        (jax.ShapeDtypeStruct((planes, rows, cols), f32), packed_side),
        flops=2 * rows * slots * planes * cols,
        moved=2 * slots * planes * cols + 4 * rows * planes * cols,
    )(token, arrived)
    if across == 2:
        sides = [lax.ppermute(edge, "gx", [(0, 1), (1, 0)])]
    else:
        sides = [lax.ppermute(edge, "gx", eastward), lax.ppermute(edge, "gx", westward)]
    outer = jax.ShapeDtypeStruct((moving + planes + 1 + (len(sides) + 4) // 2, RIM, cols), f32)
    up, down = call(outer_body, (outer, outer), moved=16 * (moving + planes) * RIM * cols)(
        force, edge, cells, wet, from_west, from_east, *sides
    )
    even = lax.axis_index("gy") % 2 == 0
    far = lax.ppermute(jnp.where(even, down, up).astype(jnp.float16), "gy", odd_pairs).astype(f32)
    near = lax.ppermute(jnp.where(even, up, down).astype(jnp.float16), "gy", even_pairs).astype(f32)
    above, below = jnp.where(even, near, far), jnp.where(even, far, near)
    tile = 2 * RIM
    middle, ends, part = call(
        inner_body,
        (
            jax.ShapeDtypeStruct((fields, levels, rows - 2 * tile, cols), f32),
            jax.ShapeDtypeStruct((fields, levels, 2 * tile, cols), f32),
            jax.ShapeDtypeStruct((1, LANES), f32),
        ),
        flops=60 * planes * rows * wide,
        moved=8 * planes * rows * wide,
        scratch_shapes=[
            pltpu.VMEM((moving, rows, wide), f32),
            pltpu.VMEM((planes, rows, wide), f32),
            pltpu.VMEM((planes, rows, wide), f32),
        ],
    )(mask, begun, force, edge, *sides)
    whole = pl.BlockSpec(memory_space=pltpu.VMEM)
    new_state, parts = call(
        functools.partial(steps_body, len(sides)),
        (jax.ShapeDtypeStruct(state.shape, f32), jax.ShapeDtypeStruct((along * across, LANES), f32)),
        flops=60 * planes * 3 * tile * wide,
        moved=8 * planes * 3 * tile * wide,
        in_specs=[whole] * (10 + len(sides)),
        out_specs=[pl.BlockSpec(memory_space=pl.ANY), whole],
        scratch_shapes=[
            pltpu.VMEM((moving, 3 * tile, wide), f32),
            pltpu.VMEM((planes, tile, wide), f32),
            pltpu.VMEM((planes, 3 * tile, wide), f32),
            pltpu.VMEM((planes, 3 * tile, wide), f32),
            pltpu.VMEM((fields, levels, 2 * tile, cols), f32),
            pltpu.SemaphoreType.DMA((5,)),
        ],
    )(full, mask, begun, force, edge, above, below, middle, ends, part, *sides)
    every = lax.all_to_all(parts, ("gy", "gx"), split_axis=0, concat_axis=0, tiled=True)
    me = lax.axis_index("gy").astype(jnp.int32).reshape(1)
    profile = call(
        functools.partial(profile_body, across, along),
        jax.ShapeDtypeStruct((3, rows), f32),
        in_specs=[pl.BlockSpec(memory_space=pltpu.SMEM), pl.BlockSpec(memory_space=pltpu.VMEM)],
    )(me, every)
    return new_state, profile


def solution(mesh):
    in_specs = (
        P(None, None, "gy", "gx"),
        P(("gy", "gx"), None, None),
        P(("gy", "gx"), None),
        P(("gy", "gx")),
        P(("gy", "gx")),
        P("gy", "gx"),
    )
    out_specs = (P(None, None, "gy", "gx"), P(None, "gy"))
    return jax.shard_map(
        per_device, mesh=mesh, in_specs=in_specs, out_specs=out_specs, check_vma=False
    )
```

```python
import functools

import jax
import jax.numpy as jnp
from jax import lax
from jax.experimental import pallas as pl
from jax.experimental.pallas import tpu as pltpu
from jax.sharding import PartitionSpec as P

SEND = 64
STEPS = 3

KH = 0.2
KZ = 0.05
ADV = 0.25
PG = 0.5
GAMMA = 0.5
DISPERSE = 2.0

EDGE = 3
RIM = 4
LANES = 128
STATE_SCALE = 8192.0
FORCE_SCALE = 64.0
SUM_SCALE = 128.0
VMEM_LIMIT = 16 * 1024 * 1024
VMEM_MOST = 60 * 1024 * 1024


def call(body, out_shape, flops=0, moved=0, limit=VMEM_LIMIT, **more):
    return pl.pallas_call(
        body,
        out_shape=out_shape,
        compiler_params=pltpu.CompilerParams(vmem_limit_bytes=limit),
        cost_estimate=pl.CostEstimate(flops=flops, bytes_accessed=moved, transcendentals=0),
        **more,
    )


def iota(shape, dim):
    return lax.broadcasted_iota(jnp.int32, shape, dim)


def gather_body(capacity, slots, far, *refs):
    sources, out_ref, targets, held_ref, copied, sent = refs[:4], refs[4], refs[5:9], refs[9], refs[10], refs[11]
    copies = [
        pltpu.make_async_copy(source, target, copied.at[k]) for k, (source, target) in enumerate(zip(sources, targets))
    ]
    for copy in copies:
        copy.start()
    dest_ref, pick_ref, offset_ref, rows_ref = targets
    send, planes, cols = rows_ref.shape
    for copy in copies[:3]:
        copy.wait()
    dest = dest_ref[...]
    eye = iota((send, send), 0) == iota((send, send), 1)
    dest_column = jnp.sum(jnp.where(eye, dest, 0), axis=1, keepdims=True)
    earlier = (dest_column == dest) & (iota((send, send), 0) < iota((send, send), 1))
    rank = jnp.sum(earlier.astype(jnp.int32), axis=0, keepdims=True)
    half = slots // capacity
    mine = lax.axis_index("gy") >= half
    there = (dest >= half) != mine if far else (dest >= half) == mine
    slot_of = jnp.where(there, jnp.where(dest >= half, dest - half, dest) * capacity + rank, -1)
    taken = iota((slots, send), 0) == slot_of
    source = jnp.sum(jnp.where(taken, pick_ref[...] + 1, 0), axis=1, keepdims=True) - 1
    label = jnp.sum(jnp.where(taken, offset_ref[...] + 1, 0), axis=1, keepdims=True)
    group = 8
    lane = iota((slots, send * group), 1)
    select = jnp.concatenate(
        [(lane == source * group + j).astype(jnp.float32).astype(jnp.bfloat16) for j in range(group)], axis=0
    )
    width = planes * cols
    held_ref[:, width:] = jnp.broadcast_to(label, (slots, LANES)).astype(jnp.float32).astype(jnp.bfloat16)
    copies[3].wait()
    parts = []

    def send_columns(start, size):
        part = pltpu.make_async_copy(
            held_ref.at[:, pl.ds(start, size)], out_ref.at[:, pl.ds(start, size)], sent.at[len(parts)]
        )
        part.start()
        parts.append(part)

    send_columns(width, LANES)
    for g in range(planes // group):
        block = rows_ref[:, g * group : (g + 1) * group, :].reshape(send * group, cols)
        got = jnp.dot(select, block, preferred_element_type=jnp.float32).astype(jnp.bfloat16)
        for j in range(group):
            at = (g * group + j) * cols
            held_ref[:, at : at + cols] = got[j * slots : (j + 1) * slots]
        send_columns(g * group * cols, group * cols)
    for part in parts:
        part.wait()


def landing_of(arrived_ref, rows):
    slots, width = arrived_ref.shape
    label = arrived_ref[:, width - LANES :].astype(jnp.float32)
    landing = (label == (iota((slots, LANES), 1) + 1).astype(jnp.float32)).astype(jnp.float32)
    return landing.T[:rows].astype(jnp.bfloat16)


def landed(landing, values):
    return jnp.dot(landing, values, preferred_element_type=jnp.float32)


def far_body(token_ref, arrived_ref, sums_ref):
    rows = sums_ref.shape[0]
    slots, width = arrived_ref.shape
    landing = landing_of(arrived_ref, rows)
    step = 2 * LANES
    for at in range(0, width - LANES, step):
        sums_ref[:, at : at + step] = landed(landing, arrived_ref[:, at : at + step]) * SUM_SCALE
    sums_ref[:, width - LANES :] = landed(landing, jnp.full((slots, LANES), SUM_SCALE, jnp.bfloat16))


def come_body(sums_ref, token_ref):
    token_ref[...] = jnp.zeros_like(token_ref)


def landing_body(planes, cols, token_ref, arrived_ref, sums_ref, force_ref, edge_ref):
    slots = arrived_ref.shape[0]
    rows = force_ref.shape[1]
    landing = landing_of(arrived_ref, rows)
    far = 1.0 / SUM_SCALE
    count = landed(landing, jnp.ones((slots, LANES), jnp.bfloat16)) + sums_ref[:, planes * cols :] * far
    moving = 2 * planes // 3
    edge = count
    for j in range(planes):
        at = slice(j * cols, (j + 1) * cols)
        force = landed(landing, arrived_ref[:, at]) + sums_ref[:, at] * far
        force_ref[j] = force
        if j < moving:
            edge = packed(edge, force[:, :LANES], 0, EDGE * j)
            edge = packed(edge, force[:, cols - LANES :], LANES - EDGE, EDGE * (moving + j))
    edge_ref[...] = edge


def packed(into, tile, start, at):
    lane = iota(tile.shape, 1)
    shifted = pltpu.roll(tile, (at - start) % LANES, 1)
    return jnp.where((lane >= at) & (lane < at + EDGE), shifted, into)


def sides_body(state_ref, wet_ref, first_ref, last_ref):
    planes, rows, cols = state_ref.shape
    first = jnp.zeros((rows, LANES), jnp.float32)
    last = jnp.zeros((rows, LANES), jnp.float32)
    for j in range(planes + 1):
        own = state_ref[j] if j < planes else wet_ref[...].astype(jnp.float32)
        first = packed(first, own[:, :LANES], 0, EDGE * j)
        last = packed(last, own[:, cols - LANES :], LANES - EDGE, EDGE * j)
    first_ref[...] = first
    last_ref[...] = last


def side_tile(west, west_at, east, east_at):
    lane = iota(west.shape, 1)
    right = pltpu.roll(east, (LANES - east_at) % LANES, 1)
    left = pltpu.roll(west, (2 * LANES - EDGE - west_at) % LANES, 1)
    return jnp.where(lane < EDGE, right, jnp.where(lane >= LANES - EDGE, left, 0.0))


def around(field):
    rows, cols = field.shape
    return (
        pltpu.roll(field, cols - 1, 1),
        pltpu.roll(field, 1, 1),
        pltpu.roll(field, rows - 1, 0),
        pltpu.roll(field, 1, 0),
    )


def around_between(field, north_row, south_row):
    east, west, north, south = around(field)
    row = iota(field.shape, 0)
    return east, west, jnp.where(row == field.shape[0] - 1, north_row, north), jnp.where(row == 0, south_row, south)


def moved(load, near, levels, z):
    upper, lower = min(z + 1, levels - 1), max(z - 1, 0)
    results = []
    fields = [load(f * levels + z) for f in range(3)]
    tracer, across, along = fields
    around_tracer = near(z, tracer)
    east, west, north, south = around_tracer
    ddx, ddy = 0.5 * (east - west), 0.5 * (north - south)
    extra = (ADV * (across * ddx + along * ddy), PG * ddx, PG * ddy)
    for f, centre in enumerate(fields):
        sides = around_tracer if f == 0 else near(f * levels + z, centre)
        lap = (sides[0] + sides[1]) + (sides[2] + sides[3]) - 4.0 * centre
        lapz = load(f * levels + upper) + load(f * levels + lower) - 2.0 * centre
        results.append(centre + KH * lap + KZ * lapz - extra[f])
    return results


def added(sign, along, tracer, across_near, along_near):
    return [
        (KH - sign * 0.5 * ADV * along) * tracer,
        KH * across_near,
        KH * along_near - sign * 0.5 * PG * tracer,
    ]


def begin_body(state_ref, wet_ref, west_ref, east_ref, tips_ref, mask_ref, begun_ref, token_ref, full_ref):
    planes, rows, cols = state_ref.shape
    levels = planes // 3
    tile = 2 * RIM
    west, east = west_ref[...], east_ref[...]
    for j in range(planes):
        full_ref[j, :, :cols] = state_ref[j]
        full_ref[j, :, cols:] = side_tile(west, EDGE * j, east, EDGE * j)
        tips_ref[j, :tile] = full_ref[j, :tile]
        tips_ref[j, tile:] = full_ref[j, rows - tile :]
    mask_ref[:, :cols] = wet_ref[...].astype(jnp.float32)
    mask_ref[:, cols:] = side_tile(west, EDGE * planes, east, EDGE * planes)
    for z in range(levels):
        values = moved(lambda j: full_ref[j], lambda j, field: around_between(field, 0.0, 0.0), levels, z)
        for f, value in enumerate(values):
            begun_ref[f * levels + z] = value
    token_ref[...] = jnp.zeros_like(token_ref)


def outer_body(force_ref, edge_ref, tips_ref, mask_ref, west_ref, east_ref, *refs):
    sides, (up_ref, down_ref) = refs[:-2], refs[-2:]
    planes, rows, cols = force_ref.shape
    moving = 2 * planes // 3
    ends = ((up_ref, slice(rows - RIM, rows), slice(3 * RIM, 4 * RIM)), (down_ref, slice(0, RIM), slice(0, RIM)))
    for out_ref, at, tip in ends:
        out_ref[:moving] = force_ref[:moving, at] * FORCE_SCALE
        out_ref[moving : moving + planes] = tips_ref[:, tip, :cols] * STATE_SCALE
        out_ref[moving + planes] = mask_ref[at, :cols] * STATE_SCALE
        parts = [west_ref[at], east_ref[at], edge_ref[at]] + [side[at] for side in sides]
        for k, part in enumerate(parts):
            lane = (k % 2) * LANES
            out_ref[moving + planes + 1 + k // 2, :, lane : lane + LANES] = part * (STATE_SCALE if k < 2 else FORCE_SCALE)


def factors(mask, own, west, east, force_rows, push_ref):
    moving, total, wide = push_ref.shape
    cols = wide - LANES

    def counts(edge):
        return jnp.broadcast_to(edge[:, LANES - 1 :], (total, LANES))

    lane = iota((total, LANES), 1)
    count_side = jnp.where(lane < LANES // 2, counts(east), counts(west))
    relax = mask / (1.0 + GAMMA * jnp.concatenate([counts(own)] * (cols // LANES) + [count_side], axis=1))
    half = GAMMA * relax
    for j in range(moving):
        push_ref[j, :, :cols] = force_rows(j) * half[:, :cols]
        push_ref[j, :, cols:] = side_tile(west, EDGE * (moving + j), east, EDGE * j) * half[:, cols:]
    return relax


def finish(relax, push_ref, levels, values, z, at=(slice(None),)):
    tracer, across, along = values
    rated = relax[at]
    return (tracer * rated + push_ref[(z, *at)], across * rated, along * rated + push_ref[(levels + z, *at)])


def two_more(relax, push_ref, one_ref, two_ref, last):
    levels = one_ref.shape[0] // 3
    cols = one_ref.shape[2] - LANES
    for z in range(levels):
        values = moved(lambda j: one_ref[j], lambda j, field: around(field), levels, z)
        for f, value in enumerate(finish(relax, push_ref, levels, values, z)):
            two_ref[f * levels + z] = value
    for z in range(levels):
        values = moved(
            lambda j: two_ref[j, :, :cols],
            lambda j, field: tuple(side[:, :cols] for side in around(two_ref[j])),
            levels,
            z,
        )
        last(z, finish(relax, push_ref, levels, values, z, (slice(None), slice(0, cols))))


def terms(values, stokes):
    rows, total = stokes.shape[0], values[0].shape[0]
    tracer = values[0]
    ddy = pltpu.roll(tracer, total - 1, 0)[:rows] - pltpu.roll(tracer, 1, 0)[:rows]
    return [values[2][:rows] * tracer[:rows], stokes * tracer[:rows], ddy]


def transports(sums, count, child, all_rows):
    raw = [jnp.sum(value, axis=1, keepdims=True) for value in sums]
    raw = [raw[0], raw[1] / (1.0 + count), raw[2] * (-0.5 * DISPERSE)]
    lane = iota(child.shape, 1)
    part = jnp.zeros(child.shape, jnp.float32)
    for q in range(3):
        part = part + jnp.where((child >= 0) & (lane == q * all_rows + child), raw[q], 0.0)
    return jnp.sum(part, axis=0, keepdims=True)


def inner_body(mask_ref, begun_ref, force_ref, edge_ref, *refs):
    side_refs, (middle_ref, ends_ref, part_ref, push_ref, one_ref, two_ref) = refs[:-6], refs[-6:]
    planes, rows, wide = begun_ref.shape
    levels = planes // 3
    cols = wide - LANES
    moving = 2 * levels
    tile = 2 * RIM
    relax = factors(
        mask_ref[...], edge_ref[...], side_refs[0][...], side_refs[-1][...], lambda j: force_ref[j], push_ref
    )
    for z in range(levels):
        index = [f * levels + z for f in range(3)]
        for j, value in zip(index, finish(relax, push_ref, levels, [begun_ref[j] for j in index], z)):
            one_ref[j] = value
    sums = [jnp.zeros((rows, cols), jnp.float32) for _ in range(3)]

    def last(z, values):
        for f, value in enumerate(values):
            middle_ref[f, z] = value[tile : rows - tile]
            ends_ref[f, z, :tile] = value[:tile]
            ends_ref[f, z, tile:] = value[rows - tile :]
        for q, term in enumerate(terms(values, force_ref[moving + z])):
            sums[q] = sums[q] + term

    two_more(relax, push_ref, one_ref, two_ref, last)
    row = iota((rows, LANES), 0)
    child = jnp.where((row >= RIM) & (row < rows - RIM), row, -1)
    part_ref[...] = transports(sums, edge_ref[:, LANES - 1 :], child, rows)


def steps_body(
    sides, tips_ref, mask_ref, begun_ref, force_ref, edge_ref, north_ref, south_ref, middle_ref, ends_ref, part_ref, *refs
):
    side_refs = refs[:sides]
    state_ref, parts_ref, push_ref, halo_ref, one_ref, two_ref, held_ref, sent = refs[sides:]
    planes, rows, wide = begun_ref.shape
    levels = planes // 3
    cols = wide - LANES
    moving = 2 * levels
    tile = 2 * RIM
    own_rows, total = 2 * tile, 3 * tile
    tail = slice(rows - tile, rows)
    copies = [pltpu.make_async_copy(middle_ref, state_ref.at[:, :, pl.ds(tile, rows - 2 * tile)], sent.at[0])]
    copies[0].start()

    def slab(ref, *index):
        return [ref[(*index, slice(0, tile))], ref[(*index, tail)]]

    def joined(index):
        both = jnp.concatenate([north_ref[index], south_ref[index]], axis=0)
        if index > moving + planes:
            return both
        return both * (1.0 / (FORCE_SCALE if index < moving else STATE_SCALE))

    pairs = [joined(moving + planes + 1 + k) for k in range((sides + 4) // 2)]
    outer = [
        pairs[k // 2][:, (k % 2) * LANES : (k % 2 + 1) * LANES] * (1.0 / (STATE_SCALE if k < 2 else FORCE_SCALE))
        for k in range(3 + sides)
    ]
    edges = [jnp.concatenate([*slab(side), outer[3 + k]], axis=0) for k, side in enumerate(side_refs)]
    own = jnp.concatenate([*slab(edge_ref), outer[2]], axis=0)

    def halo(index, at):
        return jnp.concatenate([joined(index), side_tile(outer[0], at, outer[1], at)], axis=1)

    mask = jnp.concatenate([*slab(mask_ref), halo(moving + planes, EDGE * planes)], axis=0)
    relax = factors(
        mask,
        own,
        edges[0],
        edges[-1],
        lambda j: jnp.concatenate([*slab(force_ref, j), joined(j)], axis=0),
        push_ref,
    )
    for j in range(planes):
        halo_ref[j] = halo(moving + j, EDGE * j)
    row = iota((tile, wide), 0)

    def near(j, field):
        return around_between(field, tips_ref[j, :1], tips_ref[j, own_rows - 1 :])

    for z in range(levels):
        index = [f * levels + z for f in range(3)]
        beyond = [halo_ref[j] for j in index]
        north = [jnp.where(row == tile - 1, value[:1], 0.0) for value in beyond]
        south = [jnp.where(row == 0, value[tile - 1 :], 0.0) for value in beyond]
        first = added(-1.0, tips_ref[index[2], :tile], *south)
        final = added(1.0, tips_ref[index[2], tile:], *north)
        blocks = (
            [begun_ref[j, :tile] + extra for j, extra in zip(index, first)],
            [begun_ref[j, tail] + extra for j, extra in zip(index, final)],
            moved(lambda j: halo_ref[j], near, levels, z),
        )
        for k, values in enumerate(blocks):
            at = slice(k * tile, (k + 1) * tile)
            for j, value in zip(index, finish(relax, push_ref, levels, values, z, (at,))):
                one_ref[j, at] = value

    sums = [jnp.zeros((own_rows, cols), jnp.float32) for _ in range(3)]
    row = iota((tile, cols), 0)
    batch = levels // 2

    def last(z, values):
        for f, value in enumerate(values):
            held_ref[f, z, :tile] = jnp.where(row < RIM, value[:tile], ends_ref[f, z, :tile])
            held_ref[f, z, tile:] = jnp.where(row < RIM, ends_ref[f, z, tile:], value[tile:own_rows])
        stokes = jnp.concatenate(slab(force_ref, moving + z), axis=0)
        for q, term in enumerate(terms(values, stokes)):
            sums[q] = sums[q] + term
        if z % batch == batch - 1:
            at = pl.ds(z + 1 - batch, batch)
            for k, start in enumerate((0, rows - tile)):
                copies.append(
                    pltpu.make_async_copy(
                        held_ref.at[:, at, pl.ds(k * tile, tile)],
                        state_ref.at[:, at, pl.ds(start, tile)],
                        sent.at[len(copies)],
                    )
                )
                copies[-1].start()

    two_more(relax, push_ref, one_ref, two_ref, last)
    row = iota((own_rows, LANES), 0)
    child = jnp.where(row < RIM, row, jnp.where(row >= own_rows - RIM, row + rows - own_rows, -1))
    part = transports(sums, own[:own_rows, LANES - 1 :], child, rows) + part_ref[...]
    parts_ref[...] = jnp.broadcast_to(part, parts_ref.shape)
    for copy in copies:
        copy.wait()


def profile_body(across, along, me_ref, parts_ref, out_ref):
    rows = out_ref.shape[1]
    parts = parts_ref[...]
    devices = parts.shape[0]
    total = parts
    for k in range(1, across):
        total = total + pltpu.roll(parts, devices - k, 0)
    row = iota(parts.shape, 0)
    squares = jnp.sum(jnp.where(row % across == 0, total * total, 0.0), keepdims=True)
    scale = jnp.sqrt(squares / (3 * rows * along) + 1e-06)
    mine = jnp.sum(jnp.where(row == me_ref[0] * across, total, 0.0), axis=0, keepdims=True) / scale
    for q in range(3):
        out_ref[q : q + 1, :] = mine[:, q * rows : (q + 1) * rows]


def per_device(state, parent_rows, dest, pick, offset, wet):
    fields, levels, rows, cols = state.shape
    planes = fields * levels
    moving = 2 * levels
    along, across = lax.axis_size("gy"), lax.axis_size("gx")
    capacity = 2 * SEND // along
    wide = cols + LANES
    f32 = jnp.float32
    even_pairs = [(i, i ^ 1) for i in range(along)]
    odd_pairs = [(i, ((i + 1) ^ 1) - 1) for i in range(1, along - 1)]
    eastward = [(i, i + 1) for i in range(across - 1)]
    westward = [(i + 1, i) for i in range(across - 1)]

    half = along // 2
    slots = half * capacity
    width = planes * cols + LANES
    halves = [list(range(half)), list(range(half, along))]

    def gathered(far):
        return call(
            functools.partial(gather_body, capacity, slots, far),
            jax.ShapeDtypeStruct((slots, width), jnp.bfloat16),
            flops=2 * 8 * slots * SEND * planes * cols,
            moved=2 * (SEND + slots) * planes * cols,
            limit=VMEM_MOST,
            in_specs=[pl.BlockSpec(memory_space=pl.ANY)] * 4,
            out_specs=pl.BlockSpec(memory_space=pl.ANY),
            scratch_shapes=[pltpu.VMEM((1, SEND), jnp.int32)] * 3
            + [
                pltpu.VMEM(parent_rows.shape, jnp.bfloat16),
                pltpu.VMEM((slots, width), jnp.bfloat16),
                pltpu.SemaphoreType.DMA((4,)),
                pltpu.SemaphoreType.DMA((4,)),
            ],
        )(dest.reshape(1, SEND), pick.reshape(1, SEND), offset.reshape(1, SEND), parent_rows)

    def exchanged(payload):
        return lax.all_to_all(payload, "gy", split_axis=0, concat_axis=0, tiled=True, axis_index_groups=halves)

    far_rows = exchanged(gathered(True))

    cells = state.reshape(planes, rows, cols)
    packed_side = jax.ShapeDtypeStruct((rows, LANES), f32)
    first, last = call(sides_body, (packed_side, packed_side), moved=4 * planes * rows * cols)(cells, wet)
    from_west = lax.ppermute(last, "gx", eastward)
    from_east = lax.ppermute(first, "gx", westward)
    own_wide = jax.ShapeDtypeStruct((planes, rows, wide), f32)
    tips, mask, begun, token = call(
        begin_body,
        (jax.ShapeDtypeStruct((planes, 4 * RIM, wide), f32), jax.ShapeDtypeStruct((rows, wide), f32), own_wide, jax.ShapeDtypeStruct((8, LANES), f32)),
        flops=20 * planes * rows * wide,
        moved=12 * planes * rows * wide,
        scratch_shapes=[pltpu.VMEM((planes, rows, wide), f32)],
    )(cells, wet, from_west, from_east)

    sums = call(
        far_body,
        jax.ShapeDtypeStruct((rows, width), f32),
        flops=2 * rows * slots * width,
        moved=2 * slots * width + 4 * rows * width,
    )(token, far_rows)
    mirrored = [(i, (i + half) % along) for i in range(along)]
    sums, near_rows = lax.optimization_barrier((sums.astype(jnp.float16), gathered(False)))
    sums = lax.ppermute(sums, "gy", mirrored)
    arrived = exchanged(near_rows)
    come = call(
        come_body,
        jax.ShapeDtypeStruct((8, LANES), f32),
        flops=10**11,
        in_specs=[pl.BlockSpec(memory_space=pl.ANY)],
    )(sums[:8, :LANES].astype(f32))
    sums, arrived = lax.optimization_barrier((sums, arrived))
    sums = sums.astype(f32)

    force, edge = call(
        functools.partial(landing_body, planes, cols),
        (jax.ShapeDtypeStruct((planes, rows, cols), f32), packed_side),
        flops=2 * rows * slots * planes * cols,
        moved=2 * slots * planes * cols + 4 * rows * planes * cols,
    )(come, arrived, sums)
    if across == 2:
        sides = [lax.ppermute(edge, "gx", [(0, 1), (1, 0)])]
    else:
        sides = [lax.ppermute(edge, "gx", eastward), lax.ppermute(edge, "gx", westward)]
    outer = jax.ShapeDtypeStruct((moving + planes + 1 + (len(sides) + 4) // 2, RIM, cols), f32)
    up, down = call(outer_body, (outer, outer), moved=16 * (moving + planes) * RIM * cols)(
        force, edge, tips, mask, from_west, from_east, *sides
    )
    even = lax.axis_index("gy") % 2 == 0
    far = lax.ppermute(jnp.where(even, down, up).astype(jnp.float16), "gy", odd_pairs).astype(f32)
    near = lax.ppermute(jnp.where(even, up, down).astype(jnp.float16), "gy", even_pairs).astype(f32)
    above, below = jnp.where(even, near, far), jnp.where(even, far, near)
    tile = 2 * RIM
    middle, ends, part = call(
        inner_body,
        (
            jax.ShapeDtypeStruct((fields, levels, rows - 2 * tile, cols), f32),
            jax.ShapeDtypeStruct((fields, levels, 2 * tile, cols), f32),
            jax.ShapeDtypeStruct((1, LANES), f32),
        ),
        flops=60 * planes * rows * wide,
        moved=8 * planes * rows * wide,
        scratch_shapes=[
            pltpu.VMEM((moving, rows, wide), f32),
            pltpu.VMEM((planes, rows, wide), f32),
            pltpu.VMEM((planes, rows, wide), f32),
        ],
    )(mask, begun, force, edge, *sides)
    whole = pl.BlockSpec(memory_space=pltpu.VMEM)
    new_state, parts = call(
        functools.partial(steps_body, len(sides)),
        (jax.ShapeDtypeStruct(state.shape, f32), jax.ShapeDtypeStruct((along * across, LANES), f32)),
        flops=60 * planes * 3 * tile * wide,
        moved=8 * planes * 3 * tile * wide,
        in_specs=[whole] * (10 + len(sides)),
        out_specs=[pl.BlockSpec(memory_space=pl.ANY), whole],
        scratch_shapes=[
            pltpu.VMEM((moving, 3 * tile, wide), f32),
            pltpu.VMEM((planes, tile, wide), f32),
            pltpu.VMEM((planes, 3 * tile, wide), f32),
            pltpu.VMEM((planes, 3 * tile, wide), f32),
            pltpu.VMEM((fields, levels, 2 * tile, cols), f32),
            pltpu.SemaphoreType.DMA((5,)),
        ],
    )(tips, mask, begun, force, edge, above, below, middle, ends, part, *sides)
    every = lax.all_to_all(parts, ("gy", "gx"), split_axis=0, concat_axis=0, tiled=True)
    me = lax.axis_index("gy").astype(jnp.int32).reshape(1)
    profile = call(
        functools.partial(profile_body, across, along),
        jax.ShapeDtypeStruct((3, rows), f32),
        in_specs=[pl.BlockSpec(memory_space=pltpu.SMEM), pl.BlockSpec(memory_space=pltpu.VMEM)],
    )(me, every)
    return new_state, profile


def solution(mesh):
    in_specs = (
        P(None, None, "gy", "gx"),
        P(("gy", "gx"), None, None),
        P(("gy", "gx"), None),
        P(("gy", "gx")),
        P(("gy", "gx")),
        P("gy", "gx"),
    )
    out_specs = (P(None, None, "gy", "gx"), P(None, "gy"))
    return jax.shard_map(
        per_device, mesh=mesh, in_specs=in_specs, out_specs=out_specs, check_vma=False
    )
```

```python
import functools

import jax
import jax.numpy as jnp
from jax import lax
from jax.experimental import pallas as pl
from jax.experimental.pallas import tpu as pltpu
from jax.sharding import PartitionSpec as P

SEND = 64
STEPS = 3

KH = 0.2
KZ = 0.05
ADV = 0.25
PG = 0.5
GAMMA = 0.5
DISPERSE = 2.0

EDGE = 3
RIM = 4
LANES = 128
STATE_SCALE = 8192.0
FORCE_SCALE = 64.0
SUM_SCALE = 128.0
VMEM_LIMIT = 16 * 1024 * 1024
VMEM_MOST = 60 * 1024 * 1024


def call(body, out_shape, flops=0, moved=0, limit=VMEM_LIMIT, **more):
    return pl.pallas_call(
        body,
        out_shape=out_shape,
        compiler_params=pltpu.CompilerParams(vmem_limit_bytes=limit),
        cost_estimate=pl.CostEstimate(flops=flops, bytes_accessed=moved, transcendentals=0),
        **more,
    )


def iota(shape, dim):
    return lax.broadcasted_iota(jnp.int32, shape, dim)


def gather_body(capacity, slots, far, *refs):
    if far:
        sources, out_ref, targets, held_ref, sent, copied = refs[:4], refs[4], refs[5:9], *refs[9:]
        copies = [
            pltpu.make_async_copy(source, target, copied.at[k])
            for k, (source, target) in enumerate(zip(sources, targets))
        ]
    else:
        targets, (out_ref, held_ref, sent), copies = refs[:4], refs[4:], []
    for copy in copies:
        copy.start()
    dest_ref, pick_ref, offset_ref, rows_ref = targets
    send, planes, cols = rows_ref.shape
    for copy in copies[:3]:
        copy.wait()
    dest = dest_ref[...]
    eye = iota((send, send), 0) == iota((send, send), 1)
    dest_column = jnp.sum(jnp.where(eye, dest, 0), axis=1, keepdims=True)
    earlier = (dest_column == dest) & (iota((send, send), 0) < iota((send, send), 1))
    rank = jnp.sum(earlier.astype(jnp.int32), axis=0, keepdims=True)
    half = slots // capacity
    mine = lax.axis_index("gy") >= half
    there = (dest >= half) != mine if far else (dest >= half) == mine
    slot_of = jnp.where(there, jnp.where(dest >= half, dest - half, dest) * capacity + rank, -1)
    taken = iota((slots, send), 0) == slot_of
    source = jnp.sum(jnp.where(taken, pick_ref[...] + 1, 0), axis=1, keepdims=True) - 1
    label = jnp.sum(jnp.where(taken, offset_ref[...] + 1, 0), axis=1, keepdims=True)
    group = 8
    lane = iota((slots, send * group), 1)
    select = jnp.concatenate(
        [(lane == source * group + j).astype(jnp.float32).astype(jnp.bfloat16) for j in range(group)], axis=0
    )
    width = planes * cols
    held_ref[:, width:] = jnp.broadcast_to(label, (slots, LANES)).astype(jnp.float32).astype(jnp.bfloat16)
    for copy in copies[3:]:
        copy.wait()
    parts = []

    def send_columns(start, size):
        part = pltpu.make_async_copy(
            held_ref.at[:, pl.ds(start, size)], out_ref.at[:, pl.ds(start, size)], sent.at[len(parts)]
        )
        part.start()
        parts.append(part)

    send_columns(width, LANES)
    for g in range(planes // group):
        block = rows_ref[:, g * group : (g + 1) * group, :].reshape(send * group, cols)
        got = jnp.dot(select, block, preferred_element_type=jnp.float32).astype(jnp.bfloat16)
        for j in range(group):
            at = (g * group + j) * cols
            held_ref[:, at : at + cols] = got[j * slots : (j + 1) * slots]
        send_columns(g * group * cols, group * cols)
    for part in parts:
        part.wait()


def landing_of(arrived_ref, rows):
    slots, width = arrived_ref.shape
    label = arrived_ref[:, width - LANES :].astype(jnp.float32)
    landing = (label == (iota((slots, LANES), 1) + 1).astype(jnp.float32)).astype(jnp.float32)
    return landing.T[:rows].astype(jnp.bfloat16)


def landed(landing, values):
    return jnp.dot(landing, values, preferred_element_type=jnp.float32)


def far_body(token_ref, arrived_ref, sums_ref):
    rows = sums_ref.shape[0]
    slots, width = arrived_ref.shape
    landing = landing_of(arrived_ref, rows)
    step = 2 * LANES
    for at in range(0, width - LANES, step):
        sums_ref[:, at : at + step] = landed(landing, arrived_ref[:, at : at + step]) * SUM_SCALE
    sums_ref[:, width - LANES :] = landed(landing, jnp.full((slots, LANES), SUM_SCALE, jnp.bfloat16))


def come_body(sums_ref, token_ref):
    token_ref[...] = jnp.zeros_like(token_ref)


def landing_body(planes, cols, token_ref, arrived_ref, sums_ref, force_ref, edge_ref):
    slots = arrived_ref.shape[0]
    rows = force_ref.shape[1]
    landing = landing_of(arrived_ref, rows)
    far = 1.0 / SUM_SCALE
    count = landed(landing, jnp.ones((slots, LANES), jnp.bfloat16)) + sums_ref[:, planes * cols :] * far
    moving = 2 * planes // 3
    edge = count
    for j in range(planes):
        at = slice(j * cols, (j + 1) * cols)
        force = landed(landing, arrived_ref[:, at]) + sums_ref[:, at] * far
        force_ref[j] = force
        if j < moving:
            edge = packed(edge, force[:, :LANES], 0, EDGE * j)
            edge = packed(edge, force[:, cols - LANES :], LANES - EDGE, EDGE * (moving + j))
    edge_ref[...] = edge


def packed(into, tile, start, at):
    lane = iota(tile.shape, 1)
    shifted = pltpu.roll(tile, (at - start) % LANES, 1)
    return jnp.where((lane >= at) & (lane < at + EDGE), shifted, into)


def sides_body(state_ref, wet_ref, first_ref, last_ref):
    planes, rows, cols = state_ref.shape
    first = jnp.zeros((rows, LANES), jnp.float32)
    last = jnp.zeros((rows, LANES), jnp.float32)
    for j in range(planes + 1):
        own = state_ref[j] if j < planes else wet_ref[...].astype(jnp.float32)
        first = packed(first, own[:, :LANES], 0, EDGE * j)
        last = packed(last, own[:, cols - LANES :], LANES - EDGE, EDGE * j)
    first_ref[...] = first
    last_ref[...] = last


def side_tile(west, west_at, east, east_at):
    lane = iota(west.shape, 1)
    right = pltpu.roll(east, (LANES - east_at) % LANES, 1)
    left = pltpu.roll(west, (2 * LANES - EDGE - west_at) % LANES, 1)
    return jnp.where(lane < EDGE, right, jnp.where(lane >= LANES - EDGE, left, 0.0))


def around(field):
    rows, cols = field.shape
    return (
        pltpu.roll(field, cols - 1, 1),
        pltpu.roll(field, 1, 1),
        pltpu.roll(field, rows - 1, 0),
        pltpu.roll(field, 1, 0),
    )


def around_between(field, north_row, south_row):
    east, west, north, south = around(field)
    row = iota(field.shape, 0)
    return east, west, jnp.where(row == field.shape[0] - 1, north_row, north), jnp.where(row == 0, south_row, south)


def moved(load, near, levels, z):
    upper, lower = min(z + 1, levels - 1), max(z - 1, 0)
    results = []
    fields = [load(f * levels + z) for f in range(3)]
    tracer, across, along = fields
    around_tracer = near(z, tracer)
    east, west, north, south = around_tracer
    ddx, ddy = 0.5 * (east - west), 0.5 * (north - south)
    extra = (ADV * (across * ddx + along * ddy), PG * ddx, PG * ddy)
    for f, centre in enumerate(fields):
        sides = around_tracer if f == 0 else near(f * levels + z, centre)
        lap = (sides[0] + sides[1]) + (sides[2] + sides[3]) - 4.0 * centre
        lapz = load(f * levels + upper) + load(f * levels + lower) - 2.0 * centre
        results.append(centre + KH * lap + KZ * lapz - extra[f])
    return results


def added(sign, along, tracer, across_near, along_near):
    return [
        (KH - sign * 0.5 * ADV * along) * tracer,
        KH * across_near,
        KH * along_near - sign * 0.5 * PG * tracer,
    ]


def begin_body(state_ref, wet_ref, west_ref, east_ref, tips_ref, mask_ref, begun_ref, packs_ref, token_ref, full_ref):
    planes, rows, cols = state_ref.shape
    levels = planes // 3
    tile = 2 * RIM
    west, east = west_ref[...], east_ref[...]
    tips_ref[:, :tile] = state_ref[:, :tile]
    tips_ref[:, tile:] = state_ref[:, rows - tile :]
    for j in range(planes):
        full_ref[j, :, :cols] = state_ref[j]
        full_ref[j, :, cols:] = side_tile(west, EDGE * j, east, EDGE * j)
    mask_ref[:, :cols] = wet_ref[...].astype(jnp.float32)
    mask_ref[:, cols:] = side_tile(west, EDGE * planes, east, EDGE * planes)
    packs = [jnp.zeros((rows, LANES), jnp.float32) for _ in range(2)]
    for z in range(levels):
        values = moved(lambda j: full_ref[j], lambda j, field: around_between(field, 0.0, 0.0), levels, z)
        for f, value in enumerate(values):
            j = f * levels + z
            begun_ref[j] = value[:, :cols]
            packs[0] = packed(packs[0], value[:, cols:], LANES - EDGE, EDGE * j)
            packs[1] = packed(packs[1], value[:, cols:], 0, EDGE * j)
    packs_ref[0], packs_ref[1] = packs
    token_ref[...] = jnp.zeros_like(token_ref)


def widened(plane, west, east, at):
    return jnp.concatenate([plane, side_tile(west, at, east, at)], axis=1)


def outer_body(force_ref, edge_ref, tips_ref, mask_ref, west_ref, east_ref, *refs):
    sides, (up_ref, down_ref) = refs[:-2], refs[-2:]
    planes, rows, cols = force_ref.shape
    moving = 2 * planes // 3
    ends = ((up_ref, slice(rows - RIM, rows), slice(3 * RIM, 4 * RIM)), (down_ref, slice(0, RIM), slice(0, RIM)))
    for out_ref, at, tip in ends:
        out_ref[:moving] = force_ref[:moving, at] * FORCE_SCALE
        out_ref[moving : moving + planes] = tips_ref[:, tip] * STATE_SCALE
        out_ref[moving + planes] = mask_ref[at, :cols] * STATE_SCALE
        parts = [west_ref[at], east_ref[at], edge_ref[at]] + [side[at] for side in sides]
        for k, part in enumerate(parts):
            lane = (k % 2) * LANES
            out_ref[moving + planes + 1 + k // 2, :, lane : lane + LANES] = part * (STATE_SCALE if k < 2 else FORCE_SCALE)


def factors(mask, own, west, east, force_rows, push_ref):
    moving, total, wide = push_ref.shape
    cols = wide - LANES

    def counts(edge):
        return jnp.broadcast_to(edge[:, LANES - 1 :], (total, LANES))

    lane = iota((total, LANES), 1)
    count_side = jnp.where(lane < LANES // 2, counts(east), counts(west))
    relax = mask / (1.0 + GAMMA * jnp.concatenate([counts(own)] * (cols // LANES) + [count_side], axis=1))
    half = GAMMA * relax
    for j in range(moving):
        push_ref[j, :, :cols] = force_rows(j) * half[:, :cols]
        push_ref[j, :, cols:] = side_tile(west, EDGE * (moving + j), east, EDGE * j) * half[:, cols:]
    return relax


def finish(relax, push_ref, levels, values, z, at=(slice(None),)):
    tracer, across, along = values
    rated = relax[at]
    return (tracer * rated + push_ref[(z, *at)], across * rated, along * rated + push_ref[(levels + z, *at)])


def two_more(relax, push_ref, one_ref, two_ref, last):
    levels = one_ref.shape[0] // 3
    cols = one_ref.shape[2] - LANES
    for z in range(levels):
        values = moved(lambda j: one_ref[j], lambda j, field: around(field), levels, z)
        for f, value in enumerate(finish(relax, push_ref, levels, values, z)):
            two_ref[f * levels + z] = value
    for z in range(levels):
        values = moved(
            lambda j: two_ref[j, :, :cols],
            lambda j, field: tuple(side[:, :cols] for side in around(two_ref[j])),
            levels,
            z,
        )
        last(z, finish(relax, push_ref, levels, values, z, (slice(None), slice(0, cols))))


def terms(values, stokes):
    rows, total = stokes.shape[0], values[0].shape[0]
    tracer = values[0]
    ddy = pltpu.roll(tracer, total - 1, 0)[:rows] - pltpu.roll(tracer, 1, 0)[:rows]
    return [values[2][:rows] * tracer[:rows], stokes * tracer[:rows], ddy]


def transports(sums, count, child, all_rows):
    raw = [jnp.sum(value, axis=1, keepdims=True) for value in sums]
    raw = [raw[0], raw[1] / (1.0 + count), raw[2] * (-0.5 * DISPERSE)]
    lane = iota(child.shape, 1)
    part = jnp.zeros(child.shape, jnp.float32)
    for q in range(3):
        part = part + jnp.where((child >= 0) & (lane == q * all_rows + child), raw[q], 0.0)
    return jnp.sum(part, axis=0, keepdims=True)


def inner_body(mask_ref, begun_ref, packs_ref, force_ref, edge_ref, *refs):
    side_refs, (middle_ref, ends_ref, part_ref, push_ref, one_ref, two_ref) = refs[:-6], refs[-6:]
    planes, rows, cols = begun_ref.shape
    levels = planes // 3
    moving = 2 * levels
    tile = 2 * RIM
    west, east = packs_ref[0], packs_ref[1]
    relax = factors(
        mask_ref[...], edge_ref[...], side_refs[0][...], side_refs[-1][...], lambda j: force_ref[j], push_ref
    )
    for z in range(levels):
        index = [f * levels + z for f in range(3)]
        values = [widened(begun_ref[j], west, east, EDGE * j) for j in index]
        for j, value in zip(index, finish(relax, push_ref, levels, values, z)):
            one_ref[j] = value
    sums = [jnp.zeros((rows, cols), jnp.float32) for _ in range(3)]

    def last(z, values):
        for f, value in enumerate(values):
            middle_ref[f, z] = value[tile : rows - tile]
            ends_ref[f, z, :tile] = value[:tile]
            ends_ref[f, z, tile:] = value[rows - tile :]
        for q, term in enumerate(terms(values, force_ref[moving + z])):
            sums[q] = sums[q] + term

    two_more(relax, push_ref, one_ref, two_ref, last)
    row = iota((rows, LANES), 0)
    child = jnp.where((row >= RIM) & (row < rows - RIM), row, -1)
    part_ref[...] = transports(sums, edge_ref[:, LANES - 1 :], child, rows)


def steps_body(
    sides, tips_ref, west_ref, east_ref, mask_ref, begun_ref, packs_ref, force_ref, edge_ref, north_ref, south_ref, *refs
):
    ends_ref, part_ref = refs[:2]
    refs = refs[2:]
    side_refs = refs[:sides]
    held_ref, parts_ref, push_ref, halo_ref, one_ref, two_ref = refs[sides:]
    planes, rows, cols = begun_ref.shape
    wide = cols + LANES
    levels = planes // 3
    moving = 2 * levels
    tile = 2 * RIM
    own_rows, total = 2 * tile, 3 * tile
    tail = slice(rows - tile, rows)

    def slab(ref, *index):
        return [ref[(*index, slice(0, tile))], ref[(*index, tail)]]

    def joined(index, scale):
        return jnp.concatenate([north_ref[index], south_ref[index]], axis=0) * (1.0 / scale)

    def half_of(k, scale):
        lane = (k % 2) * LANES
        return joined(moving + planes + 1 + k // 2, scale)[:, lane : lane + LANES]

    beside = [half_of(k, STATE_SCALE) for k in range(2)]
    outer = [half_of(2 + k, FORCE_SCALE) for k in range(1 + sides)]
    edges = [jnp.concatenate([*slab(side), outer[1 + k]], axis=0) for k, side in enumerate(side_refs)]
    own = jnp.concatenate([*slab(edge_ref), outer[0]], axis=0)

    def halo(index, at):
        return widened(joined(moving + index, STATE_SCALE), *beside, at)

    mask = jnp.concatenate([*slab(mask_ref), halo(planes, EDGE * planes)], axis=0)
    relax = factors(
        mask,
        own,
        edges[0],
        edges[-1],
        lambda j: jnp.concatenate([*slab(force_ref, j), joined(j, FORCE_SCALE)], axis=0),
        push_ref,
    )
    for j in range(planes):
        halo_ref[j] = halo(j, EDGE * j)
    row = iota((tile, wide), 0)
    packs = [slab(packs_ref, k) for k in range(2)]
    wests, easts = slab(west_ref), slab(east_ref)

    def tip(j, k):
        return widened(tips_ref[j, k * tile : (k + 1) * tile], wests[k], easts[k], EDGE * j)

    def begun(j, k):
        return widened(slab(begun_ref, j)[k], packs[0][k], packs[1][k], EDGE * j)

    def near(j, field):
        return around_between(field, tip(j, 0)[:1], tip(j, 1)[tile - 1 :])

    for z in range(levels):
        index = [f * levels + z for f in range(3)]
        beyond = [halo_ref[j] for j in index]
        north = [jnp.where(row == tile - 1, value[:1], 0.0) for value in beyond]
        south = [jnp.where(row == 0, value[tile - 1 :], 0.0) for value in beyond]
        first = added(-1.0, tip(index[2], 0), *south)
        final = added(1.0, tip(index[2], 1), *north)
        blocks = (
            [begun(j, 0) + extra for j, extra in zip(index, first)],
            [begun(j, 1) + extra for j, extra in zip(index, final)],
            moved(lambda j: halo_ref[j], near, levels, z),
        )
        for k, values in enumerate(blocks):
            at = slice(k * tile, (k + 1) * tile)
            for j, value in zip(index, finish(relax, push_ref, levels, values, z, (at,))):
                one_ref[j, at] = value

    sums = [jnp.zeros((own_rows, cols), jnp.float32) for _ in range(3)]
    row = iota((tile, cols), 0)

    def last(z, values):
        for f, value in enumerate(values):
            held_ref[f, z, :tile] = jnp.where(row < RIM, value[:tile], ends_ref[f, z, :tile])
            held_ref[f, z, tile:] = jnp.where(row < RIM, ends_ref[f, z, tile:], value[tile:own_rows])
        stokes = jnp.concatenate(slab(force_ref, moving + z), axis=0)
        for q, term in enumerate(terms(values, stokes)):
            sums[q] = sums[q] + term

    two_more(relax, push_ref, one_ref, two_ref, last)
    row = iota((own_rows, LANES), 0)
    child = jnp.where(row < RIM, row, jnp.where(row >= own_rows - RIM, row + rows - own_rows, -1))
    part = transports(sums, own[:own_rows, LANES - 1 :], child, rows) + part_ref[...]
    parts_ref[...] = jnp.broadcast_to(part, parts_ref.shape)


def whole_body(middle_ref, ends_ref, state_ref, sent):
    rows = state_ref.shape[2]
    tile = ends_ref.shape[2] // 2
    copies = [
        pltpu.make_async_copy(source, state_ref.at[:, :, pl.ds(start, size)], sent.at[k])
        for k, (source, start, size) in enumerate(
            (
                (middle_ref, tile, rows - 2 * tile),
                (ends_ref.at[:, :, pl.ds(0, tile)], 0, tile),
                (ends_ref.at[:, :, pl.ds(tile, tile)], rows - tile, tile),
            )
        )
    ]
    for copy in copies:
        copy.start()
    for copy in copies:
        copy.wait()


def profile_body(across, along, parts_ref, out_ref):
    rows = out_ref.shape[1]
    parts = parts_ref[...]
    devices = parts.shape[0]
    total = parts
    for k in range(1, across):
        total = total + pltpu.roll(parts, devices - k, 0)
    row = iota(parts.shape, 0)
    squares = jnp.sum(jnp.where(row % across == 0, total * total, 0.0), keepdims=True)
    scale = jnp.sqrt(squares / (3 * rows * along) + 1e-06)
    mine = jnp.sum(jnp.where(row == lax.axis_index("gy") * across, total, 0.0), axis=0, keepdims=True) / scale
    for q in range(3):
        out_ref[q : q + 1, :] = mine[:, q * rows : (q + 1) * rows]


def per_device(state, parent_rows, dest, pick, offset, wet):
    fields, levels, rows, cols = state.shape
    planes = fields * levels
    moving = 2 * levels
    along, across = lax.axis_size("gy"), lax.axis_size("gx")
    capacity = 2 * SEND // along
    wide = cols + LANES
    f32 = jnp.float32
    even_pairs = [(i, i ^ 1) for i in range(along)]
    odd_pairs = [(i, ((i + 1) ^ 1) - 1) for i in range(1, along - 1)]
    swapped = [(0, 1), (1, 0)]
    eastward = [(i, i + 1) for i in range(across - 1)]
    westward = [(i + 1, i) for i in range(across - 1)]

    half = along // 2
    slots = half * capacity
    width = planes * cols + LANES
    halves = [list(range(half)), list(range(half, along))]

    def gathered(far):
        fetched = [pltpu.VMEM((1, SEND), jnp.int32)] * 3 + [pltpu.VMEM(parent_rows.shape, jnp.bfloat16)] if far else []
        return call(
            functools.partial(gather_body, capacity, slots, far),
            jax.ShapeDtypeStruct((slots, width), jnp.bfloat16),
            flops=2 * 8 * slots * SEND * planes * cols,
            moved=2 * (SEND + slots) * planes * cols,
            limit=VMEM_MOST,
            in_specs=[pl.BlockSpec(memory_space=pl.ANY if far else pltpu.VMEM)] * 4,
            out_specs=pl.BlockSpec(memory_space=pl.ANY),
            scratch_shapes=fetched
            + [
                pltpu.VMEM((slots, width), jnp.bfloat16),
                pltpu.SemaphoreType.DMA((4,)),
            ]
            + ([pltpu.SemaphoreType.DMA((4,))] if far else []),
        )(dest.reshape(1, SEND), pick.reshape(1, SEND), offset.reshape(1, SEND), parent_rows)

    def exchanged(payload):
        return lax.all_to_all(payload, "gy", split_axis=0, concat_axis=0, tiled=True, axis_index_groups=halves)

    far_rows = exchanged(gathered(True))

    cells = state.reshape(planes, rows, cols)
    packed_side = jax.ShapeDtypeStruct((rows, LANES), f32)
    first, last = call(sides_body, (packed_side, packed_side), moved=4 * planes * rows * cols)(cells, wet)
    if across == 2:
        west_one = lax.axis_index("gx") == 0
        other = lax.ppermute(jnp.where(west_one, last, first), "gx", swapped)
        from_west, from_east = jnp.where(west_one, 0.0, other), jnp.where(west_one, other, 0.0)
    else:
        from_west = lax.ppermute(last, "gx", eastward)
        from_east = lax.ppermute(first, "gx", westward)
    tips, mask, begun, packs, token = call(
        begin_body,
        (
            jax.ShapeDtypeStruct((planes, 4 * RIM, cols), f32),
            jax.ShapeDtypeStruct((rows, wide), f32),
            jax.ShapeDtypeStruct((planes, rows, cols), f32),
            jax.ShapeDtypeStruct((2, rows, LANES), f32),
            jax.ShapeDtypeStruct((8, LANES), f32),
        ),
        flops=20 * planes * rows * wide,
        moved=12 * planes * rows * wide,
        scratch_shapes=[pltpu.VMEM((planes, rows, wide), f32)],
    )(cells, wet, from_west, from_east)

    sums = call(
        far_body,
        jax.ShapeDtypeStruct((rows, width), f32),
        flops=2 * rows * slots * width,
        moved=2 * slots * width + 4 * rows * width,
    )(token, far_rows)
    mirrored = [(i, (i + half) % along) for i in range(along)]
    sums, near_rows = lax.optimization_barrier((sums.astype(jnp.float16), gathered(False)))
    sums = lax.ppermute(sums, "gy", mirrored)
    arrived = exchanged(near_rows)
    come = call(
        come_body,
        jax.ShapeDtypeStruct((8, LANES), f32),
        flops=10**11,
    )(sums[:8, :LANES].astype(f32))
    sums, arrived = lax.optimization_barrier((sums, arrived))
    sums = sums.astype(f32)

    force, edge = call(
        functools.partial(landing_body, planes, cols),
        (jax.ShapeDtypeStruct((planes, rows, cols), f32), packed_side),
        flops=2 * rows * slots * planes * cols,
        moved=2 * slots * planes * cols + 4 * rows * planes * cols,
    )(come, arrived, sums)
    if across == 2:
        sides = [lax.ppermute(edge, "gx", swapped)]
    else:
        sides = [lax.ppermute(edge, "gx", eastward), lax.ppermute(edge, "gx", westward)]
    outer = jax.ShapeDtypeStruct((moving + planes + 1 + (len(sides) + 4) // 2, RIM, cols), f32)
    up, down = call(outer_body, (outer, outer), moved=16 * (moving + planes) * RIM * cols)(
        force, edge, tips, mask, from_west, from_east, *sides
    )
    even = lax.axis_index("gy") % 2 == 0
    far = lax.ppermute(jnp.where(even, down, up).astype(jnp.float16), "gy", odd_pairs).astype(f32)
    near = lax.ppermute(jnp.where(even, up, down).astype(jnp.float16), "gy", even_pairs).astype(f32)
    above, below = jnp.where(even, near, far), jnp.where(even, far, near)
    tile = 2 * RIM
    middle, ends, part = call(
        inner_body,
        (
            jax.ShapeDtypeStruct((fields, levels, rows - 2 * tile, cols), f32),
            jax.ShapeDtypeStruct((fields, levels, 2 * tile, cols), f32),
            jax.ShapeDtypeStruct((1, LANES), f32),
        ),
        flops=60 * planes * rows * wide,
        moved=8 * planes * rows * wide,
        scratch_shapes=[
            pltpu.VMEM((moving, rows, wide), f32),
            pltpu.VMEM((planes, rows, wide), f32),
            pltpu.VMEM((planes, rows, wide), f32),
        ],
    )(mask, begun, packs, force, edge, *sides)
    ends, parts = call(
        functools.partial(steps_body, len(sides)),
        (
            jax.ShapeDtypeStruct((fields, levels, 2 * tile, cols), f32),
            jax.ShapeDtypeStruct((along * across, LANES), f32),
        ),
        flops=60 * planes * 3 * tile * wide,
        moved=8 * planes * 3 * tile * wide,
        scratch_shapes=[
            pltpu.VMEM((moving, 3 * tile, wide), f32),
            pltpu.VMEM((planes, tile, wide), f32),
            pltpu.VMEM((planes, 3 * tile, wide), f32),
            pltpu.VMEM((planes, 3 * tile, wide), f32),
        ],
    )(tips, from_west, from_east, mask, begun, packs, force, edge, above, below, ends, part, *sides)
    new_state = call(
        whole_body,
        jax.ShapeDtypeStruct(state.shape, f32),
        moved=8 * planes * rows * cols,
        out_specs=pl.BlockSpec(memory_space=pl.ANY),
        scratch_shapes=[pltpu.SemaphoreType.DMA((3,))],
    )(middle, ends)
    every = lax.all_to_all(parts, ("gy", "gx"), split_axis=0, concat_axis=0, tiled=True)
    profile = call(functools.partial(profile_body, across, along), jax.ShapeDtypeStruct((3, rows), f32))(every)
    return new_state, profile


def solution(mesh):
    in_specs = (
        P(None, None, "gy", "gx"),
        P(("gy", "gx"), None, None),
        P(("gy", "gx"), None),
        P(("gy", "gx")),
        P(("gy", "gx")),
        P("gy", "gx"),
    )
    out_specs = (P(None, None, "gy", "gx"), P(None, "gy"))
    return jax.shard_map(
        per_device, mesh=mesh, in_specs=in_specs, out_specs=out_specs, check_vma=False
    )
```

```python
import functools

import jax
import jax.numpy as jnp
from jax import lax
from jax.experimental import pallas as pl
from jax.experimental.pallas import tpu as pltpu
from jax.sharding import PartitionSpec as P

SEND = 64
STEPS = 3

KH = 0.2
KZ = 0.05
ADV = 0.25
PG = 0.5
GAMMA = 0.5
DISPERSE = 2.0

EDGE = 3
RIM = 4
LANES = 128
STATE_SCALE = 8192.0
FORCE_SCALE = 64.0
SUM_SCALE = 128.0
VMEM_LIMIT = 16 * 1024 * 1024
VMEM_MOST = 60 * 1024 * 1024


def call(body, out_shape, flops=0, moved=0, limit=VMEM_LIMIT, **more):
    return pl.pallas_call(
        body,
        out_shape=out_shape,
        compiler_params=pltpu.CompilerParams(vmem_limit_bytes=limit),
        cost_estimate=pl.CostEstimate(flops=flops, bytes_accessed=moved, transcendentals=0),
        **more,
    )


def iota(shape, dim):
    return lax.broadcasted_iota(jnp.int32, shape, dim)


def gather_body(capacity, slots, far, *refs):
    if far:
        sources, out_ref, targets, held_ref, sent, copied = refs[:4], refs[4], refs[5:9], *refs[9:]
        copies = [
            pltpu.make_async_copy(source, target, copied.at[k])
            for k, (source, target) in enumerate(zip(sources, targets))
        ]
    else:
        targets, (out_ref, held_ref, sent), copies = refs[:4], refs[4:], []
    for copy in copies:
        copy.start()
    dest_ref, pick_ref, offset_ref, rows_ref = targets
    send, planes, cols = rows_ref.shape
    for copy in copies[:3]:
        copy.wait()
    dest = dest_ref[...]
    eye = iota((send, send), 0) == iota((send, send), 1)
    dest_column = jnp.sum(jnp.where(eye, dest, 0), axis=1, keepdims=True)
    earlier = (dest_column == dest) & (iota((send, send), 0) < iota((send, send), 1))
    rank = jnp.sum(earlier.astype(jnp.int32), axis=0, keepdims=True)
    half = slots // capacity
    mine = lax.axis_index("gy") >= half
    there = (dest >= half) != mine if far else (dest >= half) == mine
    slot_of = jnp.where(there, jnp.where(dest >= half, dest - half, dest) * capacity + rank, -1)
    taken = iota((slots, send), 0) == slot_of
    source = jnp.sum(jnp.where(taken, pick_ref[...] + 1, 0), axis=1, keepdims=True) - 1
    label = jnp.sum(jnp.where(taken, offset_ref[...] + 1, 0), axis=1, keepdims=True)
    group = 8
    lane = iota((slots, send * group), 1)
    select = jnp.concatenate(
        [(lane == source * group + j).astype(jnp.float32).astype(jnp.bfloat16) for j in range(group)], axis=0
    )
    width = planes * cols
    held_ref[:, width:] = jnp.broadcast_to(label, (slots, LANES)).astype(jnp.float32).astype(jnp.bfloat16)
    for copy in copies[3:]:
        copy.wait()
    parts = []

    def send_columns(start, size):
        part = pltpu.make_async_copy(
            held_ref.at[:, pl.ds(start, size)], out_ref.at[:, pl.ds(start, size)], sent.at[len(parts)]
        )
        part.start()
        parts.append(part)

    send_columns(width, LANES)
    for g in range(planes // group):
        block = rows_ref[:, g * group : (g + 1) * group, :].reshape(send * group, cols)
        got = jnp.dot(select, block, preferred_element_type=jnp.float32).astype(jnp.bfloat16)
        for j in range(group):
            at = (g * group + j) * cols
            held_ref[:, at : at + cols] = got[j * slots : (j + 1) * slots]
        send_columns(g * group * cols, group * cols)
    for part in parts:
        part.wait()


def landing_of(arrived_ref, rows):
    slots, width = arrived_ref.shape
    label = arrived_ref[:, width - LANES :].astype(jnp.float32)
    landing = (label == (iota((slots, LANES), 1) + 1).astype(jnp.float32)).astype(jnp.float32)
    return landing.T[:rows].astype(jnp.bfloat16)


def landed(landing, values):
    return jnp.dot(landing, values, preferred_element_type=jnp.float32)


def far_body(token_ref, arrived_ref, sums_ref, stokes_ref):
    rows, width = sums_ref.shape
    slots = arrived_ref.shape[0]
    landing = landing_of(arrived_ref, rows)
    moving, step = width - LANES, 2 * LANES
    for at in range(0, moving, step):
        sums_ref[:, at : at + step] = landed(landing, arrived_ref[:, at : at + step]) * SUM_SCALE
    sums_ref[:, moving:] = landed(landing, jnp.full((slots, LANES), SUM_SCALE, jnp.bfloat16))
    for at in range(0, stokes_ref.shape[1], step):
        there = slice(moving + at, moving + at + step)
        stokes_ref[:, at : at + step] = landed(landing, arrived_ref[:, there]) * SUM_SCALE


def come_body(sums_ref, token_ref):
    token_ref[...] = jnp.zeros_like(token_ref)


def landing_body(planes, cols, token_ref, arrived_ref, sums_ref, force_ref, edge_ref):
    slots = arrived_ref.shape[0]
    rows = force_ref.shape[1]
    landing = landing_of(arrived_ref, rows)
    far = 1.0 / SUM_SCALE
    moving = 2 * planes // 3
    count = landed(landing, jnp.ones((slots, LANES), jnp.bfloat16)) + sums_ref[:, moving * cols :] * far
    edge = count
    for j in range(planes):
        at = slice(j * cols, (j + 1) * cols)
        force = landed(landing, arrived_ref[:, at])
        if j < moving:
            force = force + sums_ref[:, at] * far
        force_ref[j] = force
        if j < moving:
            edge = packed(edge, force[:, :LANES], 0, EDGE * j)
            edge = packed(edge, force[:, cols - LANES :], LANES - EDGE, EDGE * (moving + j))
    edge_ref[...] = edge


def packed(into, tile, start, at):
    lane = iota(tile.shape, 1)
    shifted = pltpu.roll(tile, (at - start) % LANES, 1)
    return jnp.where((lane >= at) & (lane < at + EDGE), shifted, into)


def sides_body(state_ref, wet_ref, first_ref, last_ref):
    planes, rows, cols = state_ref.shape
    first = jnp.zeros((rows, LANES), jnp.float32)
    last = jnp.zeros((rows, LANES), jnp.float32)
    for j in range(planes + 1):
        own = state_ref[j] if j < planes else wet_ref[...].astype(jnp.float32)
        first = packed(first, own[:, :LANES], 0, EDGE * j)
        last = packed(last, own[:, cols - LANES :], LANES - EDGE, EDGE * j)
    first_ref[...] = first
    last_ref[...] = last


def side_tile(west, west_at, east, east_at):
    lane = iota(west.shape, 1)
    right = pltpu.roll(east, (LANES - east_at) % LANES, 1)
    left = pltpu.roll(west, (2 * LANES - EDGE - west_at) % LANES, 1)
    return jnp.where(lane < EDGE, right, jnp.where(lane >= LANES - EDGE, left, 0.0))


def around(field):
    rows, cols = field.shape
    return (
        pltpu.roll(field, cols - 1, 1),
        pltpu.roll(field, 1, 1),
        pltpu.roll(field, rows - 1, 0),
        pltpu.roll(field, 1, 0),
    )


def around_between(field, north_row, south_row):
    east, west, north, south = around(field)
    row = iota(field.shape, 0)
    return east, west, jnp.where(row == field.shape[0] - 1, north_row, north), jnp.where(row == 0, south_row, south)


def moved(load, near, levels, z):
    upper, lower = min(z + 1, levels - 1), max(z - 1, 0)
    results = []
    fields = [load(f * levels + z) for f in range(3)]
    tracer, across, along = fields
    around_tracer = near(z, tracer)
    east, west, north, south = around_tracer
    ddx, ddy = east - west, north - south
    extra = (0.5 * ADV * (across * ddx + along * ddy), 0.5 * PG * ddx, 0.5 * PG * ddy)
    for f, centre in enumerate(fields):
        sides = around_tracer if f == 0 else near(f * levels + z, centre)
        beside = KH * ((sides[0] + sides[1]) + (sides[2] + sides[3]))
        beyond = KZ * (load(f * levels + upper) + load(f * levels + lower))
        results.append((1.0 - 4.0 * KH - 2.0 * KZ) * centre + beside + (beyond - extra[f]))
    return results


def added(sign, along, tracer, across_near, along_near):
    return [
        (KH - sign * 0.5 * ADV * along) * tracer,
        KH * across_near,
        KH * along_near - sign * 0.5 * PG * tracer,
    ]


def begin_body(state_ref, wet_ref, west_ref, east_ref, tips_ref, mask_ref, begun_ref, packs_ref, token_ref, full_ref):
    planes, rows, cols = state_ref.shape
    levels = planes // 3
    tile = 2 * RIM
    west, east = west_ref[...], east_ref[...]
    tips_ref[:, :tile] = state_ref[:, :tile]
    tips_ref[:, tile:] = state_ref[:, rows - tile :]
    for j in range(planes):
        full_ref[j, :, :cols] = state_ref[j]
        full_ref[j, :, cols:] = side_tile(west, EDGE * j, east, EDGE * j)
    mask_ref[:, :cols] = wet_ref[...].astype(jnp.float32)
    mask_ref[:, cols:] = side_tile(west, EDGE * planes, east, EDGE * planes)
    packs = [jnp.zeros((rows, LANES), jnp.float32) for _ in range(2)]
    for z in range(levels):
        values = moved(lambda j: full_ref[j], lambda j, field: around_between(field, 0.0, 0.0), levels, z)
        for f, value in enumerate(values):
            j = f * levels + z
            begun_ref[j] = value[:, :cols]
            packs[0] = packed(packs[0], value[:, cols:], LANES - EDGE, EDGE * j)
            packs[1] = packed(packs[1], value[:, cols:], 0, EDGE * j)
    packs_ref[0], packs_ref[1] = packs
    token_ref[...] = jnp.zeros_like(token_ref)


def widened(plane, west, east, at):
    return jnp.concatenate([plane, side_tile(west, at, east, at)], axis=1)


def outer_body(force_ref, edge_ref, tips_ref, mask_ref, west_ref, east_ref, *refs):
    sides, (up_ref, down_ref) = refs[:-2], refs[-2:]
    planes, rows, cols = force_ref.shape
    moving = 2 * planes // 3
    ends = ((up_ref, slice(rows - RIM, rows), slice(3 * RIM, 4 * RIM)), (down_ref, slice(0, RIM), slice(0, RIM)))
    for out_ref, at, tip in ends:
        out_ref[:moving] = force_ref[:moving, at] * FORCE_SCALE
        out_ref[moving : moving + planes] = tips_ref[:, tip] * STATE_SCALE
        out_ref[moving + planes] = mask_ref[at, :cols] * STATE_SCALE
        parts = [west_ref[at], east_ref[at], edge_ref[at]] + [side[at] for side in sides]
        for k, part in enumerate(parts):
            lane = (k % 2) * LANES
            out_ref[moving + planes + 1 + k // 2, :, lane : lane + LANES] = part * (STATE_SCALE if k < 2 else FORCE_SCALE)


def factors(mask, own, west, east, force_rows, push_ref):
    moving, total, wide = push_ref.shape
    cols = wide - LANES

    def counts(edge):
        return jnp.broadcast_to(edge[:, LANES - 1 :], (total, LANES))

    lane = iota((total, LANES), 1)
    count_side = jnp.where(lane < LANES // 2, counts(east), counts(west))
    relax = mask / (1.0 + GAMMA * jnp.concatenate([counts(own)] * (cols // LANES) + [count_side], axis=1))
    half = GAMMA * relax
    for j in range(moving):
        push_ref[j, :, :cols] = force_rows(j) * half[:, :cols]
        push_ref[j, :, cols:] = side_tile(west, EDGE * (moving + j), east, EDGE * j) * half[:, cols:]
    return relax


def finish(relax, push_ref, levels, values, z, at=(slice(None),)):
    tracer, across, along = values
    rated = relax[at]
    return (tracer * rated + push_ref[(z, *at)], across * rated, along * rated + push_ref[(levels + z, *at)])


def two_more(relax, push_ref, one_ref, two_ref, last):
    levels = one_ref.shape[0] // 3
    cols = one_ref.shape[2] - LANES
    for z in range(levels):
        values = moved(lambda j: one_ref[j], lambda j, field: around(field), levels, z)
        for f, value in enumerate(finish(relax, push_ref, levels, values, z)):
            two_ref[f * levels + z] = value
    for z in range(levels):
        values = moved(
            lambda j: two_ref[j, :, :cols],
            lambda j, field: tuple(side[:, :cols] for side in around(two_ref[j])),
            levels,
            z,
        )
        last(z, finish(relax, push_ref, levels, values, z, (slice(None), slice(0, cols))))


def terms(values, stokes):
    rows, total = stokes.shape[0], values[0].shape[0]
    tracer = values[0]
    ddy = pltpu.roll(tracer, total - 1, 0)[:rows] - pltpu.roll(tracer, 1, 0)[:rows]
    return [values[2][:rows] * tracer[:rows], stokes * tracer[:rows], ddy]


def transports(sums, count, child, all_rows):
    raw = [jnp.sum(value, axis=1, keepdims=True) for value in sums]
    raw = [raw[0], raw[1] / (1.0 + count), raw[2] * (-0.5 * DISPERSE)]
    lane = iota(child.shape, 1)
    part = jnp.zeros(child.shape, jnp.float32)
    for q in range(3):
        part = part + jnp.where((child >= 0) & (lane == q * all_rows + child), raw[q], 0.0)
    return jnp.sum(part, axis=0, keepdims=True)


def inner_body(mask_ref, begun_ref, packs_ref, force_ref, edge_ref, *refs):
    side_refs, (middle_ref, ends_ref, part_ref, push_ref, one_ref, two_ref) = refs[:-6], refs[-6:]
    planes, rows, cols = begun_ref.shape
    levels = planes // 3
    moving = 2 * levels
    tile = 2 * RIM
    west, east = packs_ref[0], packs_ref[1]
    relax = factors(
        mask_ref[...], edge_ref[...], side_refs[0][...], side_refs[-1][...], lambda j: force_ref[j], push_ref
    )
    for z in range(levels):
        index = [f * levels + z for f in range(3)]
        values = [widened(begun_ref[j], west, east, EDGE * j) for j in index]
        for j, value in zip(index, finish(relax, push_ref, levels, values, z)):
            one_ref[j] = value
    sums = [jnp.zeros((rows, cols), jnp.float32) for _ in range(3)]

    def last(z, values):
        for f, value in enumerate(values):
            middle_ref[f, z] = value[tile : rows - tile]
            ends_ref[f, z, :tile] = value[:tile]
            ends_ref[f, z, tile:] = value[rows - tile :]
        for q, term in enumerate(terms(values, force_ref[moving + z])):
            sums[q] = sums[q] + term

    two_more(relax, push_ref, one_ref, two_ref, last)
    row = iota((rows, LANES), 0)
    child = jnp.where((row >= RIM) & (row < rows - RIM), row, -1)
    part_ref[...] = transports(sums, edge_ref[:, LANES - 1 :], child, rows)


def steps_body(
    sides, stokes_ref, tips_ref, west_ref, east_ref, mask_ref, begun_ref, packs_ref, force_ref, edge_ref, north_ref, south_ref, *refs
):
    middle_ref, ends_ref, part_ref = refs[:3]
    refs = refs[3:]
    side_refs = refs[:sides]
    held_ref, parts_ref, push_ref, halo_ref, one_ref, two_ref = refs[sides:]
    planes, rows, cols = begun_ref.shape
    wide = cols + LANES
    levels = planes // 3
    moving = 2 * levels
    tile = 2 * RIM
    own_rows, total = 2 * tile, 3 * tile
    tail = slice(rows - tile, rows)

    def slab(ref, *index):
        return [ref[(*index, slice(0, tile))], ref[(*index, tail)]]

    def joined(index, scale):
        return jnp.concatenate([north_ref[index], south_ref[index]], axis=0) * (1.0 / scale)

    def half_of(k, scale):
        lane = (k % 2) * LANES
        return joined(moving + planes + 1 + k // 2, scale)[:, lane : lane + LANES]

    beside = [half_of(k, STATE_SCALE) for k in range(2)]
    outer = [half_of(2 + k, FORCE_SCALE) for k in range(1 + sides)]
    edges = [jnp.concatenate([*slab(side), outer[1 + k]], axis=0) for k, side in enumerate(side_refs)]
    own = jnp.concatenate([*slab(edge_ref), outer[0]], axis=0)

    def halo(index, at):
        return widened(joined(moving + index, STATE_SCALE), *beside, at)

    mask = jnp.concatenate([*slab(mask_ref), halo(planes, EDGE * planes)], axis=0)
    relax = factors(
        mask,
        own,
        edges[0],
        edges[-1],
        lambda j: jnp.concatenate([*slab(force_ref, j), joined(j, FORCE_SCALE)], axis=0),
        push_ref,
    )
    for j in range(planes):
        halo_ref[j] = halo(j, EDGE * j)
    row = iota((tile, wide), 0)
    packs = [slab(packs_ref, k) for k in range(2)]
    wests, easts = slab(west_ref), slab(east_ref)

    def tip(j, k):
        return widened(tips_ref[j, k * tile : (k + 1) * tile], wests[k], easts[k], EDGE * j)

    def begun(j, k):
        return widened(slab(begun_ref, j)[k], packs[0][k], packs[1][k], EDGE * j)

    def near(j, field):
        return around_between(field, tip(j, 0)[:1], tip(j, 1)[tile - 1 :])

    for z in range(levels):
        index = [f * levels + z for f in range(3)]
        beyond = [halo_ref[j] for j in index]
        north = [jnp.where(row == tile - 1, value[:1], 0.0) for value in beyond]
        south = [jnp.where(row == 0, value[tile - 1 :], 0.0) for value in beyond]
        first = added(-1.0, tip(index[2], 0), *south)
        final = added(1.0, tip(index[2], 1), *north)
        blocks = (
            [begun(j, 0) + extra for j, extra in zip(index, first)],
            [begun(j, 1) + extra for j, extra in zip(index, final)],
            moved(lambda j: halo_ref[j], near, levels, z),
        )
        for k, values in enumerate(blocks):
            at = slice(k * tile, (k + 1) * tile)
            for j, value in zip(index, finish(relax, push_ref, levels, values, z, (at,))):
                one_ref[j, at] = value

    sums = [jnp.zeros((own_rows, cols), jnp.float32) for _ in range(3)]
    row = iota((tile, cols), 0)

    def last(z, values):
        for f, value in enumerate(values):
            held_ref[f, z, :tile] = jnp.where(row < RIM, value[:tile], ends_ref[f, z, :tile])
            held_ref[f, z, tile:] = jnp.where(row < RIM, ends_ref[f, z, tile:], value[tile:own_rows])
        stokes = jnp.concatenate(slab(force_ref, moving + z), axis=0)
        for q, term in enumerate(terms(values, stokes)):
            sums[q] = sums[q] + term

    two_more(relax, push_ref, one_ref, two_ref, last)
    beyond = jnp.zeros((rows, cols), jnp.float32)
    for z in range(levels):
        tracer = [held_ref[0, z, :tile], middle_ref[0, z], held_ref[0, z, tile:]]
        beyond = beyond + stokes_ref[:, z * cols : (z + 1) * cols] * jnp.concatenate(tracer, axis=0)
    beyond = jnp.sum(beyond, axis=1, keepdims=True) / (SUM_SCALE * (1.0 + edge_ref[:, LANES - 1 :]))
    row, lane = iota((rows, LANES), 0), iota((rows, LANES), 1)
    beyond = jnp.sum(jnp.where(lane == rows + row, beyond, 0.0), axis=0, keepdims=True)
    row = iota((own_rows, LANES), 0)
    child = jnp.where(row < RIM, row, jnp.where(row >= own_rows - RIM, row + rows - own_rows, -1))
    part = transports(sums, own[:own_rows, LANES - 1 :], child, rows) + (part_ref[...] + beyond)
    parts_ref[...] = jnp.broadcast_to(part, parts_ref.shape)


def whole_body(middle_ref, ends_ref, state_ref, sent):
    rows = state_ref.shape[2]
    tile = ends_ref.shape[2] // 2
    copies = [
        pltpu.make_async_copy(source, state_ref.at[:, :, pl.ds(start, size)], sent.at[k])
        for k, (source, start, size) in enumerate(
            (
                (middle_ref, tile, rows - 2 * tile),
                (ends_ref.at[:, :, pl.ds(0, tile)], 0, tile),
                (ends_ref.at[:, :, pl.ds(tile, tile)], rows - tile, tile),
            )
        )
    ]
    for copy in copies:
        copy.start()
    for copy in copies:
        copy.wait()


def profile_body(across, along, parts_ref, out_ref):
    rows = out_ref.shape[1]
    parts = parts_ref[...]
    devices = parts.shape[0]
    total = parts
    for k in range(1, across):
        total = total + pltpu.roll(parts, devices - k, 0)
    row = iota(parts.shape, 0)
    squares = jnp.sum(jnp.where(row % across == 0, total * total, 0.0), keepdims=True)
    scale = jnp.sqrt(squares / (3 * rows * along) + 1e-06)
    mine = jnp.sum(jnp.where(row == lax.axis_index("gy") * across, total, 0.0), axis=0, keepdims=True) / scale
    for q in range(3):
        out_ref[q : q + 1, :] = mine[:, q * rows : (q + 1) * rows]


def per_device(state, parent_rows, dest, pick, offset, wet):
    fields, levels, rows, cols = state.shape
    planes = fields * levels
    moving = 2 * levels
    along, across = lax.axis_size("gy"), lax.axis_size("gx")
    capacity = 2 * SEND // along
    wide = cols + LANES
    f32 = jnp.float32
    even_pairs = [(i, i ^ 1) for i in range(along)]
    odd_pairs = [(i, ((i + 1) ^ 1) - 1) for i in range(1, along - 1)]
    swapped = [(0, 1), (1, 0)]
    eastward = [(i, i + 1) for i in range(across - 1)]
    westward = [(i + 1, i) for i in range(across - 1)]

    half = along // 2
    slots = half * capacity
    width = planes * cols + LANES
    halves = [list(range(half)), list(range(half, along))]

    def gathered(far):
        fetched = [pltpu.VMEM((1, SEND), jnp.int32)] * 3 + [pltpu.VMEM(parent_rows.shape, jnp.bfloat16)] if far else []
        return call(
            functools.partial(gather_body, capacity, slots, far),
            jax.ShapeDtypeStruct((slots, width), jnp.bfloat16),
            flops=2 * 8 * slots * SEND * planes * cols,
            moved=2 * (SEND + slots) * planes * cols,
            limit=VMEM_MOST,
            in_specs=[pl.BlockSpec(memory_space=pl.ANY if far else pltpu.VMEM)] * 4,
            out_specs=pl.BlockSpec(memory_space=pl.ANY),
            scratch_shapes=fetched
            + [
                pltpu.VMEM((slots, width), jnp.bfloat16),
                pltpu.SemaphoreType.DMA((4,)),
            ]
            + ([pltpu.SemaphoreType.DMA((4,))] if far else []),
        )(dest.reshape(1, SEND), pick.reshape(1, SEND), offset.reshape(1, SEND), parent_rows)

    def exchanged(payload):
        return lax.all_to_all(payload, "gy", split_axis=0, concat_axis=0, tiled=True, axis_index_groups=halves)

    far_rows = exchanged(gathered(True))

    cells = state.reshape(planes, rows, cols)
    packed_side = jax.ShapeDtypeStruct((rows, LANES), f32)
    first, last = call(sides_body, (packed_side, packed_side), moved=4 * planes * rows * cols)(cells, wet)
    if across == 2:
        west_one = lax.axis_index("gx") == 0
        other = lax.ppermute(jnp.where(west_one, last, first), "gx", swapped)
        from_west, from_east = jnp.where(west_one, 0.0, other), jnp.where(west_one, other, 0.0)
    else:
        from_west = lax.ppermute(last, "gx", eastward)
        from_east = lax.ppermute(first, "gx", westward)
    tips, mask, begun, packs, token = call(
        begin_body,
        (
            jax.ShapeDtypeStruct((planes, 4 * RIM, cols), f32),
            jax.ShapeDtypeStruct((rows, wide), f32),
            jax.ShapeDtypeStruct((planes, rows, cols), f32),
            jax.ShapeDtypeStruct((2, rows, LANES), f32),
            jax.ShapeDtypeStruct((8, LANES), f32),
        ),
        flops=20 * planes * rows * wide,
        moved=12 * planes * rows * wide,
        scratch_shapes=[pltpu.VMEM((planes, rows, wide), f32)],
    )(cells, wet, from_west, from_east)

    sums, stokes = call(
        far_body,
        (
            jax.ShapeDtypeStruct((rows, moving * cols + LANES), f32),
            jax.ShapeDtypeStruct((rows, (planes - moving) * cols), f32),
        ),
        flops=2 * rows * slots * width,
        moved=2 * slots * width + 4 * rows * width,
    )(token, far_rows)
    mirrored = [(i, (i + half) % along) for i in range(along)]
    sums, near_rows = lax.optimization_barrier((sums.astype(jnp.float16), gathered(False)))
    sums = lax.ppermute(sums, "gy", mirrored)
    arrived = exchanged(near_rows)
    stokes = lax.ppermute(stokes.astype(jnp.float16), "gy", mirrored)
    come = call(
        come_body,
        jax.ShapeDtypeStruct((8, LANES), f32),
        flops=10**11,
    )(sums[:8, :LANES].astype(f32))
    sums, arrived = lax.optimization_barrier((sums, arrived))
    sums = sums.astype(f32)

    force, edge = call(
        functools.partial(landing_body, planes, cols),
        (jax.ShapeDtypeStruct((planes, rows, cols), f32), packed_side),
        flops=2 * rows * slots * planes * cols,
        moved=2 * slots * planes * cols + 4 * rows * planes * cols,
    )(come, arrived, sums)
    if across == 2:
        sides = [lax.ppermute(edge, "gx", swapped)]
    else:
        sides = [lax.ppermute(edge, "gx", eastward), lax.ppermute(edge, "gx", westward)]
    outer = jax.ShapeDtypeStruct((moving + planes + 1 + (len(sides) + 4) // 2, RIM, cols), f32)
    up, down = call(outer_body, (outer, outer), moved=16 * (moving + planes) * RIM * cols)(
        force, edge, tips, mask, from_west, from_east, *sides
    )
    even = lax.axis_index("gy") % 2 == 0
    far = lax.ppermute(jnp.where(even, down, up).astype(jnp.float16), "gy", odd_pairs).astype(f32)
    near = lax.ppermute(jnp.where(even, up, down).astype(jnp.float16), "gy", even_pairs).astype(f32)
    above, below = jnp.where(even, near, far), jnp.where(even, far, near)
    tile = 2 * RIM
    middle, ends, part = call(
        inner_body,
        (
            jax.ShapeDtypeStruct((fields, levels, rows - 2 * tile, cols), f32),
            jax.ShapeDtypeStruct((fields, levels, 2 * tile, cols), f32),
            jax.ShapeDtypeStruct((1, LANES), f32),
        ),
        flops=60 * planes * rows * wide,
        moved=8 * planes * rows * wide,
        scratch_shapes=[
            pltpu.VMEM((moving, rows, wide), f32),
            pltpu.VMEM((planes, rows, wide), f32),
            pltpu.VMEM((planes, rows, wide), f32),
        ],
    )(mask, begun, packs, force, edge, *sides)
    stokes, part = lax.optimization_barrier((stokes, part))
    stokes = stokes.astype(f32)
    ends, parts = call(
        functools.partial(steps_body, len(sides)),
        (
            jax.ShapeDtypeStruct((fields, levels, 2 * tile, cols), f32),
            jax.ShapeDtypeStruct((along * across, LANES), f32),
        ),
        flops=60 * planes * 3 * tile * wide,
        moved=8 * planes * 3 * tile * wide,
        scratch_shapes=[
            pltpu.VMEM((moving, 3 * tile, wide), f32),
            pltpu.VMEM((planes, tile, wide), f32),
            pltpu.VMEM((planes, 3 * tile, wide), f32),
            pltpu.VMEM((planes, 3 * tile, wide), f32),
        ],
    )(stokes, tips, from_west, from_east, mask, begun, packs, force, edge, above, below, middle, ends, part, *sides)
    new_state = call(
        whole_body,
        jax.ShapeDtypeStruct(state.shape, f32),
        moved=8 * planes * rows * cols,
        out_specs=pl.BlockSpec(memory_space=pl.ANY),
        scratch_shapes=[pltpu.SemaphoreType.DMA((3,))],
    )(middle, ends)
    every = lax.all_to_all(parts, ("gy", "gx"), split_axis=0, concat_axis=0, tiled=True)
    profile = call(functools.partial(profile_body, across, along), jax.ShapeDtypeStruct((3, rows), f32))(every)
    return new_state, profile


def solution(mesh):
    in_specs = (
        P(None, None, "gy", "gx"),
        P(("gy", "gx"), None, None),
        P(("gy", "gx"), None),
        P(("gy", "gx")),
        P(("gy", "gx")),
        P("gy", "gx"),
    )
    out_specs = (P(None, None, "gy", "gx"), P(None, "gy"))
    return jax.shard_map(
        per_device, mesh=mesh, in_specs=in_specs, out_specs=out_specs, check_vma=False
    )
```

```python
import functools

import jax
import jax.numpy as jnp
from jax import lax
from jax.experimental import pallas as pl
from jax.experimental.pallas import tpu as pltpu
from jax.sharding import PartitionSpec as P

SEND = 64
STEPS = 3

KH = 0.2
KZ = 0.05
ADV = 0.25
PG = 0.5
GAMMA = 0.5
DISPERSE = 2.0

EDGE = 3
RIM = 4
LANES = 128
STATE_SCALE = 8192.0
FORCE_SCALE = 64.0
SUM_SCALE = 128.0
VMEM_LIMIT = 16 * 1024 * 1024
VMEM_MOST = 60 * 1024 * 1024


def call(body, out_shape, flops=0, moved=0, limit=VMEM_LIMIT, **more):
    return pl.pallas_call(
        body,
        out_shape=out_shape,
        compiler_params=pltpu.CompilerParams(vmem_limit_bytes=limit),
        cost_estimate=pl.CostEstimate(flops=flops, bytes_accessed=moved, transcendentals=0),
        **more,
    )


def iota(shape, dim):
    return lax.broadcasted_iota(jnp.int32, shape, dim)


def gather_body(capacity, slots, far, *refs):
    if far:
        sources, out_ref, targets, held_ref, sent, copied = refs[:4], refs[4], refs[5:9], *refs[9:]
        copies = [
            pltpu.make_async_copy(source, target, copied.at[k])
            for k, (source, target) in enumerate(zip(sources, targets))
        ]
    else:
        targets, (out_ref, held_ref, sent), copies = refs[:4], refs[4:], []
    for copy in copies:
        copy.start()
    dest_ref, pick_ref, offset_ref, rows_ref = targets
    send, planes, cols = rows_ref.shape
    for copy in copies[:3]:
        copy.wait()
    dest = dest_ref[...]
    eye = iota((send, send), 0) == iota((send, send), 1)
    dest_column = jnp.sum(jnp.where(eye, dest, 0), axis=1, keepdims=True)
    earlier = (dest_column == dest) & (iota((send, send), 0) < iota((send, send), 1))
    rank = jnp.sum(earlier.astype(jnp.int32), axis=0, keepdims=True)
    half = slots // capacity
    mine = lax.axis_index("gy") >= half
    there = (dest >= half) != mine if far else (dest >= half) == mine
    slot_of = jnp.where(there, jnp.where(dest >= half, dest - half, dest) * capacity + rank, -1)
    taken = iota((slots, send), 0) == slot_of
    source = jnp.sum(jnp.where(taken, pick_ref[...] + 1, 0), axis=1, keepdims=True) - 1
    label = jnp.sum(jnp.where(taken, offset_ref[...] + 1, 0), axis=1, keepdims=True)
    group = 8
    lane = iota((slots, send * group), 1)
    select = jnp.concatenate(
        [(lane == source * group + j).astype(jnp.float32).astype(jnp.bfloat16) for j in range(group)], axis=0
    )
    width = planes * cols
    held_ref[:, width:] = jnp.broadcast_to(label, (slots, LANES)).astype(jnp.float32).astype(jnp.bfloat16)
    for copy in copies[3:]:
        copy.wait()
    parts = []

    def send_columns(start, size):
        part = pltpu.make_async_copy(
            held_ref.at[:, pl.ds(start, size)], out_ref.at[:, pl.ds(start, size)], sent.at[len(parts)]
        )
        part.start()
        parts.append(part)

    send_columns(width, LANES)
    for g in range(planes // group):
        block = rows_ref[:, g * group : (g + 1) * group, :].reshape(send * group, cols)
        got = jnp.dot(select, block, preferred_element_type=jnp.float32).astype(jnp.bfloat16)
        for j in range(group):
            at = (g * group + j) * cols
            held_ref[:, at : at + cols] = got[j * slots : (j + 1) * slots]
        send_columns(g * group * cols, group * cols)
    for part in parts:
        part.wait()


def landing_of(arrived_ref, rows):
    slots, width = arrived_ref.shape
    label = arrived_ref[:, width - LANES :].astype(jnp.float32)
    landing = (label == (iota((slots, LANES), 1) + 1).astype(jnp.float32)).astype(jnp.float32)
    return landing.T[:rows].astype(jnp.bfloat16)


def landed(landing, values):
    return jnp.dot(landing, values, preferred_element_type=jnp.float32)


def far_body(token_ref, arrived_ref, sums_ref, stokes_ref):
    rows, width = sums_ref.shape
    slots = arrived_ref.shape[0]
    landing = landing_of(arrived_ref, rows)
    moving, step = width - LANES, 2 * LANES
    for at in range(0, moving, step):
        sums_ref[:, at : at + step] = landed(landing, arrived_ref[:, at : at + step]) * SUM_SCALE
    sums_ref[:, moving:] = landed(landing, jnp.full((slots, LANES), SUM_SCALE, jnp.bfloat16))
    for at in range(0, stokes_ref.shape[1], step):
        there = slice(moving + at, moving + at + step)
        stokes_ref[:, at : at + step] = landed(landing, arrived_ref[:, there]) * SUM_SCALE


def come_body(sums_ref, token_ref):
    token_ref[...] = jnp.zeros_like(token_ref)


def landing_body(planes, cols, token_ref, arrived_ref, sums_ref, force_ref, edge_ref):
    slots = arrived_ref.shape[0]
    rows = force_ref.shape[1]
    landing = landing_of(arrived_ref, rows)
    far = 1.0 / SUM_SCALE
    moving = 2 * planes // 3
    count = landed(landing, jnp.ones((slots, LANES), jnp.bfloat16)) + sums_ref[:, moving * cols :] * far
    edge = count
    for j in range(planes):
        at = slice(j * cols, (j + 1) * cols)
        force = landed(landing, arrived_ref[:, at])
        if j < moving:
            force = force + sums_ref[:, at] * far
        force_ref[j] = force
        if j < moving:
            edge = packed(edge, force[:, :LANES], 0, EDGE * j)
            edge = packed(edge, force[:, cols - LANES :], LANES - EDGE, EDGE * (moving + j))
    edge_ref[...] = edge


def packed(into, tile, start, at):
    lane = iota(tile.shape, 1)
    shifted = pltpu.roll(tile, (at - start) % LANES, 1)
    return jnp.where((lane >= at) & (lane < at + EDGE), shifted, into)


def sides_body(state_ref, wet_ref, first_ref, last_ref):
    planes, rows, cols = state_ref.shape
    first = jnp.zeros((rows, LANES), jnp.float32)
    last = jnp.zeros((rows, LANES), jnp.float32)
    for j in range(planes + 1):
        own = state_ref[j] if j < planes else wet_ref[...].astype(jnp.float32)
        first = packed(first, own[:, :LANES], 0, EDGE * j)
        last = packed(last, own[:, cols - LANES :], LANES - EDGE, EDGE * j)
    first_ref[...] = first
    last_ref[...] = last


def side_tile(west, west_at, east, east_at):
    lane = iota(west.shape, 1)
    right = pltpu.roll(east, (LANES - east_at) % LANES, 1)
    left = pltpu.roll(west, (2 * LANES - EDGE - west_at) % LANES, 1)
    return jnp.where(lane < EDGE, right, jnp.where(lane >= LANES - EDGE, left, 0.0))


def around(field):
    rows, cols = field.shape
    return (
        pltpu.roll(field, cols - 1, 1),
        pltpu.roll(field, 1, 1),
        pltpu.roll(field, rows - 1, 0),
        pltpu.roll(field, 1, 0),
    )


def around_between(field, north_row, south_row):
    east, west, north, south = around(field)
    row = iota(field.shape, 0)
    return east, west, jnp.where(row == field.shape[0] - 1, north_row, north), jnp.where(row == 0, south_row, south)


def moved(load, near, levels, z):
    upper, lower = min(z + 1, levels - 1), max(z - 1, 0)
    results = []
    fields = [load(f * levels + z) for f in range(3)]
    tracer, across, along = fields
    around_tracer = near(z, tracer)
    east, west, north, south = around_tracer
    ddx, ddy = east - west, north - south
    extra = (0.5 * ADV * (across * ddx + along * ddy), 0.5 * PG * ddx, 0.5 * PG * ddy)
    for f, centre in enumerate(fields):
        sides = around_tracer if f == 0 else near(f * levels + z, centre)
        beside = KH * ((sides[0] + sides[1]) + (sides[2] + sides[3]))
        beyond = KZ * (load(f * levels + upper) + load(f * levels + lower))
        results.append((1.0 - 4.0 * KH - 2.0 * KZ) * centre + beside + (beyond - extra[f]))
    return results


def added(sign, along, tracer, across_near, along_near):
    return [
        (KH - sign * 0.5 * ADV * along) * tracer,
        KH * across_near,
        KH * along_near - sign * 0.5 * PG * tracer,
    ]


def begin_body(state_ref, wet_ref, west_ref, east_ref, tips_ref, mask_ref, begun_ref, packs_ref, token_ref, full_ref):
    planes, rows, cols = state_ref.shape
    levels = planes // 3
    west, east = west_ref[...], east_ref[...]
    for j in range(planes):
        tips_ref[j] = outer_rows(state_ref, j)
    for j in range(planes):
        full_ref[j, :, :cols] = state_ref[j]
        full_ref[j, :, cols:] = side_tile(west, EDGE * j, east, EDGE * j)
    mask_ref[:, :cols] = wet_ref[...].astype(jnp.float32)
    mask_ref[:, cols:] = side_tile(west, EDGE * planes, east, EDGE * planes)
    packs = [jnp.zeros((rows, LANES), jnp.float32) for _ in range(2)]
    for z in range(levels):
        values = moved(lambda j: full_ref[j], lambda j, field: around_between(field, 0.0, 0.0), levels, z)
        for f, value in enumerate(values):
            j = f * levels + z
            begun_ref[j] = value[:, :cols]
            packs[0] = packed(packs[0], value[:, cols:], LANES - EDGE, EDGE * j)
            packs[1] = packed(packs[1], value[:, cols:], 0, EDGE * j)
    packs_ref[0], packs_ref[1] = packs
    token_ref[...] = jnp.zeros_like(token_ref)


def outer_rows(ref, *index):
    rows, tile = ref.shape[len(index)], 2 * RIM
    first, last = ref[(*index, slice(0, tile))], ref[(*index, slice(rows - tile, rows))]
    return jnp.where(iota(first.shape, 0) < RIM, first, last)


def widened(plane, west, east, at):
    return jnp.concatenate([plane, side_tile(west, at, east, at)], axis=1)


def outer_body(force_ref, edge_ref, tips_ref, mask_ref, west_ref, east_ref, *refs):
    sides, (up_ref, down_ref) = refs[:-2], refs[-2:]
    planes, rows, cols = force_ref.shape
    moving = 2 * planes // 3
    ends = ((up_ref, slice(rows - RIM, rows), slice(RIM, 2 * RIM)), (down_ref, slice(0, RIM), slice(0, RIM)))
    for out_ref, at, tip in ends:
        out_ref[:moving] = force_ref[:moving, at] * FORCE_SCALE
        out_ref[moving : moving + planes] = tips_ref[:, tip] * STATE_SCALE
        out_ref[moving + planes] = mask_ref[at, :cols] * STATE_SCALE
        parts = [west_ref[at], east_ref[at], edge_ref[at]] + [side[at] for side in sides]
        for k, part in enumerate(parts):
            lane = (k % 2) * LANES
            out_ref[moving + planes + 1 + k // 2, :, lane : lane + LANES] = part * (STATE_SCALE if k < 2 else FORCE_SCALE)


def factors(mask, own, west, east, force_rows, push_ref):
    moving, total, wide = push_ref.shape
    cols = wide - LANES

    def counts(edge):
        return jnp.broadcast_to(edge[:, LANES - 1 :], (total, LANES))

    lane = iota((total, LANES), 1)
    count_side = jnp.where(lane < LANES // 2, counts(east), counts(west))
    relax = mask / (1.0 + GAMMA * jnp.concatenate([counts(own)] * (cols // LANES) + [count_side], axis=1))
    half = GAMMA * relax
    for j in range(moving):
        push_ref[j, :, :cols] = force_rows(j) * half[:, :cols]
        push_ref[j, :, cols:] = side_tile(west, EDGE * (moving + j), east, EDGE * j) * half[:, cols:]
    return relax


def finish(relax, push_ref, levels, values, z, at=(slice(None),)):
    tracer, across, along = values
    rated = relax[at]
    return (tracer * rated + push_ref[(z, *at)], across * rated, along * rated + push_ref[(levels + z, *at)])


def two_more(relax, push_ref, one_ref, two_ref, last, patched=lambda j, value: value):
    levels = one_ref.shape[0] // 3
    cols = one_ref.shape[2] - LANES
    for z in range(levels):
        values = moved(lambda j: one_ref[j], lambda j, field: around(field), levels, z)
        for f, value in enumerate(finish(relax, push_ref, levels, values, z)):
            two_ref[f * levels + z] = patched(f * levels + z, value)
    for z in range(levels):
        values = moved(
            lambda j: two_ref[j, :, :cols],
            lambda j, field: tuple(side[:, :cols] for side in around(two_ref[j])),
            levels,
            z,
        )
        last(z, finish(relax, push_ref, levels, values, z, (slice(None), slice(0, cols))))


def terms(values, stokes):
    rows, total = stokes.shape[0], values[0].shape[0]
    tracer = values[0]
    ddy = pltpu.roll(tracer, total - 1, 0)[:rows] - pltpu.roll(tracer, 1, 0)[:rows]
    return [values[2][:rows] * tracer[:rows], stokes * tracer[:rows], ddy]


def transports(sums, count, child, all_rows):
    raw = [jnp.sum(value, axis=1, keepdims=True) for value in sums]
    raw = [raw[0], raw[1] / (1.0 + count), raw[2] * (-0.5 * DISPERSE)]
    lane = iota(child.shape, 1)
    part = jnp.zeros(child.shape, jnp.float32)
    for q in range(3):
        part = part + jnp.where((child >= 0) & (lane == q * all_rows + child), raw[q], 0.0)
    return jnp.sum(part, axis=0, keepdims=True)


def inner_body(mask_ref, begun_ref, packs_ref, force_ref, edge_ref, *refs):
    side_refs, (middle_ref, ends_ref, part_ref, twos_ref, push_ref, one_ref, two_ref) = refs[:-7], refs[-7:]
    planes, rows, cols = begun_ref.shape
    levels = planes // 3
    moving = 2 * levels
    tile = 2 * RIM
    west, east = packs_ref[0], packs_ref[1]
    relax = factors(
        mask_ref[...], edge_ref[...], side_refs[0][...], side_refs[-1][...], lambda j: force_ref[j], push_ref
    )
    for z in range(levels):
        index = [f * levels + z for f in range(3)]
        values = [widened(begun_ref[j], west, east, EDGE * j) for j in index]
        for j, value in zip(index, finish(relax, push_ref, levels, values, z)):
            one_ref[j] = value
    sums = [jnp.zeros((rows, cols), jnp.float32) for _ in range(3)]

    def last(z, values):
        for f, value in enumerate(values):
            middle_ref[f, z] = value[tile : rows - tile]
            ends_ref[f, z, :tile] = value[:tile]
            ends_ref[f, z, tile:] = value[rows - tile :]
        for q, term in enumerate(terms(values, force_ref[moving + z])):
            sums[q] = sums[q] + term

    two_more(relax, push_ref, one_ref, two_ref, last)
    for j in range(planes):
        twos_ref[j] = outer_rows(two_ref, j)
    row = iota((rows, LANES), 0)
    child = jnp.where((row >= RIM) & (row < rows - RIM), row, -1)
    part_ref[...] = transports(sums, edge_ref[:, LANES - 1 :], child, rows)


def steps_body(
    sides, stokes_ref, tips_ref, west_ref, east_ref, mask_ref, begun_ref, packs_ref, force_ref, edge_ref, north_ref, south_ref, *refs
):
    middle_ref, ends_ref, part_ref, twos_ref = refs[:4]
    refs = refs[4:]
    side_refs = refs[:sides]
    held_ref, parts_ref, push_ref, halo_ref, one_ref, two_ref = refs[sides:]
    planes, rows, cols = begun_ref.shape
    wide = cols + LANES
    levels = planes // 3
    moving = 2 * levels
    tile = 2 * RIM
    total = 2 * tile

    def joined(index, scale):
        return jnp.concatenate([north_ref[index], south_ref[index]], axis=0) * (1.0 / scale)

    def half_of(k, scale):
        lane = (k % 2) * LANES
        return joined(moving + planes + 1 + k // 2, scale)[:, lane : lane + LANES]

    beside = [half_of(k, STATE_SCALE) for k in range(2)]
    outer = [half_of(2 + k, FORCE_SCALE) for k in range(1 + sides)]
    edges = [jnp.concatenate([outer_rows(side), outer[1 + k]], axis=0) for k, side in enumerate(side_refs)]
    own = jnp.concatenate([outer_rows(edge_ref), outer[0]], axis=0)

    def halo(index, at):
        return widened(joined(moving + index, STATE_SCALE), *beside, at)

    mask = jnp.concatenate([outer_rows(mask_ref), halo(planes, EDGE * planes)], axis=0)
    relax = factors(
        mask,
        own,
        edges[0],
        edges[-1],
        lambda j: jnp.concatenate([outer_rows(force_ref, j), joined(j, FORCE_SCALE)], axis=0),
        push_ref,
    )
    for j in range(planes):
        halo_ref[j] = halo(j, EDGE * j)
    row = iota((tile, wide), 0)
    packs = [outer_rows(packs_ref, k) for k in range(2)]
    wests, easts = outer_rows(west_ref), outer_rows(east_ref)

    def tip(j):
        return widened(tips_ref[j], wests, easts, EDGE * j)

    def begun(j):
        return widened(outer_rows(begun_ref, j), *packs, EDGE * j)

    def near(j, field):
        start = tip(j)
        return around_between(field, start[:1], start[tile - 1 :])

    for z in range(levels):
        index = [f * levels + z for f in range(3)]
        beyond = [halo_ref[j] for j in index]
        north = [jnp.where(row == tile - 1, value[:1], 0.0) for value in beyond]
        south = [jnp.where(row == 0, value[tile - 1 :], 0.0) for value in beyond]
        along = tip(index[2])
        extras = zip(added(-1.0, along, *south), added(1.0, along, *north))
        blocks = (
            [begun(j) + (first + final) for j, (first, final) in zip(index, extras)],
            moved(lambda j: halo_ref[j], near, levels, z),
        )
        for k, values in enumerate(blocks):
            at = slice(k * tile, (k + 1) * tile)
            for j, value in zip(index, finish(relax, push_ref, levels, values, z, (at,))):
                one_ref[j, at] = value

    meeting = (row == RIM - 1) | (row == RIM)

    def patched(j, value):
        return jnp.concatenate([jnp.where(meeting, twos_ref[j], value[:tile]), value[tile:]], axis=0)

    sums = [jnp.zeros((tile, cols), jnp.float32) for _ in range(3)]
    place = iota((tile, cols), 0)

    def last(z, values):
        finals = []
        for f, value in enumerate(values):
            ends = [ends_ref[f, z, :tile], ends_ref[f, z, tile:]]
            kept = jnp.where(place < RIM, *ends)
            final = jnp.where((place == RIM - 1) | (place == RIM), kept, value[:tile])
            held_ref[f, z, :tile] = jnp.where(place < RIM, final, ends[0])
            held_ref[f, z, tile:] = jnp.where(place < RIM, ends[1], final)
            finals.append(final)
        tracer = jnp.concatenate([finals[0], values[0][tile:]], axis=0)
        within = jnp.where(place < RIM, ends_ref[0, z, tile:], ends_ref[0, z, :tile])
        north = jnp.where(place == RIM - 1, pltpu.roll(within, tile - 1, 0), pltpu.roll(tracer, total - 1, 0)[:tile])
        south = jnp.where(place == RIM, pltpu.roll(within, 1, 0), pltpu.roll(tracer, 1, 0)[:tile])
        stokes = outer_rows(force_ref, moving + z)
        for q, term in enumerate((finals[2] * finals[0], stokes * finals[0], north - south)):
            sums[q] = sums[q] + term

    two_more(relax, push_ref, one_ref, two_ref, last, patched)
    beyond = jnp.zeros((rows, cols), jnp.float32)
    for z in range(levels):
        tracer = [held_ref[0, z, :tile], middle_ref[0, z], held_ref[0, z, tile:]]
        beyond = beyond + stokes_ref[:, z * cols : (z + 1) * cols] * jnp.concatenate(tracer, axis=0)
    beyond = jnp.sum(beyond, axis=1, keepdims=True) / (SUM_SCALE * (1.0 + edge_ref[:, LANES - 1 :]))
    row, lane = iota((rows, LANES), 0), iota((rows, LANES), 1)
    beyond = jnp.sum(jnp.where(lane == rows + row, beyond, 0.0), axis=0, keepdims=True)
    row = iota((tile, LANES), 0)
    child = jnp.where(row < RIM, row, row + rows - tile)
    part = transports(sums, own[:tile, LANES - 1 :], child, rows) + (part_ref[...] + beyond)
    parts_ref[...] = jnp.broadcast_to(part, parts_ref.shape)


def whole_body(middle_ref, ends_ref, state_ref, sent):
    rows = state_ref.shape[2]
    tile = ends_ref.shape[2] // 2
    copies = [
        pltpu.make_async_copy(source, state_ref.at[:, :, pl.ds(start, size)], sent.at[k])
        for k, (source, start, size) in enumerate(
            (
                (middle_ref, tile, rows - 2 * tile),
                (ends_ref.at[:, :, pl.ds(0, tile)], 0, tile),
                (ends_ref.at[:, :, pl.ds(tile, tile)], rows - tile, tile),
            )
        )
    ]
    for copy in copies:
        copy.start()
    for copy in copies:
        copy.wait()


def profile_body(across, along, parts_ref, out_ref):
    rows = out_ref.shape[1]
    parts = parts_ref[...]
    devices = parts.shape[0]
    total = parts
    for k in range(1, across):
        total = total + pltpu.roll(parts, devices - k, 0)
    row = iota(parts.shape, 0)
    squares = jnp.sum(jnp.where(row % across == 0, total * total, 0.0), keepdims=True)
    scale = jnp.sqrt(squares / (3 * rows * along) + 1e-06)
    mine = jnp.sum(jnp.where(row == lax.axis_index("gy") * across, total, 0.0), axis=0, keepdims=True) / scale
    for q in range(3):
        out_ref[q : q + 1, :] = mine[:, q * rows : (q + 1) * rows]


def per_device(state, parent_rows, dest, pick, offset, wet):
    fields, levels, rows, cols = state.shape
    planes = fields * levels
    moving = 2 * levels
    along, across = lax.axis_size("gy"), lax.axis_size("gx")
    capacity = 2 * SEND // along
    wide = cols + LANES
    f32 = jnp.float32
    even_pairs = [(i, i ^ 1) for i in range(along)]
    odd_pairs = [(i, ((i + 1) ^ 1) - 1) for i in range(1, along - 1)]
    swapped = [(0, 1), (1, 0)]
    eastward = [(i, i + 1) for i in range(across - 1)]
    westward = [(i + 1, i) for i in range(across - 1)]

    half = along // 2
    slots = half * capacity
    width = planes * cols + LANES
    halves = [list(range(half)), list(range(half, along))]

    def gathered(far):
        fetched = [pltpu.VMEM((1, SEND), jnp.int32)] * 3 + [pltpu.VMEM(parent_rows.shape, jnp.bfloat16)] if far else []
        return call(
            functools.partial(gather_body, capacity, slots, far),
            jax.ShapeDtypeStruct((slots, width), jnp.bfloat16),
            flops=2 * 8 * slots * SEND * planes * cols,
            moved=2 * (SEND + slots) * planes * cols,
            limit=VMEM_MOST,
            in_specs=[pl.BlockSpec(memory_space=pl.ANY if far else pltpu.VMEM)] * 4,
            out_specs=pl.BlockSpec(memory_space=pl.ANY),
            scratch_shapes=fetched
            + [
                pltpu.VMEM((slots, width), jnp.bfloat16),
                pltpu.SemaphoreType.DMA((4,)),
            ]
            + ([pltpu.SemaphoreType.DMA((4,))] if far else []),
        )(dest.reshape(1, SEND), pick.reshape(1, SEND), offset.reshape(1, SEND), parent_rows)

    def exchanged(payload):
        return lax.all_to_all(payload, "gy", split_axis=0, concat_axis=0, tiled=True, axis_index_groups=halves)

    far_rows = exchanged(gathered(True))

    cells = state.reshape(planes, rows, cols)
    packed_side = jax.ShapeDtypeStruct((rows, LANES), f32)
    first, last = call(sides_body, (packed_side, packed_side), moved=4 * planes * rows * cols)(cells, wet)
    if across == 2:
        west_one = lax.axis_index("gx") == 0
        other = lax.ppermute(jnp.where(west_one, last, first), "gx", swapped)
        from_west, from_east = jnp.where(west_one, 0.0, other), jnp.where(west_one, other, 0.0)
    else:
        from_west = lax.ppermute(last, "gx", eastward)
        from_east = lax.ppermute(first, "gx", westward)
    tips, mask, begun, packs, token = call(
        begin_body,
        (
            jax.ShapeDtypeStruct((planes, 2 * RIM, cols), f32),
            jax.ShapeDtypeStruct((rows, wide), f32),
            jax.ShapeDtypeStruct((planes, rows, cols), f32),
            jax.ShapeDtypeStruct((2, rows, LANES), f32),
            jax.ShapeDtypeStruct((8, LANES), f32),
        ),
        flops=20 * planes * rows * wide,
        moved=12 * planes * rows * wide,
        scratch_shapes=[pltpu.VMEM((planes, rows, wide), f32)],
    )(cells, wet, from_west, from_east)

    sums, stokes = call(
        far_body,
        (
            jax.ShapeDtypeStruct((rows, moving * cols + LANES), f32),
            jax.ShapeDtypeStruct((rows, (planes - moving) * cols), f32),
        ),
        flops=2 * rows * slots * width,
        moved=2 * slots * width + 4 * rows * width,
    )(token, far_rows)
    mirrored = [(i, (i + half) % along) for i in range(along)]
    sums, near_rows = lax.optimization_barrier((sums.astype(jnp.float16), gathered(False)))
    sums = lax.ppermute(sums, "gy", mirrored)
    arrived = exchanged(near_rows)
    stokes = lax.ppermute(stokes.astype(jnp.float16), "gy", mirrored)
    come = call(
        come_body,
        jax.ShapeDtypeStruct((8, LANES), f32),
        flops=10**11,
    )(sums[:8, :LANES].astype(f32))
    sums, arrived = lax.optimization_barrier((sums, arrived))
    sums = sums.astype(f32)

    force, edge = call(
        functools.partial(landing_body, planes, cols),
        (jax.ShapeDtypeStruct((planes, rows, cols), f32), packed_side),
        flops=2 * rows * slots * planes * cols,
        moved=2 * slots * planes * cols + 4 * rows * planes * cols,
    )(come, arrived, sums)
    if across == 2:
        sides = [lax.ppermute(edge, "gx", swapped)]
    else:
        sides = [lax.ppermute(edge, "gx", eastward), lax.ppermute(edge, "gx", westward)]
    outer = jax.ShapeDtypeStruct((moving + planes + 1 + (len(sides) + 4) // 2, RIM, cols), f32)
    up, down = call(outer_body, (outer, outer), moved=16 * (moving + planes) * RIM * cols)(
        force, edge, tips, mask, from_west, from_east, *sides
    )
    even = lax.axis_index("gy") % 2 == 0
    far = lax.ppermute(jnp.where(even, down, up).astype(jnp.float16), "gy", odd_pairs).astype(f32)
    near = lax.ppermute(jnp.where(even, up, down).astype(jnp.float16), "gy", even_pairs).astype(f32)
    above, below = jnp.where(even, near, far), jnp.where(even, far, near)
    tile = 2 * RIM
    middle, ends, part, twos = call(
        inner_body,
        (
            jax.ShapeDtypeStruct((fields, levels, rows - 2 * tile, cols), f32),
            jax.ShapeDtypeStruct((fields, levels, 2 * tile, cols), f32),
            jax.ShapeDtypeStruct((1, LANES), f32),
            jax.ShapeDtypeStruct((planes, tile, wide), f32),
        ),
        flops=60 * planes * rows * wide,
        moved=8 * planes * rows * wide,
        scratch_shapes=[
            pltpu.VMEM((moving, rows, wide), f32),
            pltpu.VMEM((planes, rows, wide), f32),
            pltpu.VMEM((planes, rows, wide), f32),
        ],
    )(mask, begun, packs, force, edge, *sides)
    stokes, part = lax.optimization_barrier((stokes, part))
    stokes = stokes.astype(f32)
    ends, parts = call(
        functools.partial(steps_body, len(sides)),
        (
            jax.ShapeDtypeStruct((fields, levels, 2 * tile, cols), f32),
            jax.ShapeDtypeStruct((along * across, LANES), f32),
        ),
        flops=60 * planes * 3 * tile * wide,
        moved=8 * planes * 3 * tile * wide,
        scratch_shapes=[
            pltpu.VMEM((moving, 2 * tile, wide), f32),
            pltpu.VMEM((planes, tile, wide), f32),
            pltpu.VMEM((planes, 2 * tile, wide), f32),
            pltpu.VMEM((planes, 2 * tile, wide), f32),
        ],
    )(stokes, tips, from_west, from_east, mask, begun, packs, force, edge, above, below, middle, ends, part, twos, *sides)
    new_state = call(
        whole_body,
        jax.ShapeDtypeStruct(state.shape, f32),
        moved=8 * planes * rows * cols,
        out_specs=pl.BlockSpec(memory_space=pl.ANY),
        scratch_shapes=[pltpu.SemaphoreType.DMA((3,))],
    )(middle, ends)
    every = lax.all_to_all(parts, ("gy", "gx"), split_axis=0, concat_axis=0, tiled=True)
    profile = call(functools.partial(profile_body, across, along), jax.ShapeDtypeStruct((3, rows), f32))(every)
    return new_state, profile


def solution(mesh):
    in_specs = (
        P(None, None, "gy", "gx"),
        P(("gy", "gx"), None, None),
        P(("gy", "gx"), None),
        P(("gy", "gx")),
        P(("gy", "gx")),
        P("gy", "gx"),
    )
    out_specs = (P(None, None, "gy", "gx"), P(None, "gy"))
    return jax.shard_map(
        per_device, mesh=mesh, in_specs=in_specs, out_specs=out_specs, check_vma=False
    )
```

```python
import functools

import jax
import jax.numpy as jnp
from jax import lax
from jax.experimental import pallas as pl
from jax.experimental.pallas import tpu as pltpu
from jax.sharding import PartitionSpec as P

SEND = 64
STEPS = 3

KH = 0.2
KZ = 0.05
ADV = 0.25
PG = 0.5
GAMMA = 0.5
DISPERSE = 2.0

EDGE = 3
RIM = 4
LANES = 128
STATE_SCALE = 8192.0
FORCE_SCALE = 64.0
SUM_SCALE = 128.0
VMEM_LIMIT = 16 * 1024 * 1024
VMEM_MOST = 60 * 1024 * 1024


def call(body, out_shape, flops=0, moved=0, limit=VMEM_LIMIT, **more):
    return pl.pallas_call(
        body,
        out_shape=out_shape,
        compiler_params=pltpu.CompilerParams(vmem_limit_bytes=limit),
        cost_estimate=pl.CostEstimate(flops=flops, bytes_accessed=moved, transcendentals=0),
        **more,
    )


def iota(shape, dim):
    return lax.broadcasted_iota(jnp.int32, shape, dim)


def gather_body(capacity, slots, far, *refs):
    if far:
        sources, out_ref, targets, held_ref, sent, copied = refs[:4], refs[4], refs[5:9], *refs[9:]
        copies = [
            pltpu.make_async_copy(source, target, copied.at[k])
            for k, (source, target) in enumerate(zip(sources, targets))
        ]
    else:
        targets, (out_ref, held_ref, sent), copies = refs[:4], refs[4:], []
    for copy in copies:
        copy.start()
    dest_ref, pick_ref, offset_ref, rows_ref = targets
    send, planes, cols = rows_ref.shape
    for copy in copies[:3]:
        copy.wait()
    dest = dest_ref[...]
    eye = iota((send, send), 0) == iota((send, send), 1)
    dest_column = jnp.sum(jnp.where(eye, dest, 0), axis=1, keepdims=True)
    earlier = (dest_column == dest) & (iota((send, send), 0) < iota((send, send), 1))
    rank = jnp.sum(earlier.astype(jnp.int32), axis=0, keepdims=True)
    half = slots // capacity
    mine = lax.axis_index("gy") >= half
    there = (dest >= half) != mine if far else (dest >= half) == mine
    slot_of = jnp.where(there, jnp.where(dest >= half, dest - half, dest) * capacity + rank, -1)
    taken = iota((slots, send), 0) == slot_of
    source = jnp.sum(jnp.where(taken, pick_ref[...] + 1, 0), axis=1, keepdims=True) - 1
    label = jnp.sum(jnp.where(taken, offset_ref[...] + 1, 0), axis=1, keepdims=True)
    group = 8
    lane = iota((slots, send * group), 1)
    select = jnp.concatenate(
        [(lane == source * group + j).astype(jnp.float32).astype(jnp.bfloat16) for j in range(group)], axis=0
    )
    width = planes * cols
    held_ref[:, width:] = jnp.broadcast_to(label, (slots, LANES)).astype(jnp.float32).astype(jnp.bfloat16)
    for copy in copies[3:]:
        copy.wait()
    parts = []

    def send_columns(start, size):
        part = pltpu.make_async_copy(
            held_ref.at[:, pl.ds(start, size)], out_ref.at[:, pl.ds(start, size)], sent.at[len(parts)]
        )
        part.start()
        parts.append(part)

    send_columns(width, LANES)
    for g in range(planes // group):
        block = rows_ref[:, g * group : (g + 1) * group, :].reshape(send * group, cols)
        got = jnp.dot(select, block, preferred_element_type=jnp.float32).astype(jnp.bfloat16)
        for j in range(group):
            at = (g * group + j) * cols
            held_ref[:, at : at + cols] = got[j * slots : (j + 1) * slots]
        send_columns(g * group * cols, group * cols)
    for part in parts:
        part.wait()


def landing_of(arrived_ref, rows):
    slots, width = arrived_ref.shape
    label = arrived_ref[:, width - LANES :].astype(jnp.float32)
    landing = (label == (iota((slots, LANES), 1) + 1).astype(jnp.float32)).astype(jnp.float32)
    return landing.T[:rows].astype(jnp.bfloat16)


def landed(landing, values):
    return jnp.dot(landing, values, preferred_element_type=jnp.float32)


def far_body(token_ref, arrived_ref, sums_ref, stokes_ref):
    rows, width = sums_ref.shape
    slots = arrived_ref.shape[0]
    landing = landing_of(arrived_ref, rows)
    moving, step = width - LANES, 2 * LANES
    for at in range(0, moving, step):
        sums_ref[:, at : at + step] = landed(landing, arrived_ref[:, at : at + step]) * SUM_SCALE
    sums_ref[:, moving:] = landed(landing, jnp.full((slots, LANES), SUM_SCALE, jnp.bfloat16))
    for at in range(0, stokes_ref.shape[1], step):
        there = slice(moving + at, moving + at + step)
        stokes_ref[:, at : at + step] = landed(landing, arrived_ref[:, there]) * SUM_SCALE


def come_body(sums_ref, token_ref):
    token_ref[...] = jnp.zeros_like(token_ref)


def landing_body(planes, cols, token_ref, arrived_ref, sums_ref, force_ref, edge_ref):
    slots = arrived_ref.shape[0]
    rows = force_ref.shape[1]
    landing = landing_of(arrived_ref, rows)
    far = 1.0 / SUM_SCALE
    moving = 2 * planes // 3
    count = landed(landing, jnp.ones((slots, LANES), jnp.bfloat16)) + sums_ref[:, moving * cols :] * far
    edge = count
    for j in range(planes):
        at = slice(j * cols, (j + 1) * cols)
        force = landed(landing, arrived_ref[:, at])
        if j < moving:
            force = force + sums_ref[:, at] * far
        force_ref[j] = force
        if j < moving:
            edge = packed(edge, force[:, :LANES], 0, EDGE * j)
            edge = packed(edge, force[:, cols - LANES :], LANES - EDGE, EDGE * (moving + j))
    edge_ref[...] = edge


def packed(into, tile, start, at):
    lane = iota(tile.shape, 1)
    shifted = pltpu.roll(tile, (at - start) % LANES, 1)
    return jnp.where((lane >= at) & (lane < at + EDGE), shifted, into)


def sides_body(state_ref, wet_ref, first_ref, last_ref):
    planes, rows, cols = state_ref.shape
    first = jnp.zeros((rows, LANES), jnp.float32)
    last = jnp.zeros((rows, LANES), jnp.float32)
    for j in range(planes + 1):
        own = state_ref[j] if j < planes else wet_ref[...].astype(jnp.float32)
        first = packed(first, own[:, :LANES], 0, EDGE * j)
        last = packed(last, own[:, cols - LANES :], LANES - EDGE, EDGE * j)
    first_ref[...] = first
    last_ref[...] = last


def side_tile(west, west_at, east, east_at):
    lane = iota(west.shape, 1)
    right = pltpu.roll(east, (LANES - east_at) % LANES, 1)
    left = pltpu.roll(west, (2 * LANES - EDGE - west_at) % LANES, 1)
    return jnp.where(lane < EDGE, right, jnp.where(lane >= LANES - EDGE, left, 0.0))


def around(field):
    rows, cols = field.shape
    return (
        pltpu.roll(field, cols - 1, 1),
        pltpu.roll(field, 1, 1),
        pltpu.roll(field, rows - 1, 0),
        pltpu.roll(field, 1, 0),
    )


def around_between(field, north_row, south_row):
    east, west, north, south = around(field)
    row = iota(field.shape, 0)
    return east, west, jnp.where(row == field.shape[0] - 1, north_row, north), jnp.where(row == 0, south_row, south)


def moved(load, near, levels, z):
    upper, lower = min(z + 1, levels - 1), max(z - 1, 0)
    results = []
    fields = [load(f * levels + z) for f in range(3)]
    tracer, across, along = fields
    around_tracer = near(z, tracer)
    east, west, north, south = around_tracer
    ddx, ddy = east - west, north - south
    extra = (0.5 * ADV * (across * ddx + along * ddy), 0.5 * PG * ddx, 0.5 * PG * ddy)
    for f, centre in enumerate(fields):
        sides = around_tracer if f == 0 else near(f * levels + z, centre)
        beside = KH * ((sides[0] + sides[1]) + (sides[2] + sides[3]))
        beyond = KZ * (load(f * levels + upper) + load(f * levels + lower))
        results.append((1.0 - 4.0 * KH - 2.0 * KZ) * centre + beside + (beyond - extra[f]))
    return results


def added(sign, along, tracer, across_near, along_near):
    return [
        (KH - sign * 0.5 * ADV * along) * tracer,
        KH * across_near,
        KH * along_near - sign * 0.5 * PG * tracer,
    ]


def begin_body(state_ref, wet_ref, west_ref, east_ref, tips_ref, mask_ref, begun_ref, packs_ref, token_ref, full_ref):
    planes, rows, cols = state_ref.shape
    levels = planes // 3
    west, east = west_ref[...], east_ref[...]
    for j in range(planes):
        tips_ref[j] = outer_rows(state_ref, j)
    for j in range(planes):
        full_ref[j, :, :cols] = state_ref[j]
        full_ref[j, :, cols:] = side_tile(west, EDGE * j, east, EDGE * j)
    mask_ref[:, :cols] = wet_ref[...].astype(jnp.float32)
    mask_ref[:, cols:] = side_tile(west, EDGE * planes, east, EDGE * planes)
    packs = [jnp.zeros((rows, LANES), jnp.float32) for _ in range(2)]
    for z in range(levels):
        values = moved(lambda j: full_ref[j], lambda j, field: around_between(field, 0.0, 0.0), levels, z)
        for f, value in enumerate(values):
            j = f * levels + z
            begun_ref[j] = value[:, :cols]
            packs[0] = packed(packs[0], value[:, cols:], LANES - EDGE, EDGE * j)
            packs[1] = packed(packs[1], value[:, cols:], 0, EDGE * j)
    packs_ref[0], packs_ref[1] = packs
    token_ref[...] = jnp.zeros_like(token_ref)


def outer_rows(ref, *index):
    rows, tile = ref.shape[len(index)], 2 * RIM
    first, last = ref[(*index, slice(0, tile))], ref[(*index, slice(rows - tile, rows))]
    return jnp.where(iota(first.shape, 0) < RIM, first, last)


def widened(plane, west, east, at):
    return jnp.concatenate([plane, side_tile(west, at, east, at)], axis=1)


def places(planes, sides):
    levels = planes // 3
    counts = [RIM] * levels + [EDGE] * (2 * levels) + [EDGE] * levels + [EDGE - 1] * levels + [EDGE] * (2 + (sides + 2) // 2)
    starts = [sum(counts[:k]) for k in range(len(counts))]
    return list(zip(starts, counts))


def outer_body(force_ref, edge_ref, tips_ref, mask_ref, west_ref, east_ref, *refs):
    sides, (up_ref, down_ref) = refs[:-2], refs[-2:]
    planes, rows, cols = force_ref.shape
    moving = 2 * planes // 3
    where = places(planes, len(sides))
    for out_ref, up in ((up_ref, True), (down_ref, False)):

        def put(place, ref, index, scale, lanes=slice(None)):
            start, count = where[place]
            at = slice(ref.shape[len(index)] - count, None) if up else slice(0, count)
            out_ref[start : start + count, lanes] = ref[(*index, at, slice(0, cols))] * scale

        out_ref[where[-1][0] :] = jnp.zeros((out_ref.shape[0] - where[-1][0], cols), jnp.float32)
        for j in range(planes):
            put(j, tips_ref, (j,), STATE_SCALE)
        for j in range(moving):
            put(planes + j, force_ref, (j,), FORCE_SCALE)
        put(planes + moving, mask_ref, (), STATE_SCALE)
        for k, part in enumerate((west_ref, east_ref, edge_ref, *sides)):
            lane = (k % 2) * LANES
            scale = STATE_SCALE if k < 2 else FORCE_SCALE
            put(planes + moving + 1 + k // 2, part, (), scale, slice(lane, lane + LANES))


def factors(mask, own, west, east, force_rows, push_ref):
    moving, total, wide = push_ref.shape
    cols = wide - LANES

    def counts(edge):
        return jnp.broadcast_to(edge[:, LANES - 1 :], (total, LANES))

    lane = iota((total, LANES), 1)
    count_side = jnp.where(lane < LANES // 2, counts(east), counts(west))
    relax = mask / (1.0 + GAMMA * jnp.concatenate([counts(own)] * (cols // LANES) + [count_side], axis=1))
    half = GAMMA * relax
    for j in range(moving):
        push_ref[j, :, :cols] = force_rows(j) * half[:, :cols]
        push_ref[j, :, cols:] = side_tile(west, EDGE * (moving + j), east, EDGE * j) * half[:, cols:]
    return relax


def finish(relax, push_ref, levels, values, z, at=(slice(None),)):
    tracer, across, along = values
    rated = relax[at]
    return (tracer * rated + push_ref[(z, *at)], across * rated, along * rated + push_ref[(levels + z, *at)])


def two_more(relax, push_ref, one_ref, two_ref, last, patched=lambda j, value: value):
    levels = one_ref.shape[0] // 3
    cols = one_ref.shape[2] - LANES
    for z in range(levels):
        values = moved(lambda j: one_ref[j], lambda j, field: around(field), levels, z)
        for f, value in enumerate(finish(relax, push_ref, levels, values, z)):
            two_ref[f * levels + z] = patched(f * levels + z, value)
    for z in range(levels):
        values = moved(
            lambda j: two_ref[j, :, :cols],
            lambda j, field: tuple(side[:, :cols] for side in around(two_ref[j])),
            levels,
            z,
        )
        last(z, finish(relax, push_ref, levels, values, z, (slice(None), slice(0, cols))))


def terms(values, stokes):
    rows, total = stokes.shape[0], values[0].shape[0]
    tracer = values[0]
    ddy = pltpu.roll(tracer, total - 1, 0)[:rows] - pltpu.roll(tracer, 1, 0)[:rows]
    return [values[2][:rows] * tracer[:rows], stokes * tracer[:rows], ddy]


def transports(sums, count, child, all_rows):
    raw = [jnp.sum(value, axis=1, keepdims=True) for value in sums]
    raw = [raw[0], raw[1] / (1.0 + count), raw[2] * (-0.5 * DISPERSE)]
    lane = iota(child.shape, 1)
    part = jnp.zeros(child.shape, jnp.float32)
    for q in range(3):
        part = part + jnp.where((child >= 0) & (lane == q * all_rows + child), raw[q], 0.0)
    return jnp.sum(part, axis=0, keepdims=True)


def inner_body(mask_ref, begun_ref, packs_ref, force_ref, edge_ref, *refs):
    side_refs, (middle_ref, ends_ref, part_ref, twos_ref, push_ref, one_ref, two_ref) = refs[:-7], refs[-7:]
    planes, rows, cols = begun_ref.shape
    levels = planes // 3
    moving = 2 * levels
    tile = 2 * RIM
    west, east = packs_ref[0], packs_ref[1]
    relax = factors(
        mask_ref[...], edge_ref[...], side_refs[0][...], side_refs[-1][...], lambda j: force_ref[j], push_ref
    )
    for z in range(levels):
        index = [f * levels + z for f in range(3)]
        values = [widened(begun_ref[j], west, east, EDGE * j) for j in index]
        for j, value in zip(index, finish(relax, push_ref, levels, values, z)):
            one_ref[j] = value
    sums = [jnp.zeros((rows, cols), jnp.float32) for _ in range(3)]

    def last(z, values):
        for f, value in enumerate(values):
            middle_ref[f, z] = value[tile : rows - tile]
            ends_ref[f, z, :tile] = value[:tile]
            ends_ref[f, z, tile:] = value[rows - tile :]
        for q, term in enumerate(terms(values, force_ref[moving + z])):
            sums[q] = sums[q] + term

    two_more(relax, push_ref, one_ref, two_ref, last)
    for j in range(planes):
        twos_ref[j] = outer_rows(two_ref, j)
    row = iota((rows, LANES), 0)
    child = jnp.where((row >= RIM) & (row < rows - RIM), row, -1)
    part_ref[...] = transports(sums, edge_ref[:, LANES - 1 :], child, rows)


def steps_body(
    sides, stokes_ref, tips_ref, west_ref, east_ref, mask_ref, begun_ref, packs_ref, force_ref, edge_ref, north_ref, south_ref, *refs
):
    middle_ref, ends_ref, part_ref, twos_ref = refs[:4]
    refs = refs[4:]
    side_refs = refs[:sides]
    held_ref, parts_ref, push_ref, halo_ref, one_ref, two_ref = refs[sides:]
    planes, rows, cols = begun_ref.shape
    wide = cols + LANES
    levels = planes // 3
    moving = 2 * levels
    tile = 2 * RIM
    total = 2 * tile

    where = places(planes, sides)

    def joined(place, scale):
        start, count = where[place]
        at = slice(start, start + count)
        parts = [north_ref[at], jnp.zeros((tile - 2 * count, cols), jnp.float32), south_ref[at]]
        return jnp.concatenate([part for part in parts if part.shape[0]], axis=0) * (1.0 / scale)

    def half_of(k, scale):
        lane = (k % 2) * LANES
        return joined(planes + moving + 1 + k // 2, scale)[:, lane : lane + LANES]

    beside = [half_of(k, STATE_SCALE) for k in range(2)]
    outer = [half_of(2 + k, FORCE_SCALE) for k in range(1 + sides)]
    edges = [jnp.concatenate([outer_rows(side), outer[1 + k]], axis=0) for k, side in enumerate(side_refs)]
    own = jnp.concatenate([outer_rows(edge_ref), outer[0]], axis=0)

    def halo(index, at):
        return widened(joined(index, STATE_SCALE), *beside, at)

    mask = jnp.concatenate([outer_rows(mask_ref), halo(planes + moving, EDGE * planes)], axis=0)
    relax = factors(
        mask,
        own,
        edges[0],
        edges[-1],
        lambda j: jnp.concatenate([outer_rows(force_ref, j), joined(planes + j, FORCE_SCALE)], axis=0),
        push_ref,
    )
    for j in range(planes):
        halo_ref[j] = halo(j, EDGE * j)
    row = iota((tile, wide), 0)
    packs = [outer_rows(packs_ref, k) for k in range(2)]
    wests, easts = outer_rows(west_ref), outer_rows(east_ref)

    def tip(j):
        return widened(tips_ref[j], wests, easts, EDGE * j)

    def begun(j):
        return widened(outer_rows(begun_ref, j), *packs, EDGE * j)

    def near(j, field):
        start = tip(j)
        return around_between(field, start[:1], start[tile - 1 :])

    for z in range(levels):
        index = [f * levels + z for f in range(3)]
        beyond = [halo_ref[j] for j in index]
        north = [jnp.where(row == tile - 1, value[:1], 0.0) for value in beyond]
        south = [jnp.where(row == 0, value[tile - 1 :], 0.0) for value in beyond]
        along = tip(index[2])
        extras = zip(added(-1.0, along, *south), added(1.0, along, *north))
        blocks = (
            [begun(j) + (first + final) for j, (first, final) in zip(index, extras)],
            moved(lambda j: halo_ref[j], near, levels, z),
        )
        for k, values in enumerate(blocks):
            at = slice(k * tile, (k + 1) * tile)
            for j, value in zip(index, finish(relax, push_ref, levels, values, z, (at,))):
                one_ref[j, at] = value

    meeting = (row == RIM - 1) | (row == RIM)

    def patched(j, value):
        return jnp.concatenate([jnp.where(meeting, twos_ref[j], value[:tile]), value[tile:]], axis=0)

    sums = [jnp.zeros((tile, cols), jnp.float32) for _ in range(3)]
    place = iota((tile, cols), 0)

    def last(z, values):
        finals = []
        for f, value in enumerate(values):
            ends = [ends_ref[f, z, :tile], ends_ref[f, z, tile:]]
            kept = jnp.where(place < RIM, *ends)
            final = jnp.where((place == RIM - 1) | (place == RIM), kept, value[:tile])
            held_ref[f, z, :tile] = jnp.where(place < RIM, final, ends[0])
            held_ref[f, z, tile:] = jnp.where(place < RIM, ends[1], final)
            finals.append(final)
        tracer = jnp.concatenate([finals[0], values[0][tile:]], axis=0)
        within = jnp.where(place < RIM, ends_ref[0, z, tile:], ends_ref[0, z, :tile])
        north = jnp.where(place == RIM - 1, pltpu.roll(within, tile - 1, 0), pltpu.roll(tracer, total - 1, 0)[:tile])
        south = jnp.where(place == RIM, pltpu.roll(within, 1, 0), pltpu.roll(tracer, 1, 0)[:tile])
        stokes = outer_rows(force_ref, moving + z)
        for q, term in enumerate((finals[2] * finals[0], stokes * finals[0], north - south)):
            sums[q] = sums[q] + term

    two_more(relax, push_ref, one_ref, two_ref, last, patched)
    beyond = jnp.zeros((rows, cols), jnp.float32)
    for z in range(levels):
        tracer = [held_ref[0, z, :tile], middle_ref[0, z], held_ref[0, z, tile:]]
        beyond = beyond + stokes_ref[:, z * cols : (z + 1) * cols] * jnp.concatenate(tracer, axis=0)
    beyond = jnp.sum(beyond, axis=1, keepdims=True) / (SUM_SCALE * (1.0 + edge_ref[:, LANES - 1 :]))
    row, lane = iota((rows, LANES), 0), iota((rows, LANES), 1)
    beyond = jnp.sum(jnp.where(lane == rows + row, beyond, 0.0), axis=0, keepdims=True)
    row = iota((tile, LANES), 0)
    child = jnp.where(row < RIM, row, row + rows - tile)
    part = transports(sums, own[:tile, LANES - 1 :], child, rows) + (part_ref[...] + beyond)
    parts_ref[...] = jnp.broadcast_to(part, parts_ref.shape)


def whole_body(middle_ref, ends_ref, state_ref, sent):
    rows = state_ref.shape[2]
    tile = ends_ref.shape[2] // 2
    copies = [
        pltpu.make_async_copy(source, state_ref.at[:, :, pl.ds(start, size)], sent.at[k])
        for k, (source, start, size) in enumerate(
            (
                (middle_ref, tile, rows - 2 * tile),
                (ends_ref.at[:, :, pl.ds(0, tile)], 0, tile),
                (ends_ref.at[:, :, pl.ds(tile, tile)], rows - tile, tile),
            )
        )
    ]
    for copy in copies:
        copy.start()
    for copy in copies:
        copy.wait()


def profile_body(across, along, parts_ref, out_ref):
    rows = out_ref.shape[1]
    parts = parts_ref[...]
    devices = parts.shape[0]
    total = parts
    for k in range(1, across):
        total = total + pltpu.roll(parts, devices - k, 0)
    row = iota(parts.shape, 0)
    squares = jnp.sum(jnp.where(row % across == 0, total * total, 0.0), keepdims=True)
    scale = jnp.sqrt(squares / (3 * rows * along) + 1e-06)
    mine = jnp.sum(jnp.where(row == lax.axis_index("gy") * across, total, 0.0), axis=0, keepdims=True) / scale
    for q in range(3):
        out_ref[q : q + 1, :] = mine[:, q * rows : (q + 1) * rows]


def per_device(state, parent_rows, dest, pick, offset, wet):
    fields, levels, rows, cols = state.shape
    planes = fields * levels
    moving = 2 * levels
    along, across = lax.axis_size("gy"), lax.axis_size("gx")
    capacity = 2 * SEND // along
    wide = cols + LANES
    f32 = jnp.float32
    even_pairs = [(i, i ^ 1) for i in range(along)]
    odd_pairs = [(i, ((i + 1) ^ 1) - 1) for i in range(1, along - 1)]
    swapped = [(0, 1), (1, 0)]
    eastward = [(i, i + 1) for i in range(across - 1)]
    westward = [(i + 1, i) for i in range(across - 1)]

    half = along // 2
    slots = half * capacity
    width = planes * cols + LANES
    halves = [list(range(half)), list(range(half, along))]

    def gathered(far):
        fetched = [pltpu.VMEM((1, SEND), jnp.int32)] * 3 + [pltpu.VMEM(parent_rows.shape, jnp.bfloat16)] if far else []
        return call(
            functools.partial(gather_body, capacity, slots, far),
            jax.ShapeDtypeStruct((slots, width), jnp.bfloat16),
            flops=2 * 8 * slots * SEND * planes * cols,
            moved=2 * (SEND + slots) * planes * cols,
            limit=VMEM_MOST,
            in_specs=[pl.BlockSpec(memory_space=pl.ANY if far else pltpu.VMEM)] * 4,
            out_specs=pl.BlockSpec(memory_space=pl.ANY),
            scratch_shapes=fetched
            + [
                pltpu.VMEM((slots, width), jnp.bfloat16),
                pltpu.SemaphoreType.DMA((4,)),
            ]
            + ([pltpu.SemaphoreType.DMA((4,))] if far else []),
        )(dest.reshape(1, SEND), pick.reshape(1, SEND), offset.reshape(1, SEND), parent_rows)

    def exchanged(payload):
        return lax.all_to_all(payload, "gy", split_axis=0, concat_axis=0, tiled=True, axis_index_groups=halves)

    far_rows = exchanged(gathered(True))

    cells = state.reshape(planes, rows, cols)
    packed_side = jax.ShapeDtypeStruct((rows, LANES), f32)
    first, last = call(sides_body, (packed_side, packed_side), moved=4 * planes * rows * cols)(cells, wet)
    if across == 2:
        west_one = lax.axis_index("gx") == 0
        other = lax.ppermute(jnp.where(west_one, last, first), "gx", swapped)
        from_west, from_east = jnp.where(west_one, 0.0, other), jnp.where(west_one, other, 0.0)
    else:
        from_west = lax.ppermute(last, "gx", eastward)
        from_east = lax.ppermute(first, "gx", westward)
    tips, mask, begun, packs, token = call(
        begin_body,
        (
            jax.ShapeDtypeStruct((planes, 2 * RIM, cols), f32),
            jax.ShapeDtypeStruct((rows, wide), f32),
            jax.ShapeDtypeStruct((planes, rows, cols), f32),
            jax.ShapeDtypeStruct((2, rows, LANES), f32),
            jax.ShapeDtypeStruct((8, LANES), f32),
        ),
        flops=20 * planes * rows * wide,
        moved=12 * planes * rows * wide,
        scratch_shapes=[pltpu.VMEM((planes, rows, wide), f32)],
    )(cells, wet, from_west, from_east)

    sums, stokes = call(
        far_body,
        (
            jax.ShapeDtypeStruct((rows, moving * cols + LANES), f32),
            jax.ShapeDtypeStruct((rows, (planes - moving) * cols), f32),
        ),
        flops=2 * rows * slots * width,
        moved=2 * slots * width + 4 * rows * width,
    )(token, far_rows)
    mirrored = [(i, (i + half) % along) for i in range(along)]
    sums, near_rows = lax.optimization_barrier((sums.astype(jnp.float16), gathered(False)))
    sums = lax.ppermute(sums, "gy", mirrored)
    arrived = exchanged(near_rows)
    stokes = lax.ppermute(stokes.astype(jnp.float16), "gy", mirrored)
    come = call(
        come_body,
        jax.ShapeDtypeStruct((8, LANES), f32),
        flops=10**11,
    )(sums[:8, :LANES].astype(f32))
    sums, arrived = lax.optimization_barrier((sums, arrived))
    sums = sums.astype(f32)

    force, edge = call(
        functools.partial(landing_body, planes, cols),
        (jax.ShapeDtypeStruct((planes, rows, cols), f32), packed_side),
        flops=2 * rows * slots * planes * cols,
        moved=2 * slots * planes * cols + 4 * rows * planes * cols,
    )(come, arrived, sums)
    if across == 2:
        sides = [lax.ppermute(edge, "gx", swapped)]
    else:
        sides = [lax.ppermute(edge, "gx", eastward), lax.ppermute(edge, "gx", westward)]
    start, count = places(planes, len(sides))[-1]
    outer = jax.ShapeDtypeStruct(((start + count + 7) // 8 * 8, cols), f32)
    up, down = call(outer_body, (outer, outer), moved=16 * (moving + planes) * RIM * cols)(
        force, edge, tips, mask, from_west, from_east, *sides
    )
    even = lax.axis_index("gy") % 2 == 0
    far = lax.ppermute(jnp.where(even, down, up).astype(jnp.float16), "gy", odd_pairs).astype(f32)
    near = lax.ppermute(jnp.where(even, up, down).astype(jnp.float16), "gy", even_pairs).astype(f32)
    above, below = jnp.where(even, near, far), jnp.where(even, far, near)
    tile = 2 * RIM
    middle, ends, part, twos = call(
        inner_body,
        (
            jax.ShapeDtypeStruct((fields, levels, rows - 2 * tile, cols), f32),
            jax.ShapeDtypeStruct((fields, levels, 2 * tile, cols), f32),
            jax.ShapeDtypeStruct((1, LANES), f32),
            jax.ShapeDtypeStruct((planes, tile, wide), f32),
        ),
        flops=60 * planes * rows * wide,
        moved=8 * planes * rows * wide,
        scratch_shapes=[
            pltpu.VMEM((moving, rows, wide), f32),
            pltpu.VMEM((planes, rows, wide), f32),
            pltpu.VMEM((planes, rows, wide), f32),
        ],
    )(mask, begun, packs, force, edge, *sides)
    stokes, part = lax.optimization_barrier((stokes, part))
    stokes = stokes.astype(f32)
    ends, parts = call(
        functools.partial(steps_body, len(sides)),
        (
            jax.ShapeDtypeStruct((fields, levels, 2 * tile, cols), f32),
            jax.ShapeDtypeStruct((along * across, LANES), f32),
        ),
        flops=60 * planes * 3 * tile * wide,
        moved=8 * planes * 3 * tile * wide,
        scratch_shapes=[
            pltpu.VMEM((moving, 2 * tile, wide), f32),
            pltpu.VMEM((planes, tile, wide), f32),
            pltpu.VMEM((planes, 2 * tile, wide), f32),
            pltpu.VMEM((planes, 2 * tile, wide), f32),
        ],
    )(stokes, tips, from_west, from_east, mask, begun, packs, force, edge, above, below, middle, ends, part, twos, *sides)
    new_state = call(
        whole_body,
        jax.ShapeDtypeStruct(state.shape, f32),
        moved=8 * planes * rows * cols,
        out_specs=pl.BlockSpec(memory_space=pl.ANY),
        scratch_shapes=[pltpu.SemaphoreType.DMA((3,))],
    )(middle, ends)
    every = lax.all_to_all(parts, ("gy", "gx"), split_axis=0, concat_axis=0, tiled=True)
    profile = call(functools.partial(profile_body, across, along), jax.ShapeDtypeStruct((3, rows), f32))(every)
    return new_state, profile


def solution(mesh):
    in_specs = (
        P(None, None, "gy", "gx"),
        P(("gy", "gx"), None, None),
        P(("gy", "gx"), None),
        P(("gy", "gx")),
        P(("gy", "gx")),
        P("gy", "gx"),
    )
    out_specs = (P(None, None, "gy", "gx"), P(None, "gy"))
    return jax.shard_map(
        per_device, mesh=mesh, in_specs=in_specs, out_specs=out_specs, check_vma=False
    )
```

```python
import functools

import jax
import jax.numpy as jnp
from jax import lax
from jax.experimental import pallas as pl
from jax.experimental.pallas import tpu as pltpu
from jax.sharding import PartitionSpec as P

SEND = 64
STEPS = 3

KH = 0.2
KZ = 0.05
ADV = 0.25
PG = 0.5
GAMMA = 0.5
DISPERSE = 2.0

EDGE = 3
RIM = 4
LANES = 128
STATE_SCALE = 8192.0
FORCE_SCALE = 64.0
SUM_SCALE = 128.0
VMEM_LIMIT = 16 * 1024 * 1024
VMEM_MOST = 60 * 1024 * 1024


def call(body, out_shape, flops=0, moved=0, limit=VMEM_LIMIT, **more):
    return pl.pallas_call(
        body,
        out_shape=out_shape,
        compiler_params=pltpu.CompilerParams(vmem_limit_bytes=limit),
        cost_estimate=pl.CostEstimate(flops=flops, bytes_accessed=moved, transcendentals=0),
        **more,
    )


def iota(shape, dim):
    return lax.broadcasted_iota(jnp.int32, shape, dim)


def gather_body(capacity, slots, far, *refs):
    if far:
        sources, out_ref, targets, held_ref, sent, copied = refs[:4], refs[4], refs[5:9], *refs[9:]
        copies = [
            pltpu.make_async_copy(source, target, copied.at[k])
            for k, (source, target) in enumerate(zip(sources, targets))
        ]
    else:
        targets, (out_ref, held_ref, sent), copies = refs[:4], refs[4:], []
    for copy in copies:
        copy.start()
    dest_ref, pick_ref, offset_ref, rows_ref = targets
    send, planes, cols = rows_ref.shape
    for copy in copies[:3]:
        copy.wait()
    dest = dest_ref[...]
    eye = iota((send, send), 0) == iota((send, send), 1)
    dest_column = jnp.sum(jnp.where(eye, dest, 0), axis=1, keepdims=True)
    earlier = (dest_column == dest) & (iota((send, send), 0) < iota((send, send), 1))
    rank = jnp.sum(earlier.astype(jnp.int32), axis=0, keepdims=True)
    half = slots // capacity
    mine = lax.axis_index("gy") >= half
    there = (dest >= half) != mine if far else (dest >= half) == mine
    slot_of = jnp.where(there, jnp.where(dest >= half, dest - half, dest) * capacity + rank, -1)
    taken = iota((slots, send), 0) == slot_of
    source = jnp.sum(jnp.where(taken, pick_ref[...] + 1, 0), axis=1, keepdims=True) - 1
    label = jnp.sum(jnp.where(taken, offset_ref[...] + 1, 0), axis=1, keepdims=True)
    group = 8
    lane = iota((slots, send * group), 1)
    select = jnp.concatenate(
        [(lane == source * group + j).astype(jnp.float32).astype(jnp.bfloat16) for j in range(group)], axis=0
    )
    width = planes * cols
    held_ref[:, width:] = jnp.broadcast_to(label, (slots, LANES)).astype(jnp.float32).astype(jnp.bfloat16)
    for copy in copies[3:]:
        copy.wait()
    parts = []

    def send_columns(start, size):
        part = pltpu.make_async_copy(
            held_ref.at[:, pl.ds(start, size)], out_ref.at[:, pl.ds(start, size)], sent.at[len(parts)]
        )
        part.start()
        parts.append(part)

    send_columns(width, LANES)
    for g in range(planes // group):
        block = rows_ref[:, g * group : (g + 1) * group, :].reshape(send * group, cols)
        got = jnp.dot(select, block, preferred_element_type=jnp.float32).astype(jnp.bfloat16)
        for j in range(group):
            at = (g * group + j) * cols
            held_ref[:, at : at + cols] = got[j * slots : (j + 1) * slots]
        send_columns(g * group * cols, group * cols)
    for part in parts:
        part.wait()


def landing_of(arrived_ref, rows):
    slots, width = arrived_ref.shape
    label = arrived_ref[:, width - LANES :].astype(jnp.float32)
    landing = (label == (iota((slots, LANES), 1) + 1).astype(jnp.float32)).astype(jnp.float32)
    return landing.T[:rows].astype(jnp.bfloat16)


def landed(landing, values):
    return jnp.dot(landing, values, preferred_element_type=jnp.float32)


def far_body(token_ref, arrived_ref, sums_ref, stokes_ref):
    rows, width = sums_ref.shape
    slots = arrived_ref.shape[0]
    landing = landing_of(arrived_ref, rows)
    moving, step = width - LANES, 2 * LANES
    for at in range(0, moving, step):
        sums_ref[:, at : at + step] = landed(landing, arrived_ref[:, at : at + step]) * SUM_SCALE
    sums_ref[:, moving:] = landed(landing, jnp.full((slots, LANES), SUM_SCALE, jnp.bfloat16))
    for at in range(0, stokes_ref.shape[1], step):
        there = slice(moving + at, moving + at + step)
        stokes_ref[:, at : at + step] = landed(landing, arrived_ref[:, there]) * SUM_SCALE


def come_body(sums_ref, token_ref):
    token_ref[...] = jnp.zeros_like(token_ref)


def landing_body(planes, cols, token_ref, arrived_ref, sums_ref, force_ref, edge_ref):
    slots = arrived_ref.shape[0]
    rows = force_ref.shape[1]
    landing = landing_of(arrived_ref, rows)
    far = 1.0 / SUM_SCALE
    moving = 2 * planes // 3
    count = landed(landing, jnp.ones((slots, LANES), jnp.bfloat16)) + sums_ref[:, moving * cols :] * far
    edge = count
    for j in range(planes):
        at = slice(j * cols, (j + 1) * cols)
        force = landed(landing, arrived_ref[:, at])
        if j < moving:
            force = force + sums_ref[:, at] * far
        force_ref[j] = force
        if j < moving:
            edge = packed(edge, force[:, :LANES], 0, EDGE * j)
            edge = packed(edge, force[:, cols - LANES :], LANES - EDGE, EDGE * (moving + j))
    edge_ref[...] = edge


def packed(into, tile, start, at):
    lane = iota(tile.shape, 1)
    shifted = pltpu.roll(tile, (at - start) % LANES, 1)
    return jnp.where((lane >= at) & (lane < at + EDGE), shifted, into)


def sides_body(state_ref, wet_ref, first_ref, last_ref):
    planes, rows, cols = state_ref.shape
    first = jnp.zeros((rows, LANES), jnp.float32)
    last = jnp.zeros((rows, LANES), jnp.float32)
    for j in range(planes + 1):
        own = state_ref[j] if j < planes else wet_ref[...].astype(jnp.float32)
        first = packed(first, own[:, :LANES], 0, EDGE * j)
        last = packed(last, own[:, cols - LANES :], LANES - EDGE, EDGE * j)
    first_ref[...] = first
    last_ref[...] = last


def side_tile(west, west_at, east, east_at):
    lane = iota(west.shape, 1)
    right = pltpu.roll(east, (LANES - east_at) % LANES, 1)
    left = pltpu.roll(west, (2 * LANES - EDGE - west_at) % LANES, 1)
    return jnp.where(lane < EDGE, right, jnp.where(lane >= LANES - EDGE, left, 0.0))


def around(field):
    rows, cols = field.shape
    return (
        pltpu.roll(field, cols - 1, 1),
        pltpu.roll(field, 1, 1),
        pltpu.roll(field, rows - 1, 0),
        pltpu.roll(field, 1, 0),
    )


def around_between(field, north_row, south_row):
    east, west, north, south = around(field)
    row = iota(field.shape, 0)
    return east, west, jnp.where(row == field.shape[0] - 1, north_row, north), jnp.where(row == 0, south_row, south)


def moved(load, near, levels, z):
    upper, lower = min(z + 1, levels - 1), max(z - 1, 0)
    results = []
    fields = [load(f * levels + z) for f in range(3)]
    tracer, across, along = fields
    around_tracer = near(z, tracer)
    east, west, north, south = around_tracer
    ddx, ddy = east - west, north - south
    extra = (0.5 * ADV * (across * ddx + along * ddy), 0.5 * PG * ddx, 0.5 * PG * ddy)
    for f, centre in enumerate(fields):
        sides = around_tracer if f == 0 else near(f * levels + z, centre)
        beside = KH * ((sides[0] + sides[1]) + (sides[2] + sides[3]))
        beyond = KZ * (load(f * levels + upper) + load(f * levels + lower))
        results.append((1.0 - 4.0 * KH - 2.0 * KZ) * centre + beside + (beyond - extra[f]))
    return results


def added(sign, along, tracer, across_near, along_near):
    return [
        (KH - sign * 0.5 * ADV * along) * tracer,
        KH * across_near,
        KH * along_near - sign * 0.5 * PG * tracer,
    ]


def begin_body(state_ref, wet_ref, west_ref, east_ref, tips_ref, mask_ref, begun_ref, packs_ref, token_ref, full_ref):
    planes, rows, cols = state_ref.shape
    levels = planes // 3
    west, east = west_ref[...], east_ref[...]
    for j in range(planes):
        tips_ref[j] = outer_rows(state_ref, j)
    for j in range(planes):
        full_ref[j, :, :cols] = state_ref[j]
        full_ref[j, :, cols:] = side_tile(west, EDGE * j, east, EDGE * j)
    mask_ref[:, :cols] = wet_ref[...].astype(jnp.float32)
    mask_ref[:, cols:] = side_tile(west, EDGE * planes, east, EDGE * planes)
    packs = [jnp.zeros((rows, LANES), jnp.float32) for _ in range(2)]
    for z in range(levels):
        values = moved(lambda j: full_ref[j], lambda j, field: around_between(field, 0.0, 0.0), levels, z)
        for f, value in enumerate(values):
            j = f * levels + z
            begun_ref[j] = value[:, :cols]
            packs[0] = packed(packs[0], value[:, cols:], LANES - EDGE, EDGE * j)
            packs[1] = packed(packs[1], value[:, cols:], 0, EDGE * j)
    packs_ref[0], packs_ref[1] = packs
    token_ref[...] = jnp.zeros_like(token_ref)


def outer_rows(ref, *index):
    rows, tile = ref.shape[len(index)], 2 * RIM
    first, last = ref[(*index, slice(0, tile))], ref[(*index, slice(rows - tile, rows))]
    return jnp.where(iota(first.shape, 0) < RIM, first, last)


def widened(plane, west, east, at):
    return jnp.concatenate([plane, side_tile(west, at, east, at)], axis=1)


def places(planes, sides):
    levels = planes // 3
    counts = [RIM] * levels + [EDGE] * (2 * levels) + [EDGE] * levels + [EDGE - 1] * levels + [EDGE] * (2 + (sides + 2) // 2)
    starts = [sum(counts[:k]) for k in range(len(counts))]
    return list(zip(starts, counts))


def outer_body(force_ref, edge_ref, tips_ref, mask_ref, west_ref, east_ref, *refs):
    sides, (up_ref, down_ref) = refs[:-2], refs[-2:]
    planes, rows, cols = force_ref.shape
    moving = 2 * planes // 3
    where = places(planes, len(sides))
    for out_ref, up in ((up_ref, True), (down_ref, False)):

        def put(place, ref, index, scale, lanes=slice(None)):
            start, count = where[place]
            at = slice(ref.shape[len(index)] - count, None) if up else slice(0, count)
            out_ref[start : start + count, lanes] = ref[(*index, at, slice(0, cols))] * scale

        out_ref[where[-1][0] :] = jnp.zeros((out_ref.shape[0] - where[-1][0], cols), jnp.float32)
        for j in range(planes):
            put(j, tips_ref, (j,), STATE_SCALE)
        for j in range(moving):
            put(planes + j, force_ref, (j,), FORCE_SCALE)
        put(planes + moving, mask_ref, (), STATE_SCALE)
        for k, part in enumerate((west_ref, east_ref, edge_ref, *sides)):
            lane = (k % 2) * LANES
            scale = STATE_SCALE if k < 2 else FORCE_SCALE
            put(planes + moving + 1 + k // 2, part, (), scale, slice(lane, lane + LANES))


def factors(mask, own, west, east, force_rows, push_ref):
    moving, total, wide = push_ref.shape
    cols = wide - LANES

    def counts(edge):
        return jnp.broadcast_to(edge[:, LANES - 1 :], (total, LANES))

    lane = iota((total, LANES), 1)
    count_side = jnp.where(lane < LANES // 2, counts(east), counts(west))
    relax = mask / (1.0 + GAMMA * jnp.concatenate([counts(own)] * (cols // LANES) + [count_side], axis=1))
    half = GAMMA * relax
    for j in range(moving):
        push_ref[j, :, :cols] = force_rows(j) * half[:, :cols]
        push_ref[j, :, cols:] = side_tile(west, EDGE * (moving + j), east, EDGE * j) * half[:, cols:]
    return relax


def finish(relax, push_ref, levels, values, z, at=(slice(None),)):
    tracer, across, along = values
    rated = relax[at]
    return (tracer * rated + push_ref[(z, *at)], across * rated, along * rated + push_ref[(levels + z, *at)])


def two_more(relax, push_ref, one_ref, two_ref, last, patched=lambda j, value: value):
    levels = one_ref.shape[0] // 3
    cols = one_ref.shape[2] - LANES
    for z in range(levels):
        values = moved(lambda j: one_ref[j], lambda j, field: around(field), levels, z)
        for f, value in enumerate(finish(relax, push_ref, levels, values, z)):
            two_ref[f * levels + z] = patched(f * levels + z, value)
    for z in range(levels):
        values = moved(
            lambda j: two_ref[j, :, :cols],
            lambda j, field: tuple(side[:, :cols] for side in around(two_ref[j])),
            levels,
            z,
        )
        last(z, finish(relax, push_ref, levels, values, z, (slice(None), slice(0, cols))))


def terms(values, stokes):
    rows, total = stokes.shape[0], values[0].shape[0]
    tracer = values[0]
    ddy = pltpu.roll(tracer, total - 1, 0)[:rows] - pltpu.roll(tracer, 1, 0)[:rows]
    return [values[2][:rows] * tracer[:rows], stokes * tracer[:rows], ddy]


def transports(sums, count, child, all_rows):
    raw = [jnp.sum(value, axis=1, keepdims=True) for value in sums]
    raw = [raw[0], raw[1] / (1.0 + count), raw[2] * (-0.5 * DISPERSE)]
    lane = iota(child.shape, 1)
    part = jnp.zeros(child.shape, jnp.float32)
    for q in range(3):
        part = part + jnp.where((child >= 0) & (lane == q * all_rows + child), raw[q], 0.0)
    return jnp.sum(part, axis=0, keepdims=True)


def inner_body(mask_ref, begun_ref, packs_ref, force_ref, edge_ref, *refs):
    side_refs, (middle_ref, ends_ref, part_ref, twos_ref, push_ref, one_ref, two_ref) = refs[:-7], refs[-7:]
    planes, rows, cols = begun_ref.shape
    levels = planes // 3
    moving = 2 * levels
    tile = 2 * RIM
    west, east = packs_ref[0], packs_ref[1]
    relax = factors(
        mask_ref[...], edge_ref[...], side_refs[0][...], side_refs[-1][...], lambda j: force_ref[j], push_ref
    )
    for z in range(levels):
        index = [f * levels + z for f in range(3)]
        values = [widened(begun_ref[j], west, east, EDGE * j) for j in index]
        for j, value in zip(index, finish(relax, push_ref, levels, values, z)):
            one_ref[j] = value
    sums = [jnp.zeros((rows, cols), jnp.float32) for _ in range(3)]

    def last(z, values):
        for f, value in enumerate(values):
            middle_ref[f, z] = value[tile : rows - tile]
            ends_ref[f, z, :tile] = value[:tile]
            ends_ref[f, z, tile:] = value[rows - tile :]
        for q, term in enumerate(terms(values, force_ref[moving + z])):
            sums[q] = sums[q] + term

    two_more(relax, push_ref, one_ref, two_ref, last)
    for j in range(planes):
        twos_ref[j] = outer_rows(two_ref, j)
    row = iota((rows, LANES), 0)
    child = jnp.where((row >= RIM) & (row < rows - RIM), row, -1)
    part_ref[...] = transports(sums, edge_ref[:, LANES - 1 :], child, rows)


def steps_body(
    sides, stokes_ref, tips_ref, west_ref, east_ref, mask_ref, begun_ref, packs_ref, force_ref, edge_ref, north_ref, south_ref, *refs
):
    middle_ref, ends_ref, part_ref, twos_ref = refs[:4]
    refs = refs[4:]
    side_refs = refs[:sides]
    held_ref, parts_ref, push_ref, halo_ref, one_ref, two_ref = refs[sides:]
    planes, rows, cols = begun_ref.shape
    wide = cols + LANES
    levels = planes // 3
    moving = 2 * levels
    tile = 2 * RIM
    total = 2 * tile

    where = places(planes, sides)

    def joined(place, scale):
        start, count = where[place]
        at = slice(start, start + count)
        parts = [north_ref[at], jnp.zeros((tile - 2 * count, cols), jnp.float32), south_ref[at]]
        return jnp.concatenate([part for part in parts if part.shape[0]], axis=0) * (1.0 / scale)

    def half_of(k, scale):
        lane = (k % 2) * LANES
        return joined(planes + moving + 1 + k // 2, scale)[:, lane : lane + LANES]

    beside = [half_of(k, STATE_SCALE) for k in range(2)]
    outer = [half_of(2 + k, FORCE_SCALE) for k in range(1 + sides)]
    edges = [jnp.concatenate([outer_rows(side), outer[1 + k]], axis=0) for k, side in enumerate(side_refs)]
    own = jnp.concatenate([outer_rows(edge_ref), outer[0]], axis=0)

    def halo(index, at):
        return widened(joined(index, STATE_SCALE), *beside, at)

    mask = jnp.concatenate([outer_rows(mask_ref), halo(planes + moving, EDGE * planes)], axis=0)
    relax = factors(
        mask,
        own,
        edges[0],
        edges[-1],
        lambda j: jnp.concatenate([outer_rows(force_ref, j), joined(planes + j, FORCE_SCALE)], axis=0),
        push_ref,
    )
    for j in range(planes):
        halo_ref[j] = halo(j, EDGE * j)
    row = iota((tile, wide), 0)
    packs = [outer_rows(packs_ref, k) for k in range(2)]
    wests, easts = outer_rows(west_ref), outer_rows(east_ref)

    def tip(j):
        return widened(tips_ref[j], wests, easts, EDGE * j)

    def begun(j):
        return widened(outer_rows(begun_ref, j), *packs, EDGE * j)

    def near(j, field):
        start = tip(j)
        return around_between(field, start[:1], start[tile - 1 :])

    for z in range(levels):
        index = [f * levels + z for f in range(3)]
        beyond = [halo_ref[j] for j in index]
        north = [jnp.where(row == tile - 1, value[:1], 0.0) for value in beyond]
        south = [jnp.where(row == 0, value[tile - 1 :], 0.0) for value in beyond]
        along = tip(index[2])
        extras = zip(added(-1.0, along, *south), added(1.0, along, *north))
        blocks = (
            [begun(j) + (first + final) for j, (first, final) in zip(index, extras)],
            moved(lambda j: halo_ref[j], near, levels, z),
        )
        for k, values in enumerate(blocks):
            at = slice(k * tile, (k + 1) * tile)
            for j, value in zip(index, finish(relax, push_ref, levels, values, z, (at,))):
                one_ref[j, at] = value

    meeting = (row == RIM - 1) | (row == RIM)

    def patched(j, value):
        return jnp.concatenate([jnp.where(meeting, twos_ref[j], value[:tile]), value[tile:]], axis=0)

    sums = [jnp.zeros((tile, cols), jnp.float32) for _ in range(3)]
    place = iota((tile, cols), 0)

    def last(z, values):
        finals = []
        for f, value in enumerate(values):
            ends = [ends_ref[f, z, :tile], ends_ref[f, z, tile:]]
            kept = jnp.where(place < RIM, *ends)
            final = jnp.where((place == RIM - 1) | (place == RIM), kept, value[:tile])
            held_ref[f, z, :tile] = jnp.where(place < RIM, final, ends[0])
            held_ref[f, z, tile:] = jnp.where(place < RIM, ends[1], final)
            finals.append(final)
        tracer = jnp.concatenate([finals[0], values[0][tile:]], axis=0)
        within = jnp.where(place < RIM, ends_ref[0, z, tile:], ends_ref[0, z, :tile])
        north = jnp.where(place == RIM - 1, pltpu.roll(within, tile - 1, 0), pltpu.roll(tracer, total - 1, 0)[:tile])
        south = jnp.where(place == RIM, pltpu.roll(within, 1, 0), pltpu.roll(tracer, 1, 0)[:tile])
        stokes = outer_rows(force_ref, moving + z)
        for q, term in enumerate((finals[2] * finals[0], stokes * finals[0], north - south)):
            sums[q] = sums[q] + term

    two_more(relax, push_ref, one_ref, two_ref, last, patched)
    beyond = jnp.zeros((rows, cols), jnp.float32)
    for z in range(levels):
        tracer = [held_ref[0, z, :tile], middle_ref[0, z], held_ref[0, z, tile:]]
        beyond = beyond + stokes_ref[:, z * cols : (z + 1) * cols] * jnp.concatenate(tracer, axis=0)
    beyond = jnp.sum(beyond, axis=1, keepdims=True) / (SUM_SCALE * (1.0 + edge_ref[:, LANES - 1 :]))
    row, lane = iota((rows, LANES), 0), iota((rows, LANES), 1)
    beyond = jnp.sum(jnp.where(lane == rows + row, beyond, 0.0), axis=0, keepdims=True)
    row = iota((tile, LANES), 0)
    child = jnp.where(row < RIM, row, row + rows - tile)
    part = transports(sums, own[:tile, LANES - 1 :], child, rows) + (part_ref[...] + beyond)
    parts_ref[...] = jnp.broadcast_to(part, parts_ref.shape)


def whole_body(middle_ref, ends_ref, state_ref, sent):
    rows = state_ref.shape[2]
    tile = ends_ref.shape[2] // 2
    copies = [
        pltpu.make_async_copy(source, state_ref.at[:, :, pl.ds(start, size)], sent.at[k])
        for k, (source, start, size) in enumerate(
            (
                (middle_ref, tile, rows - 2 * tile),
                (ends_ref.at[:, :, pl.ds(0, tile)], 0, tile),
                (ends_ref.at[:, :, pl.ds(tile, tile)], rows - tile, tile),
            )
        )
    ]
    for copy in copies:
        copy.start()
    for copy in copies:
        copy.wait()


def profile_body(across, along, parts_ref, out_ref):
    rows = out_ref.shape[1]
    parts = parts_ref[...]
    devices = parts.shape[0]
    total = parts
    for k in range(1, across):
        total = total + pltpu.roll(parts, devices - k, 0)
    row = iota(parts.shape, 0)
    squares = jnp.sum(jnp.where(row % across == 0, total * total, 0.0), keepdims=True)
    scale = jnp.sqrt(squares / (3 * rows * along) + 1e-06)
    mine = jnp.sum(jnp.where(row == lax.axis_index("gy") * across, total, 0.0), axis=0, keepdims=True) / scale
    for q in range(3):
        out_ref[q : q + 1, :] = mine[:, q * rows : (q + 1) * rows]


def per_device(state, parent_rows, dest, pick, offset, wet):
    fields, levels, rows, cols = state.shape
    planes = fields * levels
    moving = 2 * levels
    along, across = lax.axis_size("gy"), lax.axis_size("gx")
    capacity = 2 * SEND // along
    wide = cols + LANES
    f32 = jnp.float32
    even_pairs = [(i, i ^ 1) for i in range(along)]
    odd_pairs = [(i, ((i + 1) ^ 1) - 1) for i in range(1, along - 1)]
    swapped = [(0, 1), (1, 0)]
    eastward = [(i, i + 1) for i in range(across - 1)]
    westward = [(i + 1, i) for i in range(across - 1)]

    half = along // 2
    slots = half * capacity
    width = planes * cols + LANES
    halves = [list(range(half)), list(range(half, along))]

    def gathered(far):
        fetched = [pltpu.VMEM((1, SEND), jnp.int32)] * 3 + [pltpu.VMEM(parent_rows.shape, jnp.bfloat16)] if far else []
        return call(
            functools.partial(gather_body, capacity, slots, far),
            jax.ShapeDtypeStruct((slots, width), jnp.bfloat16),
            flops=2 * 8 * slots * SEND * planes * cols,
            moved=2 * (SEND + slots) * planes * cols,
            limit=VMEM_MOST,
            in_specs=[pl.BlockSpec(memory_space=pl.ANY if far else pltpu.VMEM)] * 4,
            out_specs=pl.BlockSpec(memory_space=pl.ANY),
            scratch_shapes=fetched
            + [
                pltpu.VMEM((slots, width), jnp.bfloat16),
                pltpu.SemaphoreType.DMA((4,)),
            ]
            + ([pltpu.SemaphoreType.DMA((4,))] if far else []),
        )(dest.reshape(1, SEND), pick.reshape(1, SEND), offset.reshape(1, SEND), parent_rows)

    def exchanged(payload):
        return lax.all_to_all(payload, "gy", split_axis=0, concat_axis=0, tiled=True, axis_index_groups=halves)

    far_rows = exchanged(gathered(True))

    cells = state.reshape(planes, rows, cols)
    packed_side = jax.ShapeDtypeStruct((rows, LANES), f32)
    first, last = call(sides_body, (packed_side, packed_side), moved=4 * planes * rows * cols)(cells, wet)
    if across == 2:
        west_one = lax.axis_index("gx") == 0
        other = lax.ppermute(jnp.where(west_one, last, first), "gx", swapped)
        from_west, from_east = jnp.where(west_one, 0.0, other), jnp.where(west_one, other, 0.0)
    else:
        from_west = lax.ppermute(last, "gx", eastward)
        from_east = lax.ppermute(first, "gx", westward)
    tips, mask, begun, packs, token = call(
        begin_body,
        (
            jax.ShapeDtypeStruct((planes, 2 * RIM, cols), f32),
            jax.ShapeDtypeStruct((rows, wide), f32),
            jax.ShapeDtypeStruct((planes, rows, cols), f32),
            jax.ShapeDtypeStruct((2, rows, LANES), f32),
            jax.ShapeDtypeStruct((8, LANES), f32),
        ),
        flops=20 * planes * rows * wide,
        moved=12 * planes * rows * wide,
        scratch_shapes=[pltpu.VMEM((planes, rows, wide), f32)],
    )(cells, wet, from_west, from_east)

    sums, stokes = call(
        far_body,
        (
            jax.ShapeDtypeStruct((rows, moving * cols + LANES), f32),
            jax.ShapeDtypeStruct((rows, (planes - moving) * cols), f32),
        ),
        flops=2 * rows * slots * width,
        moved=2 * slots * width + 4 * rows * width,
    )(token, far_rows)
    mirrored = [(i, (i + half) % along) for i in range(along)]
    halved = (sums.astype(jnp.float16), stokes.astype(jnp.float16), gathered(False))
    sums, stokes, near_rows = lax.optimization_barrier(halved)
    sums = lax.ppermute(sums, "gy", mirrored)
    arrived = exchanged(near_rows)
    stokes = lax.ppermute(stokes, "gy", mirrored)
    come = call(
        come_body,
        jax.ShapeDtypeStruct((8, LANES), f32),
        flops=10**11,
    )(sums[:8, :LANES].astype(f32))
    sums, arrived = lax.optimization_barrier((sums, arrived))
    sums = sums.astype(f32)

    force, edge = call(
        functools.partial(landing_body, planes, cols),
        (jax.ShapeDtypeStruct((planes, rows, cols), f32), packed_side),
        flops=2 * rows * slots * planes * cols,
        moved=2 * slots * planes * cols + 4 * rows * planes * cols,
    )(come, arrived, sums)
    if across == 2:
        sides = [lax.ppermute(edge, "gx", swapped)]
    else:
        sides = [lax.ppermute(edge, "gx", eastward), lax.ppermute(edge, "gx", westward)]
    start, count = places(planes, len(sides))[-1]
    outer = jax.ShapeDtypeStruct(((start + count + 7) // 8 * 8, cols), f32)
    up, down = call(outer_body, (outer, outer), moved=16 * (moving + planes) * RIM * cols)(
        force, edge, tips, mask, from_west, from_east, *sides
    )
    even = lax.axis_index("gy") % 2 == 0
    far = lax.ppermute(jnp.where(even, down, up).astype(jnp.float16), "gy", odd_pairs).astype(f32)
    near = lax.ppermute(jnp.where(even, up, down).astype(jnp.float16), "gy", even_pairs).astype(f32)
    above, below = jnp.where(even, near, far), jnp.where(even, far, near)
    tile = 2 * RIM
    middle, ends, part, twos = call(
        inner_body,
        (
            jax.ShapeDtypeStruct((fields, levels, rows - 2 * tile, cols), f32),
            jax.ShapeDtypeStruct((fields, levels, 2 * tile, cols), f32),
            jax.ShapeDtypeStruct((1, LANES), f32),
            jax.ShapeDtypeStruct((planes, tile, wide), f32),
        ),
        flops=60 * planes * rows * wide,
        moved=8 * planes * rows * wide,
        scratch_shapes=[
            pltpu.VMEM((moving, rows, wide), f32),
            pltpu.VMEM((planes, rows, wide), f32),
            pltpu.VMEM((planes, rows, wide), f32),
        ],
    )(mask, begun, packs, force, edge, *sides)
    stokes, part = lax.optimization_barrier((stokes, part))
    stokes = stokes.astype(f32)
    ends, parts = call(
        functools.partial(steps_body, len(sides)),
        (
            jax.ShapeDtypeStruct((fields, levels, 2 * tile, cols), f32),
            jax.ShapeDtypeStruct((along * across, LANES), f32),
        ),
        flops=60 * planes * 3 * tile * wide,
        moved=8 * planes * 3 * tile * wide,
        scratch_shapes=[
            pltpu.VMEM((moving, 2 * tile, wide), f32),
            pltpu.VMEM((planes, tile, wide), f32),
            pltpu.VMEM((planes, 2 * tile, wide), f32),
            pltpu.VMEM((planes, 2 * tile, wide), f32),
        ],
    )(stokes, tips, from_west, from_east, mask, begun, packs, force, edge, above, below, middle, ends, part, twos, *sides)
    new_state = call(
        whole_body,
        jax.ShapeDtypeStruct(state.shape, f32),
        moved=8 * planes * rows * cols,
        out_specs=pl.BlockSpec(memory_space=pl.ANY),
        scratch_shapes=[pltpu.SemaphoreType.DMA((3,))],
    )(middle, ends)
    every = lax.all_to_all(parts, ("gy", "gx"), split_axis=0, concat_axis=0, tiled=True)
    profile = call(functools.partial(profile_body, across, along), jax.ShapeDtypeStruct((3, rows), f32))(every)
    return new_state, profile


def solution(mesh):
    in_specs = (
        P(None, None, "gy", "gx"),
        P(("gy", "gx"), None, None),
        P(("gy", "gx"), None),
        P(("gy", "gx")),
        P(("gy", "gx")),
        P("gy", "gx"),
    )
    out_specs = (P(None, None, "gy", "gx"), P(None, "gy"))
    return jax.shard_map(
        per_device, mesh=mesh, in_specs=in_specs, out_specs=out_specs, check_vma=False
    )
```

```python
import functools

import jax
import jax.numpy as jnp
from jax import lax
from jax.experimental import pallas as pl
from jax.experimental.pallas import tpu as pltpu
from jax.sharding import PartitionSpec as P

SEND = 64
STEPS = 3

KH = 0.2
KZ = 0.05
ADV = 0.25
PG = 0.5
GAMMA = 0.5
DISPERSE = 2.0

EDGE = 3
RIM = 4
LANES = 128
STATE_SCALE = 8192.0
FORCE_SCALE = 64.0
SUM_SCALE = 128.0
VMEM_LIMIT = 16 * 1024 * 1024
VMEM_MOST = 60 * 1024 * 1024


def call(body, out_shape, flops=0, moved=0, limit=VMEM_LIMIT, **more):
    return pl.pallas_call(
        body,
        out_shape=out_shape,
        compiler_params=pltpu.CompilerParams(vmem_limit_bytes=limit),
        cost_estimate=pl.CostEstimate(flops=flops, bytes_accessed=moved, transcendentals=0),
        **more,
    )


def iota(shape, dim):
    return lax.broadcasted_iota(jnp.int32, shape, dim)


def gather_body(capacity, slots, far, *refs):
    if far:
        sources, out_ref, targets, held_ref, sent, copied = refs[:4], refs[4], refs[5:9], *refs[9:]
        copies = [
            pltpu.make_async_copy(source, target, copied.at[k])
            for k, (source, target) in enumerate(zip(sources, targets))
        ]
    else:
        targets, (out_ref, held_ref, sent), copies = refs[:4], refs[4:], []
    for copy in copies:
        copy.start()
    dest_ref, pick_ref, offset_ref, rows_ref = targets
    send, planes, cols = rows_ref.shape
    for copy in copies[:3]:
        copy.wait()
    dest = dest_ref[...]
    eye = iota((send, send), 0) == iota((send, send), 1)
    dest_column = jnp.sum(jnp.where(eye, dest, 0), axis=1, keepdims=True)
    earlier = (dest_column == dest) & (iota((send, send), 0) < iota((send, send), 1))
    rank = jnp.sum(earlier.astype(jnp.int32), axis=0, keepdims=True)
    half = slots // capacity
    mine = lax.axis_index("gy") >= half
    there = (dest >= half) != mine if far else (dest >= half) == mine
    slot_of = jnp.where(there, jnp.where(dest >= half, dest - half, dest) * capacity + rank, -1)
    taken = iota((slots, send), 0) == slot_of
    source = jnp.sum(jnp.where(taken, pick_ref[...] + 1, 0), axis=1, keepdims=True) - 1
    label = jnp.sum(jnp.where(taken, offset_ref[...] + 1, 0), axis=1, keepdims=True)
    group = 8
    lane = iota((slots, send * group), 1)
    select = jnp.concatenate(
        [(lane == source * group + j).astype(jnp.float32).astype(jnp.bfloat16) for j in range(group)], axis=0
    )
    width = planes * cols
    held_ref[:, width:] = jnp.broadcast_to(label, (slots, LANES)).astype(jnp.float32).astype(jnp.bfloat16)
    for copy in copies[3:]:
        copy.wait()
    parts = []

    def send_columns(start, size):
        part = pltpu.make_async_copy(
            held_ref.at[:, pl.ds(start, size)], out_ref.at[:, pl.ds(start, size)], sent.at[len(parts)]
        )
        part.start()
        parts.append(part)

    send_columns(width, LANES)
    for g in range(planes // group):
        block = rows_ref[:, g * group : (g + 1) * group, :].reshape(send * group, cols)
        got = jnp.dot(select, block, preferred_element_type=jnp.float32).astype(jnp.bfloat16)
        for j in range(group):
            at = (g * group + j) * cols
            held_ref[:, at : at + cols] = got[j * slots : (j + 1) * slots]
        send_columns(g * group * cols, group * cols)
    for part in parts:
        part.wait()


def landing_of(arrived_ref, rows):
    slots, width = arrived_ref.shape
    label = arrived_ref[:, width - LANES :].astype(jnp.float32)
    landing = (label == (iota((slots, LANES), 1) + 1).astype(jnp.float32)).astype(jnp.float32)
    return landing.T[:rows].astype(jnp.bfloat16)


def landed(landing, values):
    return jnp.dot(landing, values, preferred_element_type=jnp.float32)


def far_body(token_ref, arrived_ref, sums_ref, stokes_ref):
    rows, width = sums_ref.shape
    slots = arrived_ref.shape[0]
    landing = landing_of(arrived_ref, rows)
    moving, step = width - LANES, 2 * LANES
    for at in range(0, moving, step):
        sums_ref[:, at : at + step] = landed(landing, arrived_ref[:, at : at + step]) * SUM_SCALE
    sums_ref[:, moving:] = landed(landing, jnp.full((slots, LANES), SUM_SCALE, jnp.bfloat16))
    for at in range(0, stokes_ref.shape[1], step):
        there = slice(moving + at, moving + at + step)
        stokes_ref[:, at : at + step] = landed(landing, arrived_ref[:, there]) * SUM_SCALE


def come_body(sums_ref, token_ref):
    token_ref[...] = jnp.zeros_like(token_ref)


def landing_body(planes, cols, token_ref, arrived_ref, sums_ref, force_ref, edge_ref):
    slots = arrived_ref.shape[0]
    rows = force_ref.shape[1]
    landing = landing_of(arrived_ref, rows)
    far = 1.0 / SUM_SCALE
    moving = 2 * planes // 3
    count = landed(landing, jnp.ones((slots, LANES), jnp.bfloat16)) + sums_ref[:, moving * cols :] * far
    edge = count
    for j in range(planes):
        at = slice(j * cols, (j + 1) * cols)
        force = landed(landing, arrived_ref[:, at])
        if j < moving:
            force = force + sums_ref[:, at] * far
        force_ref[j] = force
        if j < moving:
            edge = packed(edge, force[:, :LANES], 0, EDGE * j)
            edge = packed(edge, force[:, cols - LANES :], LANES - EDGE, EDGE * (moving + j))
    edge_ref[...] = edge


def packed(into, tile, start, at):
    lane = iota(tile.shape, 1)
    shifted = pltpu.roll(tile, (at - start) % LANES, 1)
    return jnp.where((lane >= at) & (lane < at + EDGE), shifted, into)


def sides_body(state_ref, wet_ref, first_ref, last_ref):
    planes, rows, cols = state_ref.shape
    first = jnp.zeros((rows, LANES), jnp.float32)
    last = jnp.zeros((rows, LANES), jnp.float32)
    for j in range(planes + 1):
        own = state_ref[j] if j < planes else wet_ref[...].astype(jnp.float32)
        first = packed(first, own[:, :LANES], 0, EDGE * j)
        last = packed(last, own[:, cols - LANES :], LANES - EDGE, EDGE * j)
    first_ref[...] = first
    last_ref[...] = last


def side_tile(west, west_at, east, east_at):
    lane = iota(west.shape, 1)
    right = pltpu.roll(east, (LANES - east_at) % LANES, 1)
    left = pltpu.roll(west, (2 * LANES - EDGE - west_at) % LANES, 1)
    return jnp.where(lane < EDGE, right, jnp.where(lane >= LANES - EDGE, left, 0.0))


def around(field):
    rows, cols = field.shape
    return (
        pltpu.roll(field, cols - 1, 1),
        pltpu.roll(field, 1, 1),
        pltpu.roll(field, rows - 1, 0),
        pltpu.roll(field, 1, 0),
    )


def around_between(field, north_row, south_row):
    east, west, north, south = around(field)
    row = iota(field.shape, 0)
    return east, west, jnp.where(row == field.shape[0] - 1, north_row, north), jnp.where(row == 0, south_row, south)


def moved(load, near, levels, z):
    upper, lower = min(z + 1, levels - 1), max(z - 1, 0)
    results = []
    fields = [load(f * levels + z) for f in range(3)]
    tracer, across, along = fields
    around_tracer = near(z, tracer)
    east, west, north, south = around_tracer
    ddx, ddy = east - west, north - south
    extra = (0.5 * ADV * (across * ddx + along * ddy), 0.5 * PG * ddx, 0.5 * PG * ddy)
    for f, centre in enumerate(fields):
        sides = around_tracer if f == 0 else near(f * levels + z, centre)
        beside = KH * ((sides[0] + sides[1]) + (sides[2] + sides[3]))
        beyond = KZ * (load(f * levels + upper) + load(f * levels + lower))
        results.append((1.0 - 4.0 * KH - 2.0 * KZ) * centre + beside + (beyond - extra[f]))
    return results


def added(sign, along, tracer, across_near, along_near):
    return [
        (KH - sign * 0.5 * ADV * along) * tracer,
        KH * across_near,
        KH * along_near - sign * 0.5 * PG * tracer,
    ]


def begin_body(state_ref, wet_ref, west_ref, east_ref, tips_ref, mask_ref, begun_ref, packs_ref, token_ref, full_ref):
    planes, rows, cols = state_ref.shape
    levels = planes // 3
    west, east = west_ref[...], east_ref[...]
    for j in range(planes):
        tips_ref[j] = outer_rows(state_ref, j)
    for j in range(planes):
        full_ref[j, :, :cols] = state_ref[j]
        full_ref[j, :, cols:] = side_tile(west, EDGE * j, east, EDGE * j)
    mask_ref[:, :cols] = wet_ref[...].astype(jnp.float32)
    mask_ref[:, cols:] = side_tile(west, EDGE * planes, east, EDGE * planes)
    packs = [jnp.zeros((rows, LANES), jnp.float32) for _ in range(2)]
    for z in range(levels):
        values = moved(lambda j: full_ref[j], lambda j, field: around_between(field, 0.0, 0.0), levels, z)
        for f, value in enumerate(values):
            j = f * levels + z
            begun_ref[j] = value[:, :cols]
            packs[0] = packed(packs[0], value[:, cols:], LANES - EDGE, EDGE * j)
            packs[1] = packed(packs[1], value[:, cols:], 0, EDGE * j)
    packs_ref[0], packs_ref[1] = packs
    token_ref[...] = jnp.zeros_like(token_ref)


def outer_rows(ref, *index):
    rows, tile = ref.shape[len(index)], 2 * RIM
    first, last = ref[(*index, slice(0, tile))], ref[(*index, slice(rows - tile, rows))]
    return jnp.where(iota(first.shape, 0) < RIM, first, last)


def widened(plane, west, east, at):
    return jnp.concatenate([plane, side_tile(west, at, east, at)], axis=1)


def places(planes, sides):
    levels = planes // 3
    counts = [RIM] * levels + [EDGE] * (2 * levels) + [EDGE] * levels + [EDGE - 1] * levels + [EDGE] * (2 + (sides + 2) // 2)
    starts = [sum(counts[:k]) for k in range(len(counts))]
    return list(zip(starts, counts))


def outer_body(force_ref, edge_ref, tips_ref, mask_ref, west_ref, east_ref, *refs):
    sides, (up_ref, down_ref) = refs[:-2], refs[-2:]
    planes, rows, cols = force_ref.shape
    moving = 2 * planes // 3
    where = places(planes, len(sides))
    for out_ref, up in ((up_ref, True), (down_ref, False)):

        def put(place, ref, index, scale, lanes=slice(None)):
            start, count = where[place]
            at = slice(ref.shape[len(index)] - count, None) if up else slice(0, count)
            out_ref[start : start + count, lanes] = ref[(*index, at, slice(0, cols))] * scale

        out_ref[where[-1][0] :] = jnp.zeros((out_ref.shape[0] - where[-1][0], cols), jnp.float32)
        for j in range(planes):
            put(j, tips_ref, (j,), STATE_SCALE)
        for j in range(moving):
            put(planes + j, force_ref, (j,), FORCE_SCALE)
        put(planes + moving, mask_ref, (), STATE_SCALE)
        for k, part in enumerate((west_ref, east_ref, edge_ref, *sides)):
            lane = (k % 2) * LANES
            scale = STATE_SCALE if k < 2 else FORCE_SCALE
            put(planes + moving + 1 + k // 2, part, (), scale, slice(lane, lane + LANES))


def factors(mask, own, west, east, force_rows, push_ref):
    moving, total, wide = push_ref.shape
    cols = wide - LANES

    def counts(edge):
        return jnp.broadcast_to(edge[:, LANES - 1 :], (total, LANES))

    lane = iota((total, LANES), 1)
    count_side = jnp.where(lane < LANES // 2, counts(east), counts(west))
    relax = mask / (1.0 + GAMMA * jnp.concatenate([counts(own)] * (cols // LANES) + [count_side], axis=1))
    half = GAMMA * relax
    for j in range(moving):
        push_ref[j, :, :cols] = force_rows(j) * half[:, :cols]
        push_ref[j, :, cols:] = side_tile(west, EDGE * (moving + j), east, EDGE * j) * half[:, cols:]
    return relax


def finish(relax, push_ref, levels, values, z, at=(slice(None),)):
    tracer, across, along = values
    rated = relax[at]
    return (tracer * rated + push_ref[(z, *at)], across * rated, along * rated + push_ref[(levels + z, *at)])


def two_more(relax, push_ref, one_ref, two_ref, last, patched=lambda j, value: value):
    levels = one_ref.shape[0] // 3
    cols = one_ref.shape[2] - LANES
    for z in range(levels):
        values = moved(lambda j: one_ref[j], lambda j, field: around(field), levels, z)
        for f, value in enumerate(finish(relax, push_ref, levels, values, z)):
            two_ref[f * levels + z] = patched(f * levels + z, value)
    for z in range(levels):
        values = moved(
            lambda j: two_ref[j, :, :cols],
            lambda j, field: tuple(side[:, :cols] for side in around(two_ref[j])),
            levels,
            z,
        )
        last(z, finish(relax, push_ref, levels, values, z, (slice(None), slice(0, cols))))


def terms(values, stokes):
    rows, total = stokes.shape[0], values[0].shape[0]
    tracer = values[0]
    ddy = pltpu.roll(tracer, total - 1, 0)[:rows] - pltpu.roll(tracer, 1, 0)[:rows]
    return [values[2][:rows] * tracer[:rows], stokes * tracer[:rows], ddy]


def transports(sums, count, child, all_rows):
    raw = [jnp.sum(value, axis=1, keepdims=True) for value in sums]
    raw = [raw[0], raw[1] / (1.0 + count), raw[2] * (-0.5 * DISPERSE)]
    lane = iota(child.shape, 1)
    part = jnp.zeros(child.shape, jnp.float32)
    for q in range(3):
        part = part + jnp.where((child >= 0) & (lane == q * all_rows + child), raw[q], 0.0)
    return jnp.sum(part, axis=0, keepdims=True)


def inner_body(mask_ref, begun_ref, packs_ref, force_ref, edge_ref, *refs):
    side_refs, (middle_ref, ends_ref, part_ref, twos_ref, push_ref, one_ref, two_ref) = refs[:-7], refs[-7:]
    planes, rows, cols = begun_ref.shape
    levels = planes // 3
    moving = 2 * levels
    tile = 2 * RIM
    west, east = packs_ref[0], packs_ref[1]
    relax = factors(
        mask_ref[...], edge_ref[...], side_refs[0][...], side_refs[-1][...], lambda j: force_ref[j], push_ref
    )
    for z in range(levels):
        index = [f * levels + z for f in range(3)]
        values = [widened(begun_ref[j], west, east, EDGE * j) for j in index]
        for j, value in zip(index, finish(relax, push_ref, levels, values, z)):
            one_ref[j] = value
    sums = [jnp.zeros((rows, cols), jnp.float32) for _ in range(3)]

    def last(z, values):
        for f, value in enumerate(values):
            middle_ref[f, z] = value[tile : rows - tile]
            ends_ref[f, z, :tile] = value[:tile]
            ends_ref[f, z, tile:] = value[rows - tile :]
        for q, term in enumerate(terms(values, force_ref[moving + z])):
            sums[q] = sums[q] + term

    two_more(relax, push_ref, one_ref, two_ref, last)
    for j in range(planes):
        twos_ref[j] = outer_rows(two_ref, j)
    row = iota((rows, LANES), 0)
    child = jnp.where((row >= RIM) & (row < rows - RIM), row, -1)
    part_ref[...] = transports(sums, edge_ref[:, LANES - 1 :], child, rows)


def steps_body(
    sides, stokes_ref, tips_ref, west_ref, east_ref, mask_ref, begun_ref, packs_ref, force_ref, edge_ref, north_ref, south_ref, *refs
):
    middle_ref, ends_ref, part_ref, twos_ref = refs[:4]
    refs = refs[4:]
    side_refs = refs[:sides]
    held_ref, parts_ref, push_ref, halo_ref, one_ref, two_ref = refs[sides:]
    planes, rows, cols = begun_ref.shape
    wide = cols + LANES
    levels = planes // 3
    moving = 2 * levels
    tile = 2 * RIM
    total = 2 * tile

    where = places(planes, sides)

    def joined(place, scale):
        start, count = where[place]
        at = slice(start, start + count)
        parts = [north_ref[at], jnp.zeros((tile - 2 * count, cols), jnp.float32), south_ref[at]]
        return jnp.concatenate([part for part in parts if part.shape[0]], axis=0) * (1.0 / scale)

    def half_of(k, scale):
        lane = (k % 2) * LANES
        return joined(planes + moving + 1 + k // 2, scale)[:, lane : lane + LANES]

    beside = [half_of(k, STATE_SCALE) for k in range(2)]
    outer = [half_of(2 + k, FORCE_SCALE) for k in range(1 + sides)]
    edges = [jnp.concatenate([outer_rows(side), outer[1 + k]], axis=0) for k, side in enumerate(side_refs)]
    own = jnp.concatenate([outer_rows(edge_ref), outer[0]], axis=0)

    def halo(index, at):
        return widened(joined(index, STATE_SCALE), *beside, at)

    mask = jnp.concatenate([outer_rows(mask_ref), halo(planes + moving, EDGE * planes)], axis=0)
    relax = factors(
        mask,
        own,
        edges[0],
        edges[-1],
        lambda j: jnp.concatenate([outer_rows(force_ref, j), joined(planes + j, FORCE_SCALE)], axis=0),
        push_ref,
    )
    for j in range(planes):
        halo_ref[j] = halo(j, EDGE * j)
    row = iota((tile, wide), 0)
    packs = [outer_rows(packs_ref, k) for k in range(2)]
    wests, easts = outer_rows(west_ref), outer_rows(east_ref)

    def tip(j):
        return widened(tips_ref[j], wests, easts, EDGE * j)

    def begun(j):
        return widened(outer_rows(begun_ref, j), *packs, EDGE * j)

    def near(j, field):
        start = tip(j)
        return around_between(field, start[:1], start[tile - 1 :])

    for z in range(levels):
        index = [f * levels + z for f in range(3)]
        beyond = [halo_ref[j] for j in index]
        north = [jnp.where(row == tile - 1, value[:1], 0.0) for value in beyond]
        south = [jnp.where(row == 0, value[tile - 1 :], 0.0) for value in beyond]
        along = tip(index[2])
        extras = zip(added(-1.0, along, *south), added(1.0, along, *north))
        blocks = (
            [begun(j) + (first + final) for j, (first, final) in zip(index, extras)],
            moved(lambda j: halo_ref[j], near, levels, z),
        )
        for k, values in enumerate(blocks):
            at = slice(k * tile, (k + 1) * tile)
            for j, value in zip(index, finish(relax, push_ref, levels, values, z, (at,))):
                one_ref[j, at] = value

    meeting = (row == RIM - 1) | (row == RIM)

    def patched(j, value):
        return jnp.concatenate([jnp.where(meeting, twos_ref[j], value[:tile]), value[tile:]], axis=0)

    sums = [jnp.zeros((tile, cols), jnp.float32) for _ in range(3)]
    place = iota((tile, cols), 0)

    def last(z, values):
        finals = []
        for f, value in enumerate(values):
            ends = [ends_ref[f, z, :tile], ends_ref[f, z, tile:]]
            kept = jnp.where(place < RIM, *ends)
            final = jnp.where((place == RIM - 1) | (place == RIM), kept, value[:tile])
            held_ref[f, z, :tile] = jnp.where(place < RIM, final, ends[0])
            held_ref[f, z, tile:] = jnp.where(place < RIM, ends[1], final)
            finals.append(final)
        tracer = jnp.concatenate([finals[0], values[0][tile:]], axis=0)
        within = jnp.where(place < RIM, ends_ref[0, z, tile:], ends_ref[0, z, :tile])
        north = jnp.where(place == RIM - 1, pltpu.roll(within, tile - 1, 0), pltpu.roll(tracer, total - 1, 0)[:tile])
        south = jnp.where(place == RIM, pltpu.roll(within, 1, 0), pltpu.roll(tracer, 1, 0)[:tile])
        stokes = outer_rows(force_ref, moving + z)
        for q, term in enumerate((finals[2] * finals[0], stokes * finals[0], north - south)):
            sums[q] = sums[q] + term

    two_more(relax, push_ref, one_ref, two_ref, last, patched)
    beyond = jnp.zeros((rows, cols), jnp.float32)
    for z in range(levels):
        tracer = [held_ref[0, z, :tile], middle_ref[0, z], held_ref[0, z, tile:]]
        beyond = beyond + stokes_ref[:, z * cols : (z + 1) * cols] * jnp.concatenate(tracer, axis=0)
    beyond = jnp.sum(beyond, axis=1, keepdims=True) / (SUM_SCALE * (1.0 + edge_ref[:, LANES - 1 :]))
    row, lane = iota((rows, LANES), 0), iota((rows, LANES), 1)
    beyond = jnp.sum(jnp.where(lane == rows + row, beyond, 0.0), axis=0, keepdims=True)
    row = iota((tile, LANES), 0)
    child = jnp.where(row < RIM, row, row + rows - tile)
    part = transports(sums, own[:tile, LANES - 1 :], child, rows) + (part_ref[...] + beyond)
    parts_ref[...] = jnp.broadcast_to(part, parts_ref.shape)


def whole_body(middle_ref, ends_ref, state_ref, sent):
    rows = state_ref.shape[2]
    tile = ends_ref.shape[2] // 2
    copies = [
        pltpu.make_async_copy(source, state_ref.at[:, :, pl.ds(start, size)], sent.at[k])
        for k, (source, start, size) in enumerate(
            (
                (middle_ref, tile, rows - 2 * tile),
                (ends_ref.at[:, :, pl.ds(0, tile)], 0, tile),
                (ends_ref.at[:, :, pl.ds(tile, tile)], rows - tile, tile),
            )
        )
    ]
    for copy in copies:
        copy.start()
    for copy in copies:
        copy.wait()


def profile_body(across, along, parts_ref, out_ref):
    rows = out_ref.shape[1]
    parts = parts_ref[...]
    devices = parts.shape[0]
    total = parts
    for k in range(1, across):
        total = total + pltpu.roll(parts, devices - k, 0)
    row = iota(parts.shape, 0)
    squares = jnp.sum(jnp.where(row % across == 0, total * total, 0.0), keepdims=True)
    scale = jnp.sqrt(squares / (3 * rows * along) + 1e-06)
    mine = jnp.sum(jnp.where(row == lax.axis_index("gy") * across, total, 0.0), axis=0, keepdims=True) / scale
    for q in range(3):
        out_ref[q : q + 1, :] = mine[:, q * rows : (q + 1) * rows]


def per_device(state, parent_rows, dest, pick, offset, wet):
    fields, levels, rows, cols = state.shape
    planes = fields * levels
    moving = 2 * levels
    along, across = lax.axis_size("gy"), lax.axis_size("gx")
    capacity = 2 * SEND // along
    wide = cols + LANES
    f32 = jnp.float32
    even_pairs = [(i, i ^ 1) for i in range(along)]
    odd_pairs = [(i, ((i + 1) ^ 1) - 1) for i in range(1, along - 1)]
    swapped = [(0, 1), (1, 0)]
    eastward = [(i, i + 1) for i in range(across - 1)]
    westward = [(i + 1, i) for i in range(across - 1)]

    half = along // 2
    slots = half * capacity
    width = planes * cols + LANES
    halves = [list(range(half)), list(range(half, along))]

    def gathered(far):
        fetched = [pltpu.VMEM((1, SEND), jnp.int32)] * 3 + [pltpu.VMEM(parent_rows.shape, jnp.bfloat16)] if far else []
        return call(
            functools.partial(gather_body, capacity, slots, far),
            jax.ShapeDtypeStruct((slots, width), jnp.bfloat16),
            flops=2 * 8 * slots * SEND * planes * cols,
            moved=2 * (SEND + slots) * planes * cols,
            limit=VMEM_MOST,
            in_specs=[pl.BlockSpec(memory_space=pl.ANY if far else pltpu.VMEM)] * 4,
            out_specs=pl.BlockSpec(memory_space=pl.ANY),
            scratch_shapes=fetched
            + [
                pltpu.VMEM((slots, width), jnp.bfloat16),
                pltpu.SemaphoreType.DMA((4,)),
            ]
            + ([pltpu.SemaphoreType.DMA((4,))] if far else []),
        )(dest.reshape(1, SEND), pick.reshape(1, SEND), offset.reshape(1, SEND), parent_rows)

    def exchanged(payload):
        return lax.all_to_all(payload, "gy", split_axis=0, concat_axis=0, tiled=True, axis_index_groups=halves)

    far_rows = exchanged(gathered(True))

    cells = state.reshape(planes, rows, cols)
    packed_side = jax.ShapeDtypeStruct((rows, LANES), f32)
    first, last = call(sides_body, (packed_side, packed_side), moved=4 * planes * rows * cols)(cells, wet)
    if across == 2:
        west_one = lax.axis_index("gx") == 0
        other = lax.ppermute(jnp.where(west_one, last, first), "gx", swapped)
        from_west, from_east = jnp.where(west_one, 0.0, other), jnp.where(west_one, other, 0.0)
    else:
        from_west = lax.ppermute(last, "gx", eastward)
        from_east = lax.ppermute(first, "gx", westward)
    tips, mask, begun, packs, token = call(
        begin_body,
        (
            jax.ShapeDtypeStruct((planes, 2 * RIM, cols), f32),
            jax.ShapeDtypeStruct((rows, wide), f32),
            jax.ShapeDtypeStruct((planes, rows, cols), f32),
            jax.ShapeDtypeStruct((2, rows, LANES), f32),
            jax.ShapeDtypeStruct((8, LANES), f32),
        ),
        flops=20 * planes * rows * wide,
        moved=12 * planes * rows * wide,
        scratch_shapes=[pltpu.VMEM((planes, rows, wide), f32)],
    )(cells, wet, from_west, from_east)

    sums, stokes = call(
        far_body,
        (
            jax.ShapeDtypeStruct((rows, moving * cols + LANES), f32),
            jax.ShapeDtypeStruct((rows, (planes - moving) * cols), f32),
        ),
        flops=2 * rows * slots * width,
        moved=2 * slots * width + 4 * rows * width,
    )(token, far_rows)
    mirrored = [(i, (i + half) % along) for i in range(along)]
    halved = (sums.astype(jnp.float16), stokes.astype(jnp.float16), gathered(False))
    sums, stokes, near_rows = lax.optimization_barrier(halved)
    sums = lax.ppermute(sums, "gy", mirrored)
    arrived = exchanged(near_rows)
    stokes = lax.ppermute(stokes, "gy", mirrored)
    come = call(
        come_body,
        jax.ShapeDtypeStruct((8, LANES), f32),
        flops=10**11,
    )(sums[:8, :LANES].astype(f32))
    sums, arrived = lax.optimization_barrier((sums, arrived))
    sums = sums.astype(f32)

    force, edge = call(
        functools.partial(landing_body, planes, cols),
        (jax.ShapeDtypeStruct((planes, rows, cols), f32), packed_side),
        flops=2 * rows * slots * planes * cols,
        moved=2 * slots * planes * cols + 4 * rows * planes * cols,
    )(come, arrived, sums)
    if across == 2:
        sides = [lax.ppermute(edge, "gx", swapped)]
    else:
        sides = [lax.ppermute(edge, "gx", eastward), lax.ppermute(edge, "gx", westward)]
    start, count = places(planes, len(sides))[-1]
    outer = jax.ShapeDtypeStruct(((start + count + 7) // 8 * 8, cols), f32)
    up, down = call(outer_body, (outer, outer), moved=16 * (moving + planes) * RIM * cols)(
        force, edge, tips, mask, from_west, from_east, *sides
    )
    even = lax.axis_index("gy") % 2 == 0
    far = lax.ppermute(jnp.where(even, down, up).astype(jnp.float16), "gy", odd_pairs)
    far = lax.optimization_barrier(far.astype(f32))
    near = lax.ppermute(jnp.where(even, up, down).astype(jnp.float16), "gy", even_pairs).astype(f32)
    above, below = jnp.where(even, near, far), jnp.where(even, far, near)
    tile = 2 * RIM
    middle, ends, part, twos = call(
        inner_body,
        (
            jax.ShapeDtypeStruct((fields, levels, rows - 2 * tile, cols), f32),
            jax.ShapeDtypeStruct((fields, levels, 2 * tile, cols), f32),
            jax.ShapeDtypeStruct((1, LANES), f32),
            jax.ShapeDtypeStruct((planes, tile, wide), f32),
        ),
        flops=60 * planes * rows * wide,
        moved=8 * planes * rows * wide,
        scratch_shapes=[
            pltpu.VMEM((moving, rows, wide), f32),
            pltpu.VMEM((planes, rows, wide), f32),
            pltpu.VMEM((planes, rows, wide), f32),
        ],
    )(mask, begun, packs, force, edge, *sides)
    stokes, part = lax.optimization_barrier((stokes, part))
    stokes = stokes.astype(f32)
    ends, parts = call(
        functools.partial(steps_body, len(sides)),
        (
            jax.ShapeDtypeStruct((fields, levels, 2 * tile, cols), f32),
            jax.ShapeDtypeStruct((along * across, LANES), f32),
        ),
        flops=60 * planes * 3 * tile * wide,
        moved=8 * planes * 3 * tile * wide,
        scratch_shapes=[
            pltpu.VMEM((moving, 2 * tile, wide), f32),
            pltpu.VMEM((planes, tile, wide), f32),
            pltpu.VMEM((planes, 2 * tile, wide), f32),
            pltpu.VMEM((planes, 2 * tile, wide), f32),
        ],
    )(stokes, tips, from_west, from_east, mask, begun, packs, force, edge, above, below, middle, ends, part, twos, *sides)
    new_state = call(
        whole_body,
        jax.ShapeDtypeStruct(state.shape, f32),
        moved=8 * planes * rows * cols,
        out_specs=pl.BlockSpec(memory_space=pl.ANY),
        scratch_shapes=[pltpu.SemaphoreType.DMA((3,))],
    )(middle, ends)
    every = lax.all_to_all(parts, ("gy", "gx"), split_axis=0, concat_axis=0, tiled=True)
    profile = call(functools.partial(profile_body, across, along), jax.ShapeDtypeStruct((3, rows), f32))(every)
    return new_state, profile


def solution(mesh):
    in_specs = (
        P(None, None, "gy", "gx"),
        P(("gy", "gx"), None, None),
        P(("gy", "gx"), None),
        P(("gy", "gx")),
        P(("gy", "gx")),
        P("gy", "gx"),
    )
    out_specs = (P(None, None, "gy", "gx"), P(None, "gy"))
    return jax.shard_map(
        per_device, mesh=mesh, in_specs=in_specs, out_specs=out_specs, check_vma=False
    )
```
